32 devices in a mesh: parts: 2 (over y), op: 4 (over z), sec: 2 (over x), sub: 2 (over core).
Axes of the slice: x: 2, y: 2, z: 4, core: 2. Of those that a mesh axis runs over, the one named last changes fastest.
Arguments:
- psi: float32 [32, 256, 256], P(('parts', 'sec', 'sub'), 'op'), parts along dimension 0, may hold values from -6 to 6
- left_ops: float32 [32, 256, 256], P('op'), may hold values from -0.09375 to 0.09375
- right_ops: float32 [32, 256, 256], P('op'), may hold values from -0.375 to 0.375
- shifts: int32 [32], P('op'), may hold values from -1 to 1
- allowed: int32 [32, 16], P('op'), may hold values 0 or 1
Outputs:
- sigma: float32 [32, 256, 256], P(('parts', 'sec', 'sub'), 'op'), parts along dimension 0
The draws below stay inside these ranges and needn't reach their ends.
There are 2 independent parts, one for each index of `parts`. The reference program is written for one: setup_inputs(seed, part) draws one part's arguments, and reference() takes and returns one part's arrays. A program takes and returns all parts, laid end to end along the dimension named above; an argument that names none is the same for every part. Nothing has to cross between parts.
All inputs are finite; a program needn't handle non-finite values. No bound on the sum of `allowed` on one device may be relied on, other than what follows from the above.
Results may differ from the reference program's by a relative error of at most 0.0003.
Values sent between devices are 32-bit elements; how exact they have to be, the bound alone decides.
No kernel may reach another device: no remote copies, remote signals or barrier semaphores. Data moves between devices by JAX's collectives and lax.ppermute only.
A program may use at most 64 MiB of HBM per device.

```python
import jax
import jax.numpy as jnp
from jax import lax

SD = 256
KOPS = 32
NSEC = 16


def touch_ends(drawn, own_key, low, top_value):
    shape = drawn.shape
    place = [jax.random.randint(jax.random.fold_in(own_key, axis), (), 0, shape[axis]) for axis in range(len(shape))]
    drawn = drawn.at[tuple(place)].set(low)
    longest = shape.index(max(shape))
    place[longest] = (place[longest] + 1) % shape[longest]
    return drawn.at[tuple(place)].set(top_value)


def with_spikes(entries, key, source, target, shards_of, factor):
    def block_of(axis_at):
        return (jnp.arange(entries.shape[axis_at]) // (entries.shape[axis_at] // shards_of)).reshape((-1,) + (1,) * (entries.ndim - 1 - axis_at))

    near = jax.random.permutation(key, shards_of)[block_of(target)]
    other_side = (block_of(target) + shards_of // 2) % shards_of
    return jnp.where((block_of(source) == near) | (block_of(source) == other_side), factor * entries, entries)


def block_scale(rng, dims, cuts, low, largest):
    def one(position, shards_of):
        draws = jax.random.uniform(jax.random.fold_in(jax.random.fold_in(rng, 6), position), (shards_of,), jnp.float32, low / len(cuts), largest / len(cuts))
        return jnp.repeat(jnp.exp(draws), dims[position] // shards_of).reshape((-1,) + (1,) * (len(dims) - position - 1))

    loudness = one(*cuts[0])
    for cut in cuts[1:]:
        loudness = loudness * one(*cut)
    return loudness


def scatter_about(own_key, extent, spread, bound, pieces=(), kind=jnp.bfloat16):
    level = block_scale(own_key, extent, pieces, -0.22, 0.18) if pieces else 1.0
    values = jax.random.normal(own_key, extent, jnp.float32) * spread * level
    return jnp.minimum(jnp.maximum(values, -bound), bound).astype(kind)


def gaussian_with(key, dims, spread, most, pieces, heavy, kind=jnp.bfloat16):
    result = spread * jax.random.normal(key, dims, jnp.float32)
    if pieces:
        result = result * block_scale(key, dims, pieces, -0.22, 0.18)
    return jnp.clip(with_spikes(result, jax.random.fold_in(key, 3), *heavy), -most, most).astype(kind)


def setup_inputs(seed: int = 0, part: int = 0) -> dict:
    arg_keys = jax.random.split(jax.random.key(seed), 6)
    part_keys = jax.random.split(jax.random.fold_in(arg_keys[5], part), 6)
    return {
        "psi": scatter_about(part_keys[0], (NSEC, SD, SD), 1.0, 6.0, ((0, 4), (1, 4)), jnp.float32),
        "left_ops": gaussian_with(arg_keys[1], (KOPS, SD, SD), (SD * KOPS) ** -0.5, 0.09375, ((0, 4),), (0, 1, 4, 2.0), jnp.float32),
        "right_ops": scatter_about(arg_keys[2], (KOPS, SD, SD), SD ** -0.5, 0.375, ((0, 4),), jnp.float32),
        "shifts": touch_ends(jax.random.randint(arg_keys[3], (KOPS,), -1, 2), jax.random.fold_in(arg_keys[3], 1), -1, 1).astype(jnp.int32),
        "allowed": touch_ends((jax.random.randint(arg_keys[4], (KOPS, NSEC), 0, 4) < 3).astype(jnp.int32), jax.random.fold_in(arg_keys[4], 1), 0, 1),
    }


def reference(psi, left_ops, right_ops, shifts, allowed):
    sectors = jnp.arange(NSEC, dtype=jnp.int32)

    def one_operator(total, index):
        left = left_ops[index]
        right = right_ops[index]
        weight = allowed[index].astype(jnp.float32)
        middle = jnp.einsum("ij,sjl->sil", left, psi, precision=lax.Precision.HIGHEST)
        applied = jnp.einsum("sil,ml->sim", middle, right, precision=lax.Precision.HIGHEST)
        target = sectors + shifts[index]
        select = (target[:, None] == sectors[None, :]).astype(jnp.float32) * weight[:, None]
        total = total + jnp.einsum("st,sim->tim", select, applied, precision=lax.Precision.HIGHEST)
        return total, None

    start = jnp.zeros((NSEC, SD, SD), jnp.float32)
    total, _ = lax.scan(one_operator, start, jnp.arange(KOPS, dtype=jnp.int32))
    return total
```

```python
import functools

import jax
import jax.numpy as jnp
from jax import lax
from jax.experimental import pallas as pl
from jax.experimental.pallas import tpu as pltpu
from jax.sharding import PartitionSpec as P


def shifted(block, axis, distance):
    devices = range(lax.axis_size(axis))
    route = [(i - distance, i) for i in devices if i - distance in devices]
    return lax.ppermute(block, axis, route)


def split(x):
    hi = x.astype(jnp.bfloat16)
    return hi, (x - hi.astype(jnp.float32)).astype(jnp.bfloat16)


def dot3(a, b, dims):
    one = functools.partial(lax.dot_general, dimension_numbers=(dims, ((), ())), preferred_element_type=jnp.float32)
    return one(a[0], b[0]) + (one(a[0], b[1]) + one(a[1], b[0]))


def products(n, place_ref, shifts_ref, allowed_ref, *refs):
    blocks, (left_ref, right_ref), outs = refs[:n], refs[n : n + 2], refs[n + 2 : 2 * n + 4]
    psi, psi_hi, psi_lo, mid_hi, mid_lo, total = refs[2 * n + 4 :]
    nloc, rows, width = blocks[0].shape
    kops = left_ref.shape[0]
    me, first = place_ref[0], place_ref[1]
    for j in range(n):
        owner = lax.rem(me - j + n, n)
        psi[:, pl.ds(pl.multiple_of(owner * rows, rows), rows), :] = blocks[j][...]
    hi, lo = split(psi[...])
    psi_hi[...] = hi
    psi_lo[...] = lo
    total[...] = jnp.zeros_like(total)

    def one_operator(k, _):
        left = split(left_ref[k])
        right = split(right_ref[k])
        for s in range(nloc):
            middle = dot3(left, (psi_hi[s], psi_lo[s]), ((1,), (0,)))
            middle = middle * allowed_ref[k, first + s].astype(jnp.float32)
            hi, lo = split(middle)
            mid_hi[pl.ds(s * width, width), :] = hi
            mid_lo[pl.ds(s * width, width), :] = lo
        applied = dot3((mid_hi[...], mid_lo[...]), right, ((1,), (1,)))
        slot = pl.ds(shifts_ref[k] + 1, nloc)
        total[slot] += applied.reshape(nloc, width, width)
        return 0

    lax.fori_loop(0, kops, one_operator, 0)
    for j in range(n):
        target = lax.rem(me - 1 - j + 2 * n, n)
        at = pl.ds(pl.multiple_of(target * rows, rows), rows)
        outs[j][...] = total[1 : nloc + 1, at, :]
        outs[n][pl.ds(j * rows, rows), :] = total[0, at, :]
        outs[n + 1][pl.ds(j * rows, rows), :] = total[nloc + 1, at, :]


def shards(psi, left_ops, right_ops, shifts, allowed):
    nloc, rows, width = psi.shape
    kops = left_ops.shape[0]
    n = lax.axis_size("op")
    ring = [(i, (i + 1) % n) for i in range(n)]
    place = jnp.stack([lax.axis_index("op"), lax.axis_index(("sec", "sub")) * nloc]).astype(jnp.int32)
    blocks = [psi]
    for _ in range(n - 1):
        blocks.append(lax.ppermute(blocks[-1], "op", ring))
    f32, bf16 = jnp.float32, jnp.bfloat16
    smem, vmem = pl.BlockSpec(memory_space=pltpu.SMEM), pl.BlockSpec(memory_space=pltpu.VMEM)
    outs = pl.pallas_call(
        functools.partial(products, n),
        out_shape=[jax.ShapeDtypeStruct((nloc, rows, width), f32)] * n + [jax.ShapeDtypeStruct((width, width), f32)] * 2,
        in_specs=[smem] * 3 + [vmem] * (n + 2),
        out_specs=[vmem] * (n + 2),
        scratch_shapes=[
            pltpu.VMEM((nloc, width, width), f32),
            pltpu.VMEM((nloc, width, width), bf16),
            pltpu.VMEM((nloc, width, width), bf16),
            pltpu.VMEM((nloc * width, width), bf16),
            pltpu.VMEM((nloc * width, width), bf16),
            pltpu.VMEM((nloc + 2, width, width), f32),
        ],
        compiler_params=pltpu.CompilerParams(vmem_limit_bytes=40 * 2**20),
        cost_estimate=pl.CostEstimate(flops=12 * kops * nloc * width**3, bytes_accessed=8 * kops * width**2, transcendentals=0),
    )(place, shifts, allowed, *blocks, left_ops, right_ops)
    chunks, below, above = outs[:n], outs[n], outs[n + 1]
    from_prev = shifted(above, ("sec", "sub"), 1)
    from_next = shifted(below, ("sec", "sub"), -1)

    def own(j):
        at = slice(j * rows, (j + 1) * rows)
        return chunks[j].at[0].add(from_prev[at]).at[nloc - 1].add(from_next[at])

    result = own(0)
    for j in range(1, n):
        result = lax.ppermute(result, "op", ring) + own(j)
    return result


def solution(mesh):
    return jax.shard_map(
        shards,
        mesh=mesh,
        in_specs=(
            P(("parts", "sec", "sub"), "op", None),
            P("op", None, None),
            P("op", None, None),
            P("op"),
            P("op", None),
        ),
        out_specs=P(("parts", "sec", "sub"), "op", None),
        check_vma=False,
    )
```

```python
import functools

import jax
import jax.numpy as jnp
from jax import lax
from jax.experimental import pallas as pl
from jax.experimental.pallas import tpu as pltpu
from jax.sharding import PartitionSpec as P

F32, BF16 = jnp.float32, jnp.bfloat16
SMEM = pl.BlockSpec(memory_space=pltpu.SMEM)
VMEM = pl.BlockSpec(memory_space=pltpu.VMEM)


def shifted(block, axis, distance):
    devices = range(lax.axis_size(axis))
    route = [(i - distance, i) for i in devices if i - distance in devices]
    return lax.ppermute(block, axis, route)


def ring_route(n):
    order = [0] + [i for i in range(n) if i % 2] + [i for i in reversed(range(1, n)) if i % 2 == 0]
    return [(order[i], order[(i + 1) % n]) for i in range(n)]


def ring_place(n, steps_back):
    me = lax.axis_index("op")
    place = jnp.where(me == 0, 0, jnp.where(lax.rem(me, 2) == 1, (me + 1) // 2, n - me // 2))
    at = lax.rem(place - steps_back + 2 * n, n)
    return jnp.where(at == 0, 0, jnp.where(at <= n // 2, 2 * at - 1, 2 * (n - at)))


def split(x):
    hi = x.astype(BF16)
    return hi, (x - hi.astype(F32)).astype(BF16)


def dot3(a, b):
    one = functools.partial(jnp.dot, preferred_element_type=F32)
    return one(a[0], b[0]) + (one(a[0], b[1]) + one(a[1], b[0]))


def prepare(left_ref, right_ref, left_hi, left_lo, right_hi, right_lo):
    kops, width, _ = left_ref.shape

    def one_operator(k, _):
        left_hi[k], left_lo[k] = split(left_ref[k])
        at = pl.ds(pl.multiple_of(k * width, width), width)
        right_hi[at, :], right_lo[at, :] = split(right_ref[k].T)
        return 0

    lax.fori_loop(0, kops, one_operator, 0)


def first_stage(n, sectors, nloc, allowed_ref, *refs):
    blocks, (left_hi, left_lo), (middle, psi) = refs[:n], refs[n : n + 2], refs[-2:]
    kops, width, _ = left_hi.shape
    rows = blocks[0].shape[1]
    first = lax.axis_index(("sec", "sub")) * nloc
    for j in range(n):
        psi[:, pl.ds(pl.multiple_of(ring_place(n, j) * rows, rows), rows), :] = blocks[j][...]
    halves = [split(psi[i]) for i in range(len(sectors))]

    def one_operator(k, _):
        at = pl.ds(pl.multiple_of(k * width, width), width)
        for i, s in enumerate(sectors):
            block = dot3((left_hi[k], left_lo[k]), halves[i])
            middle[i, :, at] = block * allowed_ref[k, first + s].astype(F32)
        return 0

    lax.fori_loop(0, kops, one_operator, 0, unroll=2)


def first_stage_halo(n, nloc, shifts_ref, allowed_ref, *refs):
    (above_head, above_last, below_head, below_last), (left_hi, left_lo) = refs[:4], refs[4:6]
    middle, psi, psi_hi, psi_lo = refs[-4:]
    kops, width, _ = left_hi.shape
    rows = above_last.shape[1]
    first = lax.axis_index(("sec", "sub")) * nloc
    for j in range(n):
        at = pl.ds(pl.multiple_of(ring_place(n, j) * rows, rows), rows)
        psi[0, at, :] = above_head[j] if j < n - 1 else above_last[0]
        psi[1, at, :] = below_head[j] if j < n - 1 else below_last[0]
    for i in range(2):
        psi_hi[i], psi_lo[i] = split(psi[i])

    def one_operator(k, _):
        at = pl.ds(pl.multiple_of(k * width, width), width)
        up = shifts_ref[k] == 1
        which = jnp.where(up, 0, 1)
        source = jnp.where(up, jnp.maximum(first - 1, 0), jnp.minimum(first + nloc, allowed_ref.shape[1] - 1))
        block = dot3((left_hi[k], left_lo[k]), (psi_hi[which], psi_lo[which]))
        middle[0, :, at] = block * allowed_ref[k, source].astype(F32)
        return 0

    lax.fori_loop(0, kops, one_operator, 0, unroll=2)


def second_stage(n, step, shifts_ref, outer, halo, inner, right_hi, right_lo, *refs):
    outs, (mid_hi, mid_lo) = refs[:-2], refs[-2:]
    per, rows, width = outs[0].shape
    nloc = per * len(outs)
    at = pl.ds(pl.multiple_of(ring_place(n, step + 1) * rows, rows), rows)
    for k in range(shifts_ref.shape[0]):
        shift = shifts_ref[k]
        columns = slice(k * width, (k + 1) * width)
        outside = jnp.where(shift == 1, 1, jnp.where(shift == -1, nloc, 0))
        places = [(outer, 0, shift + 1), (outer, 1, shift + nloc), (halo, 0, outside)]
        places += [(inner, i, shift + i + 2) for i in range(nloc - 2)]
        for source, i, slot in places:
            mid_hi[slot, :, columns], mid_lo[slot, :, columns] = split(source[i, at, columns])

    def targets(ref):
        return ref[1 : nloc + 1].reshape(nloc * rows, -1)

    total = dot3((targets(mid_hi), targets(mid_lo)), (right_hi[...], right_lo[...])).reshape(nloc, rows, width)
    for i, out in enumerate(outs):
        out[...] = total[i * per : (i + 1) * per]


def call(body, name, flops, out_shape, operands, scratch=(), smem=0):
    return pl.pallas_call(
        body,
        name=name,
        out_shape=out_shape,
        in_specs=[SMEM] * smem + [VMEM] * (len(operands) - smem),
        out_specs=jax.tree.map(lambda _: VMEM, out_shape),
        scratch_shapes=list(scratch),
        compiler_params=pltpu.CompilerParams(vmem_limit_bytes=24 * 2**20),
        cost_estimate=pl.CostEstimate(flops=flops, bytes_accessed=2**20, transcendentals=0),
    )(*operands)


def shards(psi, left_ops, right_ops, shifts, allowed):
    nloc, rows, width = psi.shape
    kops = left_ops.shape[0]
    n = lax.axis_size("op")
    route = ring_route(n)
    one = 6 * width**3

    outer, inner = [psi[:: nloc - 1]], [psi[1 : nloc - 1]]
    for _ in range(n - 1):
        outer.append(lax.ppermute(outer[-1], "op", route))
        inner.append(lax.ppermute(inner[-1], "op", route))

    def halo(blocks):
        above = shifted(jnp.concatenate([b[1:] for b in blocks]), ("sec", "sub"), 1)
        below = shifted(jnp.concatenate([b[:1] for b in blocks]), ("sec", "sub"), -1)
        return above, below

    above_head, below_head = halo(outer[:-1])
    above_last, below_last = halo(outer[-1:])

    half = jax.ShapeDtypeStruct((kops, width, width), BF16)
    tall = jax.ShapeDtypeStruct((kops * width, width), BF16)
    left_hi, left_lo, right_hi, right_lo = call(
        prepare, "prepare", 4 * kops * one, [half, half, tall, tall], [left_ops, right_ops]
    )

    def middle(sectors):
        return jax.ShapeDtypeStruct((sectors, width, kops * width), F32)

    def two(kind):
        return pltpu.VMEM((2, width, width), kind)

    mid_outer = call(
        functools.partial(first_stage, n, (0, nloc - 1), nloc), "outer", 2 * kops * one, middle(2),
        [allowed, *outer, left_hi, left_lo], [two(F32)], 1,
    )
    mid_halo = call(
        functools.partial(first_stage_halo, n, nloc), "halo", kops * one, middle(1),
        [shifts, allowed, above_head, above_last, below_head, below_last, left_hi, left_lo], [two(F32), two(BF16), two(BF16)], 2,
    )
    mid_inner = call(
        functools.partial(first_stage, n, tuple(range(1, nloc - 1)), nloc), "inner", (nloc - 2) * kops * one, middle(nloc - 2),
        [allowed, *inner, left_hi, left_lo], [pltpu.VMEM((nloc - 2, width, width), F32)], 1,
    )

    chunk = [jax.ShapeDtypeStruct((nloc // 2, rows, width), F32)] * 2

    def own(step):
        return call(
            functools.partial(second_stage, n, step), "chunk", nloc * kops * one // n, chunk,
            [shifts, mid_outer, mid_halo, mid_inner, right_hi, right_lo],
            [pltpu.VMEM((nloc + 2, rows, kops * width), BF16)] * 2, 1,
        )

    result = own(0)
    for step in range(1, n):
        result = [lax.ppermute(r, "op", route) + o for r, o in zip(result, own(step))]
    return jnp.concatenate(result)


def solution(mesh):
    return jax.shard_map(
        shards,
        mesh=mesh,
        in_specs=(
            P(("parts", "sec", "sub"), "op", None),
            P("op", None, None),
            P("op", None, None),
            P("op"),
            P("op", None),
        ),
        out_specs=P(("parts", "sec", "sub"), "op", None),
        check_vma=False,
    )
```

```python
import functools

import jax
import jax.numpy as jnp
from jax import lax
from jax.experimental import pallas as pl
from jax.experimental.pallas import tpu as pltpu
from jax.sharding import PartitionSpec as P

F32, BF16 = jnp.float32, jnp.bfloat16
SMEM = pl.BlockSpec(memory_space=pltpu.SMEM)
VMEM = pl.BlockSpec(memory_space=pltpu.VMEM)


def shifted(block, axis, distance):
    devices = range(lax.axis_size(axis))
    route = [(i - distance, i) for i in devices if i - distance in devices]
    return lax.ppermute(block, axis, route)


def ring_route(n):
    order = [0] + [i for i in range(n) if i % 2] + [i for i in reversed(range(1, n)) if i % 2 == 0]
    return [(order[i], order[(i + 1) % n]) for i in range(n)]


def ring_place(n, steps_back):
    me = lax.axis_index("op")
    place = jnp.where(me == 0, 0, jnp.where(lax.rem(me, 2) == 1, (me + 1) // 2, n - me // 2))
    at = lax.rem(place - steps_back + 2 * n, n)
    return jnp.where(at == 0, 0, jnp.where(at <= n // 2, 2 * at - 1, 2 * (n - at)))


def split(x):
    hi = x.astype(BF16)
    return hi, (x - hi.astype(F32)).astype(BF16)


def dot3(a, b):
    one = functools.partial(jnp.dot, preferred_element_type=F32)
    return one(a[0], b[0]) + (one(a[0], b[1]) + one(a[1], b[0]))


def prepare(left_ref, right_ref, left_parts, right_hi, right_lo, zero):
    kops, width, _ = left_ref.shape
    zero[...] = jnp.zeros_like(zero)
    for k in range(kops):
        hi, lo = split(left_ref[k])
        left_parts[k] = jnp.concatenate([hi, hi, lo], axis=1)
        right_hi[k * width : (k + 1) * width, :], right_lo[k * width : (k + 1) * width, :] = split(right_ref[k].T)


def stacked(block):
    hi, lo = split(block)
    return jnp.concatenate([hi, lo, hi], axis=0)


def place_rows(n, target, blocks):
    for j, block in enumerate(blocks):
        rows = block.shape[-2]
        target[..., pl.ds(pl.multiple_of(ring_place(n, j) * rows, rows), rows), :] = block


def first_stage(n, nloc, sectors, allowed_ref, *refs):
    left_parts, middle, psi = refs[n:]
    kops, width, _ = left_parts.shape
    first = lax.axis_index(("sec", "sub")) * nloc
    place_rows(n, psi, [ref[...] for ref in refs[:n]])
    parts = [stacked(psi[i]) for i in range(len(sectors))]
    for k in range(kops):
        for i, s in enumerate(sectors):
            block = jnp.dot(left_parts[k], parts[i], preferred_element_type=F32)
            middle[i, :, k * width : (k + 1) * width] = block * allowed_ref[k, first + s].astype(F32)


def first_stage_outside(n, nloc, shifts_ref, allowed_ref, above, below, left_parts, middle, psi, parts):
    kops, width, _ = left_parts.shape
    first = lax.axis_index(("sec", "sub")) * nloc
    place_rows(n, psi.at[0], [above[j] for j in range(n)])
    place_rows(n, psi.at[1], [below[j] for j in range(n)])
    for i in range(2):
        parts[i] = stacked(psi[i])
    for k in range(kops):
        up = shifts_ref[k] == 1
        source = jnp.where(up, jnp.maximum(first - 1, 0), jnp.minimum(first + nloc, allowed_ref.shape[1] - 1))
        block = jnp.dot(left_parts[k], parts[jnp.where(up, 0, 1)], preferred_element_type=F32)
        middle[:, k * width : (k + 1) * width] = block * allowed_ref[k, source].astype(F32)


def second_stage(n, step, shifts_ref, outer, inner, outside, right_hi, right_lo, *outs):
    per, rows, width = outs[0].shape
    nloc = per * len(outs)
    at = pl.ds(pl.multiple_of(ring_place(n, step + 1) * rows, rows), rows)
    last = nloc - 1
    highs, lows = [], []
    for k in range(shifts_ref.shape[0]):
        shift = shifts_ref[k]
        columns = slice(k * width, (k + 1) * width)

        def source(t, shift=shift, columns=columns):
            s = t - shift
            block = inner[jnp.clip(s - 1, 0, nloc - 3), at, columns]
            if t <= 1:
                block = jnp.where(s == 0, outer[0, at, columns], block)
            if t >= last - 1:
                block = jnp.where(s == last, outer[1, at, columns], block)
            if t in (0, last):
                block = jnp.where((s < 0) | (s > last), outside[at, columns], block)
            return block

        hi, lo = split(jnp.concatenate([source(t) for t in range(nloc)]))
        highs.append(hi)
        lows.append(lo)
    high, low = jnp.concatenate(highs, axis=1), jnp.concatenate(lows, axis=1)
    total = dot3((high, low), (right_hi[...], right_lo[...])).reshape(nloc, rows, width)
    for i, out in enumerate(outs):
        out[...] = total[i * per : (i + 1) * per]


def call(body, name, flops, out_shape, in_specs, operands, scratch=()):
    return pl.pallas_call(
        body,
        name=name,
        out_shape=out_shape,
        in_specs=in_specs,
        out_specs=jax.tree.map(lambda _: VMEM, out_shape),
        scratch_shapes=list(scratch),
        compiler_params=pltpu.CompilerParams(vmem_limit_bytes=24 * 2**20),
        cost_estimate=pl.CostEstimate(flops=flops, bytes_accessed=2**20, transcendentals=0),
    )(*operands)


def shards(psi, left_ops, right_ops, shifts, allowed):
    nloc, rows, width = psi.shape
    kops = left_ops.shape[0]
    n = lax.axis_size("op")
    route = ring_route(n)
    one = 6 * width**3

    tall = jax.ShapeDtypeStruct((kops * width, width), BF16)
    parts = jax.ShapeDtypeStruct((kops, width, 3 * width), BF16)
    zero = jax.ShapeDtypeStruct((1, 128), F32)
    left_parts, right_hi, right_lo, zero = call(
        prepare, "prepare", 4 * kops * one, [parts, tall, tall, zero], [VMEM] * 2, [left_ops, right_ops]
    )

    outer, inner = [psi[:: nloc - 1]], [psi[1 : nloc - 1]]
    for step in range(n - 1):
        outer.append(lax.ppermute(outer[-1] + zero[0, 0] if step == 1 else outer[-1], "op", route))
        inner.append(lax.ppermute(inner[-1] + zero[0, 0] if step == 1 else inner[-1], "op", route))

    above = shifted(jnp.concatenate([b[1:] for b in outer]), ("sec", "sub"), 1)
    below = shifted(jnp.concatenate([b[:1] for b in outer]), ("sec", "sub"), -1)

    def stage(name, sectors, blocks):
        operands = [allowed, *blocks, left_parts]
        return call(
            functools.partial(first_stage, n, nloc, sectors), name, 2 * len(sectors) * kops * one,
            jax.ShapeDtypeStruct((len(sectors), width, kops * width), F32), [SMEM] + [VMEM] * (n + 1), operands,
            [pltpu.VMEM((len(sectors), width, width), F32)],
        )

    mid_outer = stage("outer", (0, nloc - 1), outer)
    mid_inner = stage("inner", tuple(range(1, nloc - 1)), inner)
    mid_outside = call(
        functools.partial(first_stage_outside, n, nloc), "outside", 2 * kops * one,
        jax.ShapeDtypeStruct((width, kops * width), F32), [SMEM] * 2 + [VMEM] * 3, [shifts, allowed, above, below, left_parts],
        [pltpu.VMEM((2, width, width), F32), pltpu.VMEM((2, 3 * width, width), BF16)],
    )
    chunk = [jax.ShapeDtypeStruct((nloc // 2, rows, width), F32)] * 2

    def own(step):
        return call(
            functools.partial(second_stage, n, step), "chunk", nloc * kops * one // n, chunk,
            [SMEM] + [VMEM] * 5, [shifts, mid_outer, mid_inner, mid_outside, right_hi, right_lo],
        )

    result = own(0)
    for step in range(1, n):
        result = [lax.ppermute(r, "op", route) + o for r, o in zip(result, own(step))]
    return jnp.concatenate(result)


def solution(mesh):
    return jax.shard_map(
        shards,
        mesh=mesh,
        in_specs=(
            P(("parts", "sec", "sub"), "op", None),
            P("op", None, None),
            P("op", None, None),
            P("op"),
            P("op", None),
        ),
        out_specs=P(("parts", "sec", "sub"), "op", None),
        check_vma=False,
    )
```

```python
import functools

import jax
import jax.numpy as jnp
from jax import lax
from jax.experimental import pallas as pl
from jax.experimental.pallas import tpu as pltpu
from jax.sharding import PartitionSpec as P

F32, BF16 = jnp.float32, jnp.bfloat16
SMEM = pl.BlockSpec(memory_space=pltpu.SMEM)
VMEM = pl.BlockSpec(memory_space=pltpu.VMEM)


def shifted(block, axis, distance):
    devices = range(lax.axis_size(axis))
    route = [(i - distance, i) for i in devices if i - distance in devices]
    return lax.ppermute(block, axis, route)


def ring_route(n):
    order = [0] + [i for i in range(n) if i % 2] + [i for i in reversed(range(1, n)) if i % 2 == 0]
    return [(order[i], order[(i + 1) % n]) for i in range(n)]


def ring_place(n, steps_back):
    me = lax.axis_index("op")
    place = jnp.where(me == 0, 0, jnp.where(lax.rem(me, 2) == 1, (me + 1) // 2, n - me // 2))
    at = lax.rem(place - steps_back + 2 * n, n)
    return jnp.where(at == 0, 0, jnp.where(at <= n // 2, 2 * at - 1, 2 * (n - at)))


def split(x):
    hi = x.astype(BF16)
    return hi, (x - hi.astype(F32)).astype(BF16)


def dot3(a, b):
    one = functools.partial(jnp.dot, preferred_element_type=F32)
    return one(a[0], b[0]) + (one(a[0], b[1]) + one(a[1], b[0]))


def prepare(left_ref, right_ref, left_parts, right_hi, right_lo, zero):
    n, kops, rows, _ = left_parts.shape
    width = left_ref.shape[1]
    zero[...] = jnp.zeros_like(zero)
    for k in range(kops):
        hi, lo = split(left_ref[k])
        parts = jnp.concatenate([hi, hi, lo], axis=1)
        for c in range(n):
            left_parts[c, k] = parts[c * rows : (c + 1) * rows]
        right_hi[k * width : (k + 1) * width, :], right_lo[k * width : (k + 1) * width, :] = split(right_ref[k].T)


def stacked(block):
    hi, lo = split(block)
    return jnp.concatenate([hi, lo, hi], axis=0)


def place_rows(n, target, blocks):
    for j, block in enumerate(blocks):
        rows = block.shape[-2]
        target[..., pl.ds(pl.multiple_of(ring_place(n, j) * rows, rows), rows), :] = block


def assemble(n, *refs):
    parts, psi = refs[n:]
    place_rows(n, psi, [ref[...] for ref in refs[:n]])
    for i in range(parts.shape[0]):
        parts[i] = stacked(psi[i])


def first_product(left, parts):
    return jnp.dot(left, parts, preferred_element_type=F32)


def chunk_left(n, step, left_parts):
    return left_parts[ring_place(n, step + 1)].reshape(-1, left_parts.shape[-1])


def own_sectors(n, *refs):
    (outer, left_parts), (inner, middle, psi) = refs[n : n + 2], refs[n + 2 :]
    assemble(n, *refs[:n], inner, psi)
    left = chunk_left(n, 0, left_parts)
    middle[0] = first_product(left, outer[0])
    for i in range(inner.shape[0]):
        middle[i + 1] = first_product(left, inner[i])
    middle[inner.shape[0] + 1] = first_product(left, outer[1])


def second_product(nloc, shifts_ref, allowed_ref, middle, right_hi, right_lo, outs):
    kops = shifts_ref.shape[0]
    rows, width = outs[0].shape[1:]
    first = lax.axis_index(("sec", "sub")) * nloc
    highs, lows = [], []
    for k in range(kops):
        shift = shifts_ref[k]
        blocks = []
        for t in range(nloc):
            below, same, above = [middle[t + d][k * rows : (k + 1) * rows] for d in range(3)]
            block = jnp.where(shift == 0, same, jnp.where(shift == 1, below, above))
            source = jnp.clip(first + t - shift, 0, allowed_ref.shape[1] - 1)
            blocks.append(block * allowed_ref[k, source].astype(F32))
        hi, lo = split(jnp.concatenate(blocks))
        highs.append(hi)
        lows.append(lo)
    high, low = jnp.concatenate(highs, axis=1), jnp.concatenate(lows, axis=1)
    total = dot3((high, low), (right_hi[...], right_lo[...])).reshape(nloc, rows, width)
    per = nloc // len(outs)
    for i, out in enumerate(outs):
        out[...] = total[i * per : (i + 1) * per]


def outside_sectors(n, above, below, left_parts, outside, middle, psi):
    place_rows(n, psi.at[0], [above[j] for j in range(n)])
    place_rows(n, psi.at[1], [below[j] for j in range(n)])
    left = chunk_left(n, 0, left_parts)
    for i in range(2):
        outside[i] = stacked(psi[i])
        middle[i] = first_product(left, outside[i])


def first_chunk(n, nloc, shifts_ref, allowed_ref, own, ends, right_hi, right_lo, *outs):
    middle = [ends[0], *[own[i] for i in range(nloc)], ends[1]]
    second_product(nloc, shifts_ref, allowed_ref, middle, right_hi, right_lo, outs)


def later_chunk(n, nloc, step, shifts_ref, allowed_ref, outer, inner, outside, left_parts, right_hi, right_lo, *outs):
    left = chunk_left(n, step, left_parts)
    sources = [outside.at[0], outer.at[0], *[inner.at[i] for i in range(nloc - 2)], outer.at[1], outside.at[1]]
    middle = [first_product(left, ref[...]) for ref in sources]
    second_product(nloc, shifts_ref, allowed_ref, middle, right_hi, right_lo, outs)


def call(body, name, flops, out_shape, in_specs, operands, scratch=()):
    return pl.pallas_call(
        body,
        name=name,
        out_shape=out_shape,
        in_specs=in_specs,
        out_specs=jax.tree.map(lambda _: VMEM, out_shape),
        scratch_shapes=list(scratch),
        compiler_params=pltpu.CompilerParams(vmem_limit_bytes=24 * 2**20),
        cost_estimate=pl.CostEstimate(flops=flops, bytes_accessed=2**20, transcendentals=0),
    )(*operands)


def shards(psi, left_ops, right_ops, shifts, allowed):
    nloc, rows, width = psi.shape
    kops = left_ops.shape[0]
    n = lax.axis_size("op")
    route = ring_route(n)
    one = 6 * width**3

    tall = jax.ShapeDtypeStruct((kops * width, width), BF16)
    parts = jax.ShapeDtypeStruct((n, kops, rows, 3 * width), BF16)
    zero = jax.ShapeDtypeStruct((1, 128), F32)
    left_parts, right_hi, right_lo, zero = call(
        prepare, "prepare", 4 * kops * one, [parts, tall, tall, zero], [VMEM] * 2, [left_ops, right_ops]
    )

    outer, inner = [psi[:: nloc - 1]], [psi[1 : nloc - 1]]
    for step in range(n - 1):
        inner.append(lax.ppermute(inner[-1] + zero[0, 0] if step == 1 else inner[-1], "op", route))
        outer.append(lax.ppermute(outer[-1] + zero[0, 0] if step == 1 else outer[-1], "op", route))

    above = shifted(jnp.concatenate([b[1:] for b in outer]), ("sec", "sub"), 1)
    below = shifted(jnp.concatenate([b[:1] for b in outer]), ("sec", "sub"), -1)

    def split_parts(sectors):
        return jax.ShapeDtypeStruct((sectors, 3 * width, width), BF16)

    def whole(sectors):
        return [pltpu.VMEM((sectors, width, width), F32)]

    parts_outer = call(functools.partial(assemble, n), "assemble", one // 2, split_parts(2), [VMEM] * n, outer, whole(2))
    parts_inner, own = call(
        functools.partial(own_sectors, n), "own", 4 * kops * one,
        [split_parts(nloc - 2), jax.ShapeDtypeStruct((nloc, kops * rows, width), F32)],
        [VMEM] * (n + 2), [*inner, parts_outer, left_parts], whole(nloc - 2),
    )
    parts_outside, ends = call(
        functools.partial(outside_sectors, n), "outside", 2 * kops * one,
        [split_parts(2), jax.ShapeDtypeStruct((2, kops * rows, width), F32)],
        [VMEM] * 3, [above, below, left_parts], whole(2),
    )
    chunk = [jax.ShapeDtypeStruct((nloc // 2, rows, width), F32)] * 2
    result = call(
        functools.partial(first_chunk, n, nloc), "first_chunk", nloc * kops * one // n, chunk,
        [SMEM] * 2 + [VMEM] * 4, [shifts, allowed, own, ends, right_hi, right_lo],
    )

    def mine(step):
        return call(
            functools.partial(later_chunk, n, nloc, step), "chunk", 4 * nloc * kops * one // n, chunk,
            [SMEM] * 2 + [VMEM] * 6,
            [shifts, allowed, parts_outer, parts_inner, parts_outside, left_parts, right_hi, right_lo],
        )

    for step in range(1, n):
        result = [lax.ppermute(r, "op", route) + o for r, o in zip(result, mine(step))]
    return jnp.concatenate(result)


def solution(mesh):
    return jax.shard_map(
        shards,
        mesh=mesh,
        in_specs=(
            P(("parts", "sec", "sub"), "op", None),
            P("op", None, None),
            P("op", None, None),
            P("op"),
            P("op", None),
        ),
        out_specs=P(("parts", "sec", "sub"), "op", None),
        check_vma=False,
    )
```

```python
import functools

import jax
import jax.numpy as jnp
from jax import lax
from jax.experimental import pallas as pl
from jax.experimental.pallas import tpu as pltpu
from jax.sharding import PartitionSpec as P

F32, BF16 = jnp.float32, jnp.bfloat16
SMEM = pl.BlockSpec(memory_space=pltpu.SMEM)
VMEM = pl.BlockSpec(memory_space=pltpu.VMEM)


def shifted(block, axis, distance):
    devices = range(lax.axis_size(axis))
    route = [(i - distance, i) for i in devices if i - distance in devices]
    return lax.ppermute(block, axis, route)


def ring_route(n):
    order = [0] + [i for i in range(n) if i % 2] + [i for i in reversed(range(1, n)) if i % 2 == 0]
    return [(order[i], order[(i + 1) % n]) for i in range(n)]


def ring_place(n, steps_back):
    me = lax.axis_index("op")
    place = jnp.where(me == 0, 0, jnp.where(lax.rem(me, 2) == 1, (me + 1) // 2, n - me // 2))
    at = lax.rem(place - steps_back + 2 * n, n)
    return jnp.where(at == 0, 0, jnp.where(at <= n // 2, 2 * at - 1, 2 * (n - at)))


def exchanged(n):
    return n == 4


def block_owner(n, j):
    return jnp.bitwise_xor(lax.axis_index("op"), j) if exchanged(n) else ring_place(n, j)


def chunk_target(n, step):
    return jnp.bitwise_xor(lax.axis_index("op"), n - 1 - step) if exchanged(n) else ring_place(n, step + 1)


def split(x):
    hi = x.astype(BF16)
    return hi, (x - hi.astype(F32)).astype(BF16)


def dot3(a, b):
    one = functools.partial(jnp.dot, preferred_element_type=F32)
    return one(a[0], b[0]) + (one(a[0], b[1]) + one(a[1], b[0]))


def prepare(left_ref, right_ref, left_parts, right_hi, right_lo, zero):
    n, kops, rows, _ = left_parts.shape
    width = left_ref.shape[1]
    zero[...] = jnp.zeros_like(zero)
    for k in range(kops):
        hi, lo = split(left_ref[k])
        parts = jnp.concatenate([hi, hi, lo], axis=1)
        for c in range(n):
            left_parts[c, k] = parts[c * rows : (c + 1) * rows]
        right_hi[k * width : (k + 1) * width, :], right_lo[k * width : (k + 1) * width, :] = split(right_ref[k].T)


def stacked(block):
    hi, lo = split(block)
    return jnp.concatenate([hi, lo, hi], axis=0)


def place_rows(n, target, blocks):
    for j, block in enumerate(blocks):
        rows = block.shape[-2]
        target[..., pl.ds(pl.multiple_of(block_owner(n, j) * rows, rows), rows), :] = block


def assemble(n, *refs):
    parts, psi = refs[n:]
    place_rows(n, psi, [ref[...] for ref in refs[:n]])
    for i in range(parts.shape[0]):
        parts[i] = stacked(psi[i])


def first_product(left, parts):
    return jnp.dot(left, parts, preferred_element_type=F32)


def chunk_left(n, step, left_parts):
    return left_parts[chunk_target(n, step)].reshape(-1, left_parts.shape[-1])


def own_sectors(n, *refs):
    (outer, left_parts), (inner, middle, psi) = refs[n : n + 2], refs[n + 2 :]
    assemble(n, *refs[:n], inner, psi)
    left = chunk_left(n, 0, left_parts)
    middle[0] = first_product(left, outer[0])
    for i in range(inner.shape[0]):
        middle[i + 1] = first_product(left, inner[i])
    middle[inner.shape[0] + 1] = first_product(left, outer[1])


def second_product(nloc, shifts_ref, allowed_ref, middle, right_hi, right_lo, out):
    kops = shifts_ref.shape[0]
    rows, width = out.shape[1:]
    first = lax.axis_index(("sec", "sub")) * nloc
    highs, lows = [], []
    for k in range(kops):
        shift = shifts_ref[k]
        blocks = []
        for t in range(nloc):
            source = jnp.clip(first + t - shift, 0, allowed_ref.shape[1] - 1)
            block = middle[t + 1 - shift, k * rows : (k + 1) * rows]
            blocks.append(block * allowed_ref[k, source].astype(F32))
        hi, lo = split(jnp.concatenate(blocks))
        highs.append(hi)
        lows.append(lo)
    high, low = jnp.concatenate(highs, axis=1), jnp.concatenate(lows, axis=1)
    out[...] = dot3((high, low), (right_hi[...], right_lo[...])).reshape(nloc, rows, width)


def first_chunk(n, nloc, shifts_ref, allowed_ref, own, above, below, left_parts, right_hi, right_lo, out, outside, psi, middle):
    place_rows(n, psi.at[0], [above[j] for j in range(n)])
    place_rows(n, psi.at[1], [below[j] for j in range(n)])
    left = chunk_left(n, 0, left_parts)
    for i in range(2):
        outside[i] = stacked(psi[i])
        middle[i * (nloc + 1)] = first_product(left, outside[i])
    for i in range(nloc):
        middle[i + 1] = own[i]
    second_product(nloc, shifts_ref, allowed_ref, middle, right_hi, right_lo, out)


def later_chunk(n, nloc, step, shifts_ref, allowed_ref, outer, inner, outside, left_parts, right_hi, right_lo, out, middle):
    left = chunk_left(n, step, left_parts)
    sources = [outside.at[0], outer.at[0], *[inner.at[i] for i in range(nloc - 2)], outer.at[1], outside.at[1]]
    for i, ref in enumerate(sources):
        middle[i] = first_product(left, ref[...])
    second_product(nloc, shifts_ref, allowed_ref, middle, right_hi, right_lo, out)


def call(body, name, flops, out_shape, in_specs, operands, scratch=()):
    return pl.pallas_call(
        body,
        name=name,
        out_shape=out_shape,
        in_specs=in_specs,
        out_specs=jax.tree.map(lambda _: VMEM, out_shape),
        scratch_shapes=list(scratch),
        compiler_params=pltpu.CompilerParams(vmem_limit_bytes=24 * 2**20),
        cost_estimate=pl.CostEstimate(flops=flops, bytes_accessed=2**20, transcendentals=0),
    )(*operands)


def gather(n, psi, zero):
    nloc = psi.shape[0]
    halves = [lambda b: b[:: nloc - 1], lambda b: b[1 : nloc - 1]]
    if not exchanged(n):
        blocks = [[part(psi)] for part in halves]
        for _ in range(n - 1):
            for held in blocks:
                held.append(lax.ppermute(held[-1], "op", ring_route(n)))
        return blocks
    two = lax.ppermute(psi, "op", [(z, z ^ 2) for z in range(n)])
    one = lax.ppermute(psi, "op", [(z, z ^ 1) for z in range(n)])
    late = 0 * two + zero[0, 0]
    blocks = []
    for part in halves:
        passed = lax.ppermute(part(two), "op", [(1, 0), (2, 3)])
        direct = lax.ppermute(part(psi) + part(late), "op", [(1, 2), (2, 1)])
        blocks.append([part(psi), part(one), part(two), passed + direct])
    return blocks


def scatter(n, mine):
    result = mine(0)
    if not exchanged(n):
        for step in range(1, n):
            result = lax.ppermute(result, "op", ring_route(n)) + mine(step)
        return result
    passed = lax.ppermute(result, "op", [(0, 1), (3, 2)])
    direct = lax.ppermute(result, "op", [(1, 2), (2, 1)])
    far = mine(1) + passed
    two = lax.ppermute(far, "op", [(z, z ^ 2) for z in range(n)])
    one = lax.ppermute(mine(2), "op", [(z, z ^ 1) for z in range(n)])
    return mine(3) + direct + two + one


def shards(psi, left_ops, right_ops, shifts, allowed):
    nloc, rows, width = psi.shape
    kops = left_ops.shape[0]
    n = lax.axis_size("op")
    one = 6 * width**3

    tall = jax.ShapeDtypeStruct((kops * width, width), BF16)
    parts = jax.ShapeDtypeStruct((n, kops, rows, 3 * width), BF16)
    zero = jax.ShapeDtypeStruct((1, 128), F32)
    left_parts, right_hi, right_lo, zero = call(
        prepare, "prepare", 4 * kops * one, [parts, tall, tall, zero], [VMEM] * 2, [left_ops, right_ops]
    )
    outer, inner = gather(n, psi, zero)
    above = shifted(jnp.concatenate([b[1:] for b in outer]), ("sec", "sub"), 1)
    below = shifted(jnp.concatenate([b[:1] for b in outer]), ("sec", "sub"), -1)

    def split_parts(sectors):
        return jax.ShapeDtypeStruct((sectors, 3 * width, width), BF16)

    def whole(sectors):
        return pltpu.VMEM((sectors, width, width), F32)

    parts_outer = call(functools.partial(assemble, n), "assemble", one // 2, split_parts(2), [VMEM] * n, outer, [whole(2)])
    parts_inner, own = call(
        functools.partial(own_sectors, n), "own", 4 * kops * one,
        [split_parts(nloc - 2), jax.ShapeDtypeStruct((nloc, kops * rows, width), F32)],
        [VMEM] * (n + 2), [*inner, parts_outer, left_parts], [whole(nloc - 2)],
    )
    chunk = jax.ShapeDtypeStruct((nloc, rows, width), F32)
    middle = pltpu.VMEM((nloc + 2, kops * rows, width), F32)
    first, parts_outside = call(
        functools.partial(first_chunk, n, nloc), "first_chunk", 2 * nloc * kops * one // n, [chunk, split_parts(2)],
        [SMEM] * 2 + [VMEM] * 6, [shifts, allowed, own, above, below, left_parts, right_hi, right_lo], [whole(2), middle],
    )

    def mine(step):
        if step == 0:
            return first
        return call(
            functools.partial(later_chunk, n, nloc, step), "chunk", 4 * nloc * kops * one // n, chunk,
            [SMEM] * 2 + [VMEM] * 6,
            [shifts, allowed, parts_outer, parts_inner, parts_outside, left_parts, right_hi, right_lo], [middle],
        )

    return scatter(n, mine)


def solution(mesh):
    return jax.shard_map(
        shards,
        mesh=mesh,
        in_specs=(
            P(("parts", "sec", "sub"), "op", None),
            P("op", None, None),
            P("op", None, None),
            P("op"),
            P("op", None),
        ),
        out_specs=P(("parts", "sec", "sub"), "op", None),
        check_vma=False,
    )
```

```python
import functools

import jax
import jax.numpy as jnp
from jax import lax
from jax.experimental import pallas as pl
from jax.experimental.pallas import tpu as pltpu
from jax.sharding import PartitionSpec as P

F32, BF16 = jnp.float32, jnp.bfloat16
SMEM = pl.BlockSpec(memory_space=pltpu.SMEM)
VMEM = pl.BlockSpec(memory_space=pltpu.VMEM)


def shifted(block, axis, distance):
    devices = range(lax.axis_size(axis))
    route = [(i - distance, i) for i in devices if i - distance in devices]
    return lax.ppermute(block, axis, route)


def ring_route(n):
    order = [0] + [i for i in range(n) if i % 2] + [i for i in reversed(range(1, n)) if i % 2 == 0]
    return [(order[i], order[(i + 1) % n]) for i in range(n)]


def ring_place(n, steps_back):
    me = lax.axis_index("op")
    place = jnp.where(me == 0, 0, jnp.where(lax.rem(me, 2) == 1, (me + 1) // 2, n - me // 2))
    at = lax.rem(place - steps_back + 2 * n, n)
    return jnp.where(at == 0, 0, jnp.where(at <= n // 2, 2 * at - 1, 2 * (n - at)))


def split(x):
    hi = x.astype(BF16)
    return hi, (x - hi.astype(F32)).astype(BF16)


def dot3(a, b):
    one = functools.partial(jnp.dot, preferred_element_type=F32)
    return one(a[0], b[0]) + (one(a[0], b[1]) + one(a[1], b[0]))


def prepare(left_ref, right_ref, left_parts, right_hi, right_lo, zero):
    n, kops, rows, _ = left_parts.shape
    width = left_ref.shape[1]
    zero[...] = jnp.zeros_like(zero)
    for k in range(kops):
        hi, lo = split(left_ref[k])
        parts = jnp.concatenate([hi, hi, lo], axis=1)
        for c in range(n):
            left_parts[c, k] = parts[c * rows : (c + 1) * rows]
        right_hi[k * width : (k + 1) * width, :], right_lo[k * width : (k + 1) * width, :] = split(right_ref[k].T)


def stacked(block):
    hi, lo = split(block)
    return jnp.concatenate([hi, lo, hi], axis=0)


def place_rows(n, target, blocks):
    for j, block in enumerate(blocks):
        rows = block.shape[-2]
        target[..., pl.ds(pl.multiple_of(ring_place(n, j) * rows, rows), rows), :] = block


def assemble(n, *refs):
    parts, psi = refs[n:]
    place_rows(n, psi, [ref[...] for ref in refs[:n]])
    for i in range(parts.shape[0]):
        parts[i] = stacked(psi[i])


def first_product(left, parts, allowed_ref, source, high, low):
    kops, sectors = allowed_ref.shape
    block = jnp.dot(left, parts, preferred_element_type=F32)
    rows = block.shape[0] // kops
    source = jnp.clip(source, 0, sectors - 1)
    for k in range(kops):
        at = slice(k * rows, (k + 1) * rows)
        high[at], low[at] = split(block[at] * allowed_ref[k, source].astype(F32))


def chunk_left(n, step, left_parts):
    return left_parts[ring_place(n, step + 1)].reshape(-1, left_parts.shape[-1])


def own_sectors(n, allowed_ref, *refs):
    (outer, left_parts), (inner, high, low, psi) = refs[n : n + 2], refs[n + 2 :]
    assemble(n, *refs[:n], inner, psi)
    left = chunk_left(n, 0, left_parts)
    nloc = high.shape[0]
    first = lax.axis_index(("sec", "sub")) * nloc
    sources = [outer.at[0], *[inner.at[i] for i in range(nloc - 2)], outer.at[1]]
    for i, ref in enumerate(sources):
        first_product(left, ref[...], allowed_ref, first + i, high.at[i], low.at[i])


def outside_sectors(n, nloc, allowed_ref, above, below, left_parts, outside, high, low, psi):
    place_rows(n, psi.at[0], [above[j] for j in range(n)])
    place_rows(n, psi.at[1], [below[j] for j in range(n)])
    left = chunk_left(n, 0, left_parts)
    first = lax.axis_index(("sec", "sub")) * nloc
    for i in range(2):
        outside[i] = stacked(psi[i])
        first_product(left, outside[i], allowed_ref, first - 1 + i * (nloc + 1), high.at[i], low.at[i])


def second_product(targets, shifts_ref, high, low, right_hi, right_lo, out):
    kops = shifts_ref.shape[0]
    _, rows, width = out.shape

    def left(parts):
        columns = []
        for k in range(kops):
            shift, at = shifts_ref[k], slice(k * rows, (k + 1) * rows)
            blocks = []
            for t in targets:
                below, same, above = [parts[t + d][at] for d in range(3)]
                blocks.append(jnp.where(shift == 0, same, jnp.where(shift == 1, below, above)))
            columns.append(jnp.concatenate(blocks))
        return jnp.concatenate(columns, axis=1)

    out[...] = dot3((left(high), left(low)), (right_hi[...], right_lo[...])).reshape(len(targets), rows, width)


def first_inner(nloc, shifts_ref, high, low, right_hi, right_lo, out):
    own = [[None, *[ref.at[i] for i in range(nloc)], None] for ref in (high, low)]
    second_product(range(1, nloc - 1), shifts_ref, *own, right_hi, right_lo, out)


def first_outer(nloc, shifts_ref, high, low, end_high, end_low, right_hi, right_lo, out):
    pairs = ((high, end_high), (low, end_low))
    held = [[ends.at[0], *[ref.at[i] for i in range(nloc)], ends.at[1]] for ref, ends in pairs]
    second_product((0, nloc - 1), shifts_ref, *held, right_hi, right_lo, out)


def later_chunk(n, nloc, step, shifts_ref, allowed_ref, outer, inner, outside, left_parts, right_hi, right_lo, outer_out, inner_out, high, low):
    left = chunk_left(n, step, left_parts)
    first = lax.axis_index(("sec", "sub")) * nloc
    sources = [outside.at[0], outer.at[0], *[inner.at[i] for i in range(nloc - 2)], outer.at[1], outside.at[1]]
    for i, ref in enumerate(sources):
        first_product(left, ref[...], allowed_ref, first - 1 + i, high.at[i], low.at[i])
    held = [[ref.at[i] for i in range(nloc + 2)] for ref in (high, low)]
    second_product(range(1, nloc - 1), shifts_ref, *held, right_hi, right_lo, inner_out)
    second_product((0, nloc - 1), shifts_ref, *held, right_hi, right_lo, outer_out)


def call(body, name, flops, out_shape, in_specs, operands, scratch=()):
    return pl.pallas_call(
        body,
        name=name,
        out_shape=out_shape,
        in_specs=in_specs,
        out_specs=jax.tree.map(lambda _: VMEM, out_shape),
        scratch_shapes=list(scratch),
        compiler_params=pltpu.CompilerParams(vmem_limit_bytes=24 * 2**20),
        cost_estimate=pl.CostEstimate(flops=flops, bytes_accessed=2**20, transcendentals=0),
    )(*operands)


def shards(psi, left_ops, right_ops, shifts, allowed):
    nloc, rows, width = psi.shape
    kops = left_ops.shape[0]
    n = lax.axis_size("op")
    route = ring_route(n)
    one = 6 * width**3

    tall = jax.ShapeDtypeStruct((kops * width, width), BF16)
    parts = jax.ShapeDtypeStruct((n, kops, rows, 3 * width), BF16)
    zero = jax.ShapeDtypeStruct((1, 128), F32)
    left_parts, right_hi, right_lo, zero = call(
        prepare, "prepare", 4 * kops * one, [parts, tall, tall, zero], [VMEM] * 2, [left_ops, right_ops]
    )

    outer, inner = [psi[:: nloc - 1]], [psi[1 : nloc - 1]]
    for step in range(n - 1):
        inner.append(lax.ppermute(inner[-1] + zero[0, 0] if step == 1 else inner[-1], "op", route))
        outer.append(lax.ppermute(outer[-1] + zero[0, 0] if step == 1 else outer[-1], "op", route))

    above = shifted(jnp.concatenate([b[1:] for b in outer]), ("sec", "sub"), 1)
    below = shifted(jnp.concatenate([b[:1] for b in outer]), ("sec", "sub"), -1)

    def split_parts(sectors):
        return jax.ShapeDtypeStruct((sectors, 3 * width, width), BF16)

    def whole(sectors):
        return [pltpu.VMEM((sectors, width, width), F32)]

    parts_outer = call(functools.partial(assemble, n), "assemble", 4 * kops * one, split_parts(2), [VMEM] * n, outer, whole(2))
    def products(sectors):
        return [jax.ShapeDtypeStruct((sectors, kops * rows, width), BF16)] * 2

    chunk = jax.ShapeDtypeStruct((2, rows, width), F32)
    chunk_inner = jax.ShapeDtypeStruct((nloc - 2, rows, width), F32)
    parts_inner, *own = call(
        functools.partial(own_sectors, n), "own", 4 * kops * one, [split_parts(nloc - 2), *products(nloc)],
        [SMEM] + [VMEM] * (n + 2), [allowed, *inner, parts_outer, left_parts], whole(nloc - 2),
    )
    result_inner = call(
        functools.partial(first_inner, nloc), "first_inner", nloc * kops * one // n, chunk_inner,
        [SMEM] + [VMEM] * 4, [shifts, *own, right_hi, right_lo],
    )
    parts_outside, *ends = call(
        functools.partial(outside_sectors, n, nloc), "outside", 2 * kops * one, [split_parts(2), *products(2)],
        [SMEM] + [VMEM] * 3, [allowed, above, below, left_parts], whole(2),
    )
    result_outer = call(
        functools.partial(first_outer, nloc), "first_outer", nloc * kops * one // n, chunk,
        [SMEM] + [VMEM] * 6, [shifts, *own, *ends, right_hi, right_lo],
    )

    def mine(step):
        return call(
            functools.partial(later_chunk, n, nloc, step), "chunk", 4 * nloc * kops * one // n, [chunk, chunk_inner],
            [SMEM] * 2 + [VMEM] * 6,
            [shifts, allowed, parts_outer, parts_inner, parts_outside, left_parts, right_hi, right_lo],
            [pltpu.VMEM((nloc + 2, kops * rows, width), BF16)] * 2,
        )

    for step in range(1, n):
        next_outer, next_inner = mine(step)
        result_inner = lax.ppermute(result_inner, "op", route) + next_inner
        result_outer = lax.ppermute(result_outer, "op", route) + next_outer
    return jnp.concatenate([result_outer[:1], result_inner, result_outer[1:]])


def solution(mesh):
    return jax.shard_map(
        shards,
        mesh=mesh,
        in_specs=(
            P(("parts", "sec", "sub"), "op", None),
            P("op", None, None),
            P("op", None, None),
            P("op"),
            P("op", None),
        ),
        out_specs=P(("parts", "sec", "sub"), "op", None),
        check_vma=False,
    )
```

```python
import functools

import jax
import jax.numpy as jnp
from jax import lax
from jax.experimental import pallas as pl
from jax.experimental.pallas import tpu as pltpu
from jax.sharding import PartitionSpec as P

F32, BF16 = jnp.float32, jnp.bfloat16
SMEM = pl.BlockSpec(memory_space=pltpu.SMEM)
VMEM = pl.BlockSpec(memory_space=pltpu.VMEM)


def shifted(block, axis, distance):
    devices = range(lax.axis_size(axis))
    route = [(i - distance, i) for i in devices if i - distance in devices]
    return lax.ppermute(block, axis, route)


def ring_route(n):
    order = [0] + [i for i in range(n) if i % 2] + [i for i in reversed(range(1, n)) if i % 2 == 0]
    return [(order[i], order[(i + 1) % n]) for i in range(n)]


def ring_place(n, steps_back):
    me = lax.axis_index("op")
    place = jnp.where(me == 0, 0, jnp.where(lax.rem(me, 2) == 1, (me + 1) // 2, n - me // 2))
    at = lax.rem(place - steps_back + 2 * n, n)
    return jnp.where(at == 0, 0, jnp.where(at <= n // 2, 2 * at - 1, 2 * (n - at)))


def split(x):
    hi = x.astype(BF16)
    return hi, (x - hi.astype(F32)).astype(BF16)


def prepare(left_ref, right_ref, left_parts, right_hi, right_lo, zero):
    n, kops, rows, _ = left_parts.shape
    width = left_ref.shape[1]
    zero[...] = jnp.zeros_like(zero)
    for k in range(kops):
        hi, lo = split(left_ref[k])
        parts = jnp.concatenate([hi, hi, lo], axis=1)
        for c in range(n):
            left_parts[c, k] = parts[c * rows : (c + 1) * rows]
        right_hi[k * width : (k + 1) * width, :], right_lo[k * width : (k + 1) * width, :] = split(right_ref[k].T)


def stacked(block):
    hi, lo = split(block)
    return jnp.concatenate([hi, lo, hi], axis=0)


def place_rows(n, target, blocks):
    for j, block in enumerate(blocks):
        rows = block.shape[-2]
        target[..., pl.ds(pl.multiple_of(ring_place(n, j) * rows, rows), rows), :] = block


def assemble(n, *refs):
    parts, psi = refs[n:]
    place_rows(n, psi, [ref[...] for ref in refs[:n]])
    for i in range(parts.shape[0]):
        parts[i] = stacked(psi[i])


def first_product(left, parts, allowed_ref, source, high, low):
    kops, sectors = allowed_ref.shape
    block = jnp.dot(left, parts, preferred_element_type=F32)
    rows = block.shape[0] // kops
    source = jnp.clip(source, 0, sectors - 1)
    for k in range(kops):
        at = slice(k * rows, (k + 1) * rows)
        high[at], low[at] = split(block[at] * allowed_ref[k, source].astype(F32))


def chunk_left(n, step, left_parts):
    return left_parts[ring_place(n, step + 1)].reshape(-1, left_parts.shape[-1])


def own_sectors(n, allowed_ref, outer, *refs):
    left_parts, inner, high, low, psi = refs[n:]
    assemble(n, *refs[:n], inner, psi)
    left = chunk_left(n, 0, left_parts)
    nloc = high.shape[0]
    first = lax.axis_index(("sec", "sub")) * nloc
    sources = [outer.at[0], *[inner.at[i] for i in range(nloc - 2)], outer.at[1]]
    for i, ref in enumerate(sources):
        first_product(left, ref[...], allowed_ref, first + i, high.at[i], low.at[i])


def outside_sectors(n, nloc, allowed_ref, above, below, left_parts, outside, high, low, psi):
    place_rows(n, psi.at[0], [above[j] for j in range(n)])
    place_rows(n, psi.at[1], [below[j] for j in range(n)])
    left = chunk_left(n, 0, left_parts)
    first = lax.axis_index(("sec", "sub")) * nloc
    for i in range(2):
        outside[i] = stacked(psi[i])
        first_product(left, outside[i], allowed_ref, first - 1 + i * (nloc + 1), high.at[i], low.at[i])


def second_product(targets, shifts_ref, high, low, right_hi, right_lo, rows):
    kops, width = shifts_ref.shape[0], right_hi.shape[1]

    def left(parts):
        columns = []
        for k in range(kops):
            shift, at = shifts_ref[k], slice(k * rows, (k + 1) * rows)
            blocks = []
            for t in targets:
                below, same, above = [parts[t + d][at] for d in range(3)]
                blocks.append(jnp.where(shift == 0, same, jnp.where(shift == 1, below, above)))
            columns.append(jnp.concatenate(blocks))
        return jnp.concatenate(columns, axis=1)

    hi, lo = left(high), left(low)
    main = jnp.dot(jnp.concatenate([hi, lo]), right_hi[...], preferred_element_type=F32)
    total = main[: hi.shape[0]] + (main[hi.shape[0] :] + jnp.dot(hi, right_lo[...], preferred_element_type=F32))
    return total.reshape(len(targets), rows, width)


def first_inner(nloc, shifts_ref, high, low, right_hi, right_lo, out):
    own = [[None, *[ref.at[i] for i in range(nloc)], None] for ref in (high, low)]
    out[...] = second_product(range(1, nloc - 1), shifts_ref, *own, right_hi, right_lo, out.shape[1])


def first_outer(nloc, shifts_ref, high, low, end_high, end_low, right_hi, right_lo, out):
    pairs = ((high, end_high), (low, end_low))
    held = [[ends.at[0], *[ref.at[i] for i in range(nloc)], ends.at[1]] for ref, ends in pairs]
    out[...] = second_product((0, nloc - 1), shifts_ref, *held, right_hi, right_lo, out.shape[1])


def later_chunk(n, nloc, step, shifts_ref, allowed_ref, outer, inner, outside, left_parts, right_hi, right_lo, outer_out, inner_out, high, low):
    left = chunk_left(n, step, left_parts)
    first = lax.axis_index(("sec", "sub")) * nloc
    sources = [outside.at[0], outer.at[0], *[inner.at[i] for i in range(nloc - 2)], outer.at[1], outside.at[1]]
    for i, ref in enumerate(sources):
        first_product(left, ref[...], allowed_ref, first - 1 + i, high.at[i], low.at[i])
    held = [[ref.at[i] for i in range(nloc + 2)] for ref in (high, low)]
    total = second_product((0, nloc - 1, *range(1, nloc - 1)), shifts_ref, *held, right_hi, right_lo, outer_out.shape[1])
    outer_out[...] = total[:2]
    inner_out[...] = total[2:]


def call(body, name, flops, out_shape, in_specs, operands, scratch=()):
    return pl.pallas_call(
        body,
        name=name,
        out_shape=out_shape,
        in_specs=in_specs,
        out_specs=jax.tree.map(lambda _: VMEM, out_shape),
        scratch_shapes=list(scratch),
        compiler_params=pltpu.CompilerParams(vmem_limit_bytes=24 * 2**20),
        cost_estimate=pl.CostEstimate(flops=flops, bytes_accessed=2**20, transcendentals=0),
    )(*operands)


def shards(psi, left_ops, right_ops, shifts, allowed):
    nloc, rows, width = psi.shape
    kops = left_ops.shape[0]
    n = lax.axis_size("op")
    route = ring_route(n)
    one = 6 * width**3

    tall = jax.ShapeDtypeStruct((kops * width, width), BF16)
    parts = jax.ShapeDtypeStruct((n, kops, rows, 3 * width), BF16)
    zero = jax.ShapeDtypeStruct((1, 128), F32)
    left_parts, right_hi, right_lo, zero = call(
        prepare, "prepare", 4 * kops * one, [parts, tall, tall, zero], [VMEM] * 2, [left_ops, right_ops]
    )

    outer, inner = [psi[:: nloc - 1]], [psi[1 : nloc - 1]]
    for step in range(n - 1):
        inner.append(lax.ppermute(inner[-1] + zero[0, 0] if step == 1 else inner[-1], "op", route))
        outer.append(lax.ppermute(outer[-1] + zero[0, 0] if step == 1 else outer[-1], "op", route))

    above = shifted(jnp.concatenate([b[1:] for b in outer]), ("sec", "sub"), 1)
    below = shifted(jnp.concatenate([b[:1] for b in outer]), ("sec", "sub"), -1)

    def split_parts(sectors):
        return jax.ShapeDtypeStruct((sectors, 3 * width, width), BF16)

    def whole(sectors):
        return [pltpu.VMEM((sectors, width, width), F32)]

    parts_outer = call(functools.partial(assemble, n), "assemble", 4 * kops * one, split_parts(2), [VMEM] * n, outer, whole(2))
    def products(sectors):
        return [jax.ShapeDtypeStruct((sectors, kops * rows, width), BF16)] * 2

    chunk = jax.ShapeDtypeStruct((2, rows, width), F32)
    chunk_inner = jax.ShapeDtypeStruct((nloc - 2, rows, width), F32)
    parts_inner, *own = call(
        functools.partial(own_sectors, n), "own", 4 * kops * one, [split_parts(nloc - 2), *products(nloc)],
        [SMEM] + [VMEM] * (n + 2), [allowed, parts_outer, *inner, left_parts], whole(nloc - 2),
    )
    result_inner = call(
        functools.partial(first_inner, nloc), "first_inner", nloc * kops * one // n, chunk_inner,
        [SMEM] + [VMEM] * 4, [shifts, *own, right_hi, right_lo],
    )
    parts_outside, *ends = call(
        functools.partial(outside_sectors, n, nloc), "outside", 2 * kops * one, [split_parts(2), *products(2)],
        [SMEM] + [VMEM] * 3, [allowed, above, below, left_parts], whole(2),
    )
    result_outer = call(
        functools.partial(first_outer, nloc), "first_outer", nloc * kops * one // n, chunk,
        [SMEM] + [VMEM] * 6, [shifts, *own, *ends, right_hi, right_lo],
    )

    def mine(step):
        return call(
            functools.partial(later_chunk, n, nloc, step), "chunk", 4 * nloc * kops * one // n, [chunk, chunk_inner],
            [SMEM] * 2 + [VMEM] * 6,
            [shifts, allowed, parts_outer, parts_inner, parts_outside, left_parts, right_hi, right_lo],
            [pltpu.VMEM((nloc + 2, kops * rows, width), BF16)] * 2,
        )

    for step in range(1, n):
        next_outer, next_inner = mine(step)
        result_inner = lax.ppermute(result_inner, "op", route) + next_inner
        result_outer = lax.ppermute(result_outer, "op", route) + next_outer
    return jnp.concatenate([result_outer[:1], result_inner, result_outer[1:]])


def solution(mesh):
    return jax.shard_map(
        shards,
        mesh=mesh,
        in_specs=(
            P(("parts", "sec", "sub"), "op", None),
            P("op", None, None),
            P("op", None, None),
            P("op"),
            P("op", None),
        ),
        out_specs=P(("parts", "sec", "sub"), "op", None),
        check_vma=False,
    )
```

```python
import functools

import jax
import jax.numpy as jnp
from jax import lax
from jax.experimental import pallas as pl
from jax.experimental.pallas import tpu as pltpu
from jax.sharding import PartitionSpec as P

F32, BF16 = jnp.float32, jnp.bfloat16
SMEM = pl.BlockSpec(memory_space=pltpu.SMEM)
VMEM = pl.BlockSpec(memory_space=pltpu.VMEM)


def shifted(block, axis, distance):
    devices = range(lax.axis_size(axis))
    route = [(i - distance, i) for i in devices if i - distance in devices]
    return lax.ppermute(block, axis, route)


def ring_route(n):
    order = [0] + [i for i in range(n) if i % 2] + [i for i in reversed(range(1, n)) if i % 2 == 0]
    return [(order[i], order[(i + 1) % n]) for i in range(n)]


def ring_place(n, steps_back):
    me = lax.axis_index("op")
    place = jnp.where(me == 0, 0, jnp.where(lax.rem(me, 2) == 1, (me + 1) // 2, n - me // 2))
    at = lax.rem(place - steps_back + 2 * n, n)
    return jnp.where(at == 0, 0, jnp.where(at <= n // 2, 2 * at - 1, 2 * (n - at)))


def split(x):
    hi = x.astype(BF16)
    return hi, (x - hi.astype(F32)).astype(BF16)


def dot3(a, b):
    one = functools.partial(jnp.dot, preferred_element_type=F32)
    return one(a[0], b[0]) + (one(a[0], b[1]) + one(a[1], b[0]))


def prepare(left_ref, right_ref, left_parts, right_hi, right_lo, zero):
    n, kops, rows, _ = left_parts.shape
    width = left_ref.shape[1]
    zero[...] = jnp.zeros_like(zero)
    for k in range(kops):
        hi, lo = split(left_ref[k])
        parts = jnp.concatenate([hi, hi, lo], axis=1)
        for c in range(n):
            left_parts[c, k] = parts[c * rows : (c + 1) * rows]
        right_hi[k * width : (k + 1) * width, :], right_lo[k * width : (k + 1) * width, :] = split(right_ref[k].T)


def stacked(block):
    hi, lo = split(block)
    return jnp.concatenate([hi, lo, hi], axis=0)


def place_rows(n, target, blocks, way=1):
    for j, block in enumerate(blocks):
        rows = block.shape[-2]
        target[..., pl.ds(pl.multiple_of(ring_place(n, way * j) * rows, rows), rows), :] = block


def assemble(n, way, *refs):
    parts, psi = refs[n:]
    place_rows(n, psi, [ref[...] for ref in refs[:n]], way)
    for i in range(parts.shape[0]):
        parts[i] = stacked(psi[i])


def first_product(left, parts, allowed_ref, source, high, low):
    kops, sectors = allowed_ref.shape
    block = jnp.dot(left, parts, preferred_element_type=F32)
    rows = block.shape[0] // kops
    source = jnp.clip(source, 0, sectors - 1)
    for k in range(kops):
        at = slice(k * rows, (k + 1) * rows)
        high[at], low[at] = split(block[at] * allowed_ref[k, source].astype(F32))


def chunk_left(n, step, left_parts):
    return left_parts[ring_place(n, step + 1)].reshape(-1, left_parts.shape[-1])


def own_sectors(n, allowed_ref, outer, *refs):
    left_parts, inner, high, low, psi = refs[n:]
    assemble(n, -1, *refs[:n], inner, psi)
    left = chunk_left(n, 0, left_parts)
    nloc = high.shape[0]
    first = lax.axis_index(("sec", "sub")) * nloc
    sources = [outer.at[0], *[inner.at[i] for i in range(nloc - 2)], outer.at[1]]
    for i, ref in enumerate(sources):
        first_product(left, ref[...], allowed_ref, first + i, high.at[i], low.at[i])


def outside_sectors(n, nloc, allowed_ref, above, below, left_parts, outside, high, low, psi):
    place_rows(n, psi.at[0], [above[j] for j in range(n)])
    place_rows(n, psi.at[1], [below[j] for j in range(n)])
    left = chunk_left(n, 0, left_parts)
    first = lax.axis_index(("sec", "sub")) * nloc
    for i in range(2):
        outside[i] = stacked(psi[i])
        first_product(left, outside[i], allowed_ref, first - 1 + i * (nloc + 1), high.at[i], low.at[i])


def second_product(targets, shifts_ref, high, low, right_hi, right_lo, out):
    kops = shifts_ref.shape[0]
    _, rows, width = out.shape

    def left(parts):
        columns = []
        for k in range(kops):
            shift, at = shifts_ref[k], slice(k * rows, (k + 1) * rows)
            blocks = []
            for t in targets:
                below, same, above = [parts[t + d][at] for d in range(3)]
                blocks.append(jnp.where(shift == 0, same, jnp.where(shift == 1, below, above)))
            columns.append(jnp.concatenate(blocks))
        return jnp.concatenate(columns, axis=1)

    out[...] = dot3((left(high), left(low)), (right_hi[...], right_lo[...])).reshape(len(targets), rows, width)


def first_inner(nloc, shifts_ref, high, low, right_hi, right_lo, out):
    own = [[None, *[ref.at[i] for i in range(nloc)], None] for ref in (high, low)]
    second_product(range(1, nloc - 1), shifts_ref, *own, right_hi, right_lo, out)


def first_outer(nloc, shifts_ref, high, low, end_high, end_low, right_hi, right_lo, out):
    pairs = ((high, end_high), (low, end_low))
    held = [[ends.at[0], *[ref.at[i] for i in range(nloc)], ends.at[1]] for ref, ends in pairs]
    second_product((0, nloc - 1), shifts_ref, *held, right_hi, right_lo, out)


def later_chunk(n, nloc, step, shifts_ref, allowed_ref, outer, inner, outside, left_parts, right_hi, right_lo, outer_out, inner_out, high, low):
    left = chunk_left(n, step, left_parts)
    first = lax.axis_index(("sec", "sub")) * nloc
    sources = [outside.at[0], outer.at[0], *[inner.at[i] for i in range(nloc - 2)], outer.at[1], outside.at[1]]
    for i, ref in enumerate(sources):
        first_product(left, ref[...], allowed_ref, first - 1 + i, high.at[i], low.at[i])
    held = [[ref.at[i] for i in range(nloc + 2)] for ref in (high, low)]
    second_product(range(1, nloc - 1), shifts_ref, *held, right_hi, right_lo, inner_out)
    second_product((0, nloc - 1), shifts_ref, *held, right_hi, right_lo, outer_out)


def call(body, name, flops, out_shape, in_specs, operands, scratch=()):
    return pl.pallas_call(
        body,
        name=name,
        out_shape=out_shape,
        in_specs=in_specs,
        out_specs=jax.tree.map(lambda _: VMEM, out_shape),
        scratch_shapes=list(scratch),
        compiler_params=pltpu.CompilerParams(vmem_limit_bytes=24 * 2**20),
        cost_estimate=pl.CostEstimate(flops=flops, bytes_accessed=2**20, transcendentals=0),
    )(*operands)


def shards(psi, left_ops, right_ops, shifts, allowed):
    nloc, rows, width = psi.shape
    kops = left_ops.shape[0]
    n = lax.axis_size("op")
    route = ring_route(n)
    back = [(target, source) for source, target in route]
    one = 6 * width**3

    tall = jax.ShapeDtypeStruct((kops * width, width), BF16)
    parts = jax.ShapeDtypeStruct((n, kops, rows, 3 * width), BF16)
    zero = jax.ShapeDtypeStruct((1, 128), F32)
    left_parts, right_hi, right_lo, zero = call(
        prepare, "prepare", 4 * kops * one, [parts, tall, tall, zero], [VMEM] * 2, [left_ops, right_ops]
    )

    outer, inner = [psi[:: nloc - 1]], [psi[1 : nloc - 1]]
    for step in range(n - 1):
        inner.append(lax.ppermute(inner[-1] + zero[0, 0] if step == 1 else inner[-1], "op", back))
        outer.append(lax.ppermute(outer[-1] + zero[0, 0] if step == 1 else outer[-1], "op", route))

    above = shifted(jnp.concatenate([b[1:] for b in outer]), ("sec", "sub"), 1)
    below = shifted(jnp.concatenate([b[:1] for b in outer]), ("sec", "sub"), -1)

    def split_parts(sectors):
        return jax.ShapeDtypeStruct((sectors, 3 * width, width), BF16)

    def whole(sectors):
        return [pltpu.VMEM((sectors, width, width), F32)]

    parts_outer = call(functools.partial(assemble, n, 1), "assemble", 4 * kops * one, split_parts(2), [VMEM] * n, outer, whole(2))
    def products(sectors):
        return [jax.ShapeDtypeStruct((sectors, kops * rows, width), BF16)] * 2

    chunk = jax.ShapeDtypeStruct((2, rows, width), F32)
    chunk_inner = jax.ShapeDtypeStruct((nloc - 2, rows, width), F32)
    parts_inner, *own = call(
        functools.partial(own_sectors, n), "own", 4 * kops * one, [split_parts(nloc - 2), *products(nloc)],
        [SMEM] + [VMEM] * (n + 2), [allowed, parts_outer, *inner, left_parts], whole(nloc - 2),
    )
    result_inner = call(
        functools.partial(first_inner, nloc), "first_inner", nloc * kops * one // n, chunk_inner,
        [SMEM] + [VMEM] * 4, [shifts, *own, right_hi, right_lo],
    )
    parts_outside, *ends = call(
        functools.partial(outside_sectors, n, nloc), "outside", 2 * kops * one, [split_parts(2), *products(2)],
        [SMEM] + [VMEM] * 3, [allowed, above, below, left_parts], whole(2),
    )
    result_outer = call(
        functools.partial(first_outer, nloc), "first_outer", nloc * kops * one // n, chunk,
        [SMEM] + [VMEM] * 6, [shifts, *own, *ends, right_hi, right_lo],
    )

    def mine(step):
        return call(
            functools.partial(later_chunk, n, nloc, step), "chunk", 4 * nloc * kops * one // n, [chunk, chunk_inner],
            [SMEM] * 2 + [VMEM] * 6,
            [shifts, allowed, parts_outer, parts_inner, parts_outside, left_parts, right_hi, right_lo],
            [pltpu.VMEM((nloc + 2, kops * rows, width), BF16)] * 2,
        )

    for step in range(1, n):
        next_outer, next_inner = mine(step)
        result_inner = lax.ppermute(result_inner, "op", route) + next_inner
        result_outer = lax.ppermute(result_outer, "op", route) + next_outer
    return jnp.concatenate([result_outer[:1], result_inner, result_outer[1:]])


def solution(mesh):
    return jax.shard_map(
        shards,
        mesh=mesh,
        in_specs=(
            P(("parts", "sec", "sub"), "op", None),
            P("op", None, None),
            P("op", None, None),
            P("op"),
            P("op", None),
        ),
        out_specs=P(("parts", "sec", "sub"), "op", None),
        check_vma=False,
    )
```

```python
import functools

import jax
import jax.numpy as jnp
from jax import lax
from jax.experimental import pallas as pl
from jax.experimental.pallas import tpu as pltpu
from jax.sharding import PartitionSpec as P

F32, BF16 = jnp.float32, jnp.bfloat16
SMEM = pl.BlockSpec(memory_space=pltpu.SMEM)
VMEM = pl.BlockSpec(memory_space=pltpu.VMEM)


def shifted(block, axis, distance):
    devices = range(lax.axis_size(axis))
    route = [(i - distance, i) for i in devices if i - distance in devices]
    return lax.ppermute(block, axis, route)


def ring_route(n):
    order = [0] + [i for i in range(n) if i % 2] + [i for i in reversed(range(1, n)) if i % 2 == 0]
    return [(order[i], order[(i + 1) % n]) for i in range(n)]


def ring_place(n, steps_back):
    me = lax.axis_index("op")
    place = jnp.where(me == 0, 0, jnp.where(lax.rem(me, 2) == 1, (me + 1) // 2, n - me // 2))
    at = lax.rem(place - steps_back + 2 * n, n)
    return jnp.where(at == 0, 0, jnp.where(at <= n // 2, 2 * at - 1, 2 * (n - at)))


def split(x):
    hi = x.astype(BF16)
    return hi, (x - hi.astype(F32)).astype(BF16)


def dot3(a, b):
    one = functools.partial(jnp.dot, preferred_element_type=F32)
    return one(a[0], b[0]) + (one(a[0], b[1]) + one(a[1], b[0]))


def prepare(left_ref, right_ref, left_parts, right_hi, right_lo, zero):
    n, kops, rows, _ = left_parts.shape
    width = left_ref.shape[1]
    zero[...] = jnp.zeros_like(zero)
    for k in range(kops):
        hi, lo = split(left_ref[k])
        parts = jnp.concatenate([hi, hi, lo], axis=1)
        for c in range(n):
            left_parts[c, k] = parts[c * rows : (c + 1) * rows]
        right_hi[k * width : (k + 1) * width, :], right_lo[k * width : (k + 1) * width, :] = split(right_ref[k].T)


def stacked(block):
    hi, lo = split(block)
    return jnp.concatenate([hi, lo, hi], axis=0)


def place_rows(n, target, blocks):
    for j, block in enumerate(blocks):
        rows = block.shape[-2]
        target[..., pl.ds(pl.multiple_of(ring_place(n, j) * rows, rows), rows), :] = block


def assemble(n, *refs):
    parts, psi = refs[n:]
    place_rows(n, psi, [ref[...] for ref in refs[:n]])
    for i in range(parts.shape[0]):
        parts[i] = stacked(psi[i])


def first_product(left, parts, allowed_ref, source, high, low):
    kops, sectors = allowed_ref.shape
    block = jnp.dot(left, parts, preferred_element_type=F32)
    rows = block.shape[0] // kops
    source = jnp.clip(source, 0, sectors - 1)
    for k in range(kops):
        at = slice(k * rows, (k + 1) * rows)
        high[at], low[at] = split(block[at] * allowed_ref[k, source].astype(F32))


def chunk_left(n, step, left_parts):
    return left_parts[ring_place(n, step + 1)].reshape(-1, left_parts.shape[-1])


def own_sectors(n, allowed_ref, outer, *refs):
    left_parts, inner, high, low, psi = refs[n:]
    assemble(n, *refs[:n], inner, psi)
    left = chunk_left(n, 0, left_parts)
    nloc = high.shape[0]
    first = lax.axis_index(("sec", "sub")) * nloc
    sources = [outer.at[0], *[inner.at[i] for i in range(nloc - 2)], outer.at[1]]
    for i, ref in enumerate(sources):
        first_product(left, ref[...], allowed_ref, first + i, high.at[i], low.at[i])


def outside_sectors(n, nloc, allowed_ref, above, below, left_parts, outside, high, low, psi):
    place_rows(n, psi.at[0], [above[j] for j in range(n)])
    place_rows(n, psi.at[1], [below[j] for j in range(n)])
    left = chunk_left(n, 0, left_parts)
    first = lax.axis_index(("sec", "sub")) * nloc
    for i in range(2):
        outside[i] = stacked(psi[i])
        first_product(left, outside[i], allowed_ref, first - 1 + i * (nloc + 1), high.at[i], low.at[i])


def second_product(targets, shifts_ref, high, low, right_hi, right_lo, out):
    kops = shifts_ref.shape[0]
    _, rows, width = out.shape

    def left(parts):
        columns = []
        for k in range(kops):
            shift, at = shifts_ref[k], slice(k * rows, (k + 1) * rows)
            blocks = []
            for t in targets:
                below, same, above = [parts[t + d][at] for d in range(3)]
                blocks.append(jnp.where(shift == 0, same, jnp.where(shift == 1, below, above)))
            columns.append(jnp.concatenate(blocks))
        return jnp.concatenate(columns, axis=1)

    out[...] = dot3((left(high), left(low)), (right_hi[...], right_lo[...])).reshape(len(targets), rows, width)


def first_inner(nloc, shifts_ref, high, low, right_hi, right_lo, out):
    own = [[None, *[ref.at[i] for i in range(nloc)], None] for ref in (high, low)]
    second_product(range(1, nloc - 1), shifts_ref, *own, right_hi, right_lo, out)


def first_outer(nloc, shifts_ref, high, low, end_high, end_low, right_hi, right_lo, out):
    pairs = ((high, end_high), (low, end_low))
    held = [[ends.at[0], *[ref.at[i] for i in range(nloc)], ends.at[1]] for ref, ends in pairs]
    second_product((0, nloc - 1), shifts_ref, *held, right_hi, right_lo, out)


def later_chunk(n, nloc, step, shifts_ref, allowed_ref, outer, inner, outside, left_parts, right_hi, right_lo, outer_out, inner_out, high, low):
    left = chunk_left(n, step, left_parts)
    first = lax.axis_index(("sec", "sub")) * nloc
    sources = [outside.at[0], outer.at[0], *[inner.at[i] for i in range(nloc - 2)], outer.at[1], outside.at[1]]
    for i, ref in enumerate(sources):
        first_product(left, ref[...], allowed_ref, first - 1 + i, high.at[i], low.at[i])
    held = [[ref.at[i] for i in range(nloc + 2)] for ref in (high, low)]
    second_product(range(1, nloc - 1), shifts_ref, *held, right_hi, right_lo, inner_out)
    second_product((0, nloc - 1), shifts_ref, *held, right_hi, right_lo, outer_out)


def call(body, name, flops, out_shape, in_specs, operands, scratch=()):
    return pl.pallas_call(
        body,
        name=name,
        out_shape=out_shape,
        in_specs=in_specs,
        out_specs=jax.tree.map(lambda _: VMEM, out_shape),
        scratch_shapes=list(scratch),
        compiler_params=pltpu.CompilerParams(vmem_limit_bytes=24 * 2**20),
        cost_estimate=pl.CostEstimate(flops=flops, bytes_accessed=2**20, transcendentals=0),
    )(*operands)


def shards(psi, left_ops, right_ops, shifts, allowed):
    nloc, rows, width = psi.shape
    kops = left_ops.shape[0]
    n = lax.axis_size("op")
    route = ring_route(n)
    one = 6 * width**3

    tall = jax.ShapeDtypeStruct((kops * width, width), BF16)
    parts = jax.ShapeDtypeStruct((n, kops, rows, 3 * width), BF16)
    zero = jax.ShapeDtypeStruct((1, 128), F32)
    left_parts, right_hi, right_lo, zero = call(
        prepare, "prepare", 4 * kops * one, [parts, tall, tall, zero], [VMEM] * 2, [left_ops, right_ops]
    )

    outer, inner = [psi[:: nloc - 1]], [psi[1 : nloc - 1]]
    for step in range(n - 1):
        inner.append(lax.ppermute(inner[-1] + zero[0, 0] if step == 1 else inner[-1], "op", route))
        outer.append(lax.ppermute(outer[-1] + zero[0, 0] if step == 1 else outer[-1], "op", route))

    above = shifted(jnp.concatenate([b[1:] for b in outer]), ("sec", "sub"), 1)
    below = shifted(jnp.concatenate([b[:1] for b in outer]), ("sec", "sub"), -1)

    def split_parts(sectors):
        return jax.ShapeDtypeStruct((sectors, 3 * width, width), BF16)

    def whole(sectors):
        return [pltpu.VMEM((sectors, width, width), F32)]

    parts_outer = call(functools.partial(assemble, n), "assemble", 4 * kops * one, split_parts(2), [VMEM] * n, outer, whole(2))
    def products(sectors):
        return [jax.ShapeDtypeStruct((sectors, kops * rows, width), BF16)] * 2

    chunk = jax.ShapeDtypeStruct((2, rows, width), F32)
    chunk_inner = jax.ShapeDtypeStruct((nloc - 2, rows, width), F32)
    parts_inner, *own = call(
        functools.partial(own_sectors, n), "own", 4 * kops * one, [split_parts(nloc - 2), *products(nloc)],
        [SMEM] + [VMEM] * (n + 2), [allowed, parts_outer, *inner, left_parts], whole(nloc - 2),
    )
    result_inner = call(
        functools.partial(first_inner, nloc), "first_inner", nloc * kops * one // n, chunk_inner,
        [SMEM] + [VMEM] * 4, [shifts, *own, right_hi, right_lo],
    )
    parts_outside, *ends = call(
        functools.partial(outside_sectors, n, nloc), "outside", 2 * kops * one, [split_parts(2), *products(2)],
        [SMEM] + [VMEM] * 3, [allowed, above, below, left_parts], whole(2),
    )
    result_outer = call(
        functools.partial(first_outer, nloc), "first_outer", nloc * kops * one // n, chunk,
        [SMEM] + [VMEM] * 6, [shifts, *own, *ends, right_hi, right_lo],
    )

    def mine(step):
        return call(
            functools.partial(later_chunk, n, nloc, step), "chunk", 4 * nloc * kops * one // n, [chunk, chunk_inner],
            [SMEM] * 2 + [VMEM] * 6,
            [shifts, allowed, parts_outer, parts_inner, parts_outside, left_parts, right_hi, right_lo],
            [pltpu.VMEM((nloc + 2, kops * rows, width), BF16)] * 2,
        )

    for step in range(1, n):
        next_outer, next_inner = mine(step)
        result_inner = lax.ppermute(result_inner, "op", route) + next_inner
        result_outer = lax.ppermute(result_outer, "op", route) + next_outer
    return jnp.concatenate([result_outer[:1], result_inner, result_outer[1:]])


def solution(mesh):
    return jax.shard_map(
        shards,
        mesh=mesh,
        in_specs=(
            P(("parts", "sec", "sub"), "op", None),
            P("op", None, None),
            P("op", None, None),
            P("op"),
            P("op", None),
        ),
        out_specs=P(("parts", "sec", "sub"), "op", None),
        check_vma=False,
    )
```

```python
import functools

import jax
import jax.numpy as jnp
from jax import lax
from jax.experimental import pallas as pl
from jax.experimental.pallas import tpu as pltpu
from jax.sharding import PartitionSpec as P

F32, BF16 = jnp.float32, jnp.bfloat16
SMEM = pl.BlockSpec(memory_space=pltpu.SMEM)
VMEM = pl.BlockSpec(memory_space=pltpu.VMEM)


def shifted(block, axis, distance):
    devices = range(lax.axis_size(axis))
    route = [(i - distance, i) for i in devices if i - distance in devices]
    return lax.ppermute(block, axis, route)


def ring_route(n):
    order = [0] + [i for i in range(n) if i % 2] + [i for i in reversed(range(1, n)) if i % 2 == 0]
    return [(order[i], order[(i + 1) % n]) for i in range(n)]


def ring_place(n, steps_back):
    me = lax.axis_index("op")
    place = jnp.where(me == 0, 0, jnp.where(lax.rem(me, 2) == 1, (me + 1) // 2, n - me // 2))
    at = lax.rem(place - steps_back + 2 * n, n)
    return jnp.where(at == 0, 0, jnp.where(at <= n // 2, 2 * at - 1, 2 * (n - at)))


def split(x):
    hi = x.astype(BF16)
    return hi, (x - hi.astype(F32)).astype(BF16)


def prepare(left_ref, right_ref, left_parts, right_parts, zero):
    n, kops, rows, _ = left_parts.shape
    width = left_ref.shape[1]
    zero[...] = jnp.zeros_like(zero)
    for k in range(kops):
        hi, lo = split(left_ref[k])
        parts = jnp.concatenate([hi, hi, lo], axis=1)
        for c in range(n):
            left_parts[c, k] = parts[c * rows : (c + 1) * rows]
        hi, lo = split(right_ref[k].T)
        right_parts[k] = jnp.concatenate([hi, hi, lo], axis=0)


def stacked(block):
    hi, lo = split(block)
    return jnp.concatenate([hi, lo, hi], axis=0)


def place_rows(n, target, blocks):
    for j, block in enumerate(blocks):
        rows = block.shape[-2]
        target[..., pl.ds(pl.multiple_of(ring_place(n, j) * rows, rows), rows), :] = block


def assemble(n, *refs):
    parts, psi = refs[n:]
    place_rows(n, psi, [ref[...] for ref in refs[:n]])
    for i in range(parts.shape[0]):
        parts[i] = stacked(psi[i])


def first_product(left, parts, allowed_ref, source, high, low):
    kops, sectors = allowed_ref.shape
    block = jnp.dot(left, parts, preferred_element_type=F32)
    rows = block.shape[0] // kops
    source = jnp.clip(source, 0, sectors - 1)
    for k in range(kops):
        at = slice(k * rows, (k + 1) * rows)
        high[at], low[at] = split(block[at] * allowed_ref[k, source].astype(F32))


def chunk_left(n, step, left_parts):
    return left_parts[ring_place(n, step + 1)].reshape(-1, left_parts.shape[-1])


def own_sectors(n, allowed_ref, outer, *refs):
    left_parts, inner, high, low, psi = refs[n:]
    assemble(n, *refs[:n], inner, psi)
    left = chunk_left(n, 0, left_parts)
    nloc = high.shape[0]
    first = lax.axis_index(("sec", "sub")) * nloc
    sources = [outer.at[0], *[inner.at[i] for i in range(nloc - 2)], outer.at[1]]
    for i, ref in enumerate(sources):
        first_product(left, ref[...], allowed_ref, first + i, high.at[i], low.at[i])


def outside_sectors(n, nloc, allowed_ref, above, below, left_parts, outside, high, low, psi):
    place_rows(n, psi.at[0], [above[j] for j in range(n)])
    place_rows(n, psi.at[1], [below[j] for j in range(n)])
    left = chunk_left(n, 0, left_parts)
    first = lax.axis_index(("sec", "sub")) * nloc
    for i in range(2):
        outside[i] = stacked(psi[i])
        first_product(left, outside[i], allowed_ref, first - 1 + i * (nloc + 1), high.at[i], low.at[i])


def second_product(targets, shifts_ref, high, low, right_parts, rows):
    total = None
    for k in range(shifts_ref.shape[0]):
        shift, at = shifts_ref[k], slice(k * rows, (k + 1) * rows)

        def left(parts):
            blocks = []
            for t in targets:
                below, same, above = [parts[t + d][at] for d in range(3)]
                blocks.append(jnp.where(shift == 0, same, jnp.where(shift == 1, below, above)))
            return jnp.concatenate(blocks)

        hi, lo = left(high), left(low)
        part = jnp.dot(jnp.concatenate([hi, lo, hi], axis=1), right_parts[k], preferred_element_type=F32)
        total = part if total is None else total + part
    return total.reshape(len(targets), rows, -1)


def first_inner(nloc, shifts_ref, high, low, right_parts, out):
    own = [[None, *[ref.at[i] for i in range(nloc)], None] for ref in (high, low)]
    out[...] = second_product(range(1, nloc - 1), shifts_ref, *own, right_parts, out.shape[1])


def first_outer(nloc, shifts_ref, high, low, end_high, end_low, right_parts, out):
    pairs = ((high, end_high), (low, end_low))
    held = [[ends.at[0], *[ref.at[i] for i in range(nloc)], ends.at[1]] for ref, ends in pairs]
    out[...] = second_product((0, nloc - 1), shifts_ref, *held, right_parts, out.shape[1])


def later_chunk(n, nloc, step, shifts_ref, allowed_ref, outer, inner, outside, left_parts, right_parts, outer_out, inner_out, high, low):
    left = chunk_left(n, step, left_parts)
    first = lax.axis_index(("sec", "sub")) * nloc
    sources = [outside.at[0], outer.at[0], *[inner.at[i] for i in range(nloc - 2)], outer.at[1], outside.at[1]]
    for i, ref in enumerate(sources):
        first_product(left, ref[...], allowed_ref, first - 1 + i, high.at[i], low.at[i])
    held = [[ref.at[i] for i in range(nloc + 2)] for ref in (high, low)]
    total = second_product((0, nloc - 1, *range(1, nloc - 1)), shifts_ref, *held, right_parts, outer_out.shape[1])
    outer_out[...] = total[:2]
    inner_out[...] = total[2:]


def call(body, name, flops, out_shape, in_specs, operands, scratch=()):
    return pl.pallas_call(
        body,
        name=name,
        out_shape=out_shape,
        in_specs=in_specs,
        out_specs=jax.tree.map(lambda _: VMEM, out_shape),
        scratch_shapes=list(scratch),
        compiler_params=pltpu.CompilerParams(vmem_limit_bytes=24 * 2**20),
        cost_estimate=pl.CostEstimate(flops=flops, bytes_accessed=2**20, transcendentals=0),
    )(*operands)


def shards(psi, left_ops, right_ops, shifts, allowed):
    nloc, rows, width = psi.shape
    kops = left_ops.shape[0]
    n = lax.axis_size("op")
    route = ring_route(n)
    one = 6 * width**3

    tall = jax.ShapeDtypeStruct((kops, 3 * width, width), BF16)
    parts = jax.ShapeDtypeStruct((n, kops, rows, 3 * width), BF16)
    zero = jax.ShapeDtypeStruct((1, 128), F32)
    left_parts, right_parts, zero = call(
        prepare, "prepare", 4 * kops * one, [parts, tall, zero], [VMEM] * 2, [left_ops, right_ops]
    )

    outer, inner = [psi[:: nloc - 1]], [psi[1 : nloc - 1]]
    for step in range(n - 1):
        inner.append(lax.ppermute(inner[-1] + zero[0, 0] if step == 1 else inner[-1], "op", route))
        outer.append(lax.ppermute(outer[-1] + zero[0, 0] if step == 1 else outer[-1], "op", route))

    above = shifted(jnp.concatenate([b[1:] for b in outer]), ("sec", "sub"), 1)
    below = shifted(jnp.concatenate([b[:1] for b in outer]), ("sec", "sub"), -1)

    def split_parts(sectors):
        return jax.ShapeDtypeStruct((sectors, 3 * width, width), BF16)

    def whole(sectors):
        return [pltpu.VMEM((sectors, width, width), F32)]

    parts_outer = call(functools.partial(assemble, n), "assemble", 4 * kops * one, split_parts(2), [VMEM] * n, outer, whole(2))
    def products(sectors):
        return [jax.ShapeDtypeStruct((sectors, kops * rows, width), BF16)] * 2

    chunk = jax.ShapeDtypeStruct((2, rows, width), F32)
    chunk_inner = jax.ShapeDtypeStruct((nloc - 2, rows, width), F32)
    parts_inner, *own = call(
        functools.partial(own_sectors, n), "own", 4 * kops * one, [split_parts(nloc - 2), *products(nloc)],
        [SMEM] + [VMEM] * (n + 2), [allowed, parts_outer, *inner, left_parts], whole(nloc - 2),
    )
    result_inner = call(
        functools.partial(first_inner, nloc), "first_inner", nloc * kops * one // n, chunk_inner,
        [SMEM] + [VMEM] * 3, [shifts, *own, right_parts],
    )
    parts_outside, *ends = call(
        functools.partial(outside_sectors, n, nloc), "outside", 2 * kops * one, [split_parts(2), *products(2)],
        [SMEM] + [VMEM] * 3, [allowed, above, below, left_parts], whole(2),
    )
    result_outer = call(
        functools.partial(first_outer, nloc), "first_outer", nloc * kops * one // n, chunk,
        [SMEM] + [VMEM] * 5, [shifts, *own, *ends, right_parts],
    )

    def mine(step):
        return call(
            functools.partial(later_chunk, n, nloc, step), "chunk", 4 * nloc * kops * one // n, [chunk, chunk_inner],
            [SMEM] * 2 + [VMEM] * 5,
            [shifts, allowed, parts_outer, parts_inner, parts_outside, left_parts, right_parts],
            [pltpu.VMEM((nloc + 2, kops * rows, width), BF16)] * 2,
        )

    for step in range(1, n):
        next_outer, next_inner = mine(step)
        result_inner = lax.ppermute(result_inner, "op", route) + next_inner
        result_outer = lax.ppermute(result_outer, "op", route) + next_outer
    return jnp.concatenate([result_outer[:1], result_inner, result_outer[1:]])


def solution(mesh):
    return jax.shard_map(
        shards,
        mesh=mesh,
        in_specs=(
            P(("parts", "sec", "sub"), "op", None),
            P("op", None, None),
            P("op", None, None),
            P("op"),
            P("op", None),
        ),
        out_specs=P(("parts", "sec", "sub"), "op", None),
        check_vma=False,
    )
```

```python
import functools

import jax
import jax.numpy as jnp
from jax import lax
from jax.experimental import pallas as pl
from jax.experimental.pallas import tpu as pltpu
from jax.sharding import PartitionSpec as P

F32, BF16 = jnp.float32, jnp.bfloat16
SMEM = pl.BlockSpec(memory_space=pltpu.SMEM)
VMEM = pl.BlockSpec(memory_space=pltpu.VMEM)


def shifted(block, axis, distance):
    devices = range(lax.axis_size(axis))
    route = [(i - distance, i) for i in devices if i - distance in devices]
    return lax.ppermute(block, axis, route)


def ring_route(n):
    order = [0] + [i for i in range(n) if i % 2] + [i for i in reversed(range(1, n)) if i % 2 == 0]
    return [(order[i], order[(i + 1) % n]) for i in range(n)]


def ring_place(n, steps_back):
    me = lax.axis_index("op")
    place = jnp.where(me == 0, 0, jnp.where(lax.rem(me, 2) == 1, (me + 1) // 2, n - me // 2))
    at = lax.rem(place - steps_back + 2 * n, n)
    return jnp.where(at == 0, 0, jnp.where(at <= n // 2, 2 * at - 1, 2 * (n - at)))


def split(x):
    hi = x.astype(BF16)
    return hi, (x - hi.astype(F32)).astype(BF16)


def dot3(a, b):
    one = functools.partial(jnp.dot, preferred_element_type=F32)
    return one(a[0], b[0]) + (one(a[0], b[1]) + one(a[1], b[0]))


def prepare(left_ref, right_ref, left_parts, right_hi, right_lo, zero):
    n, kops, rows, _ = left_parts.shape
    width = left_ref.shape[1]
    zero[...] = jnp.zeros_like(zero)
    for k in range(kops):
        hi, lo = split(left_ref[k])
        parts = jnp.concatenate([hi, hi, lo], axis=1)
        for c in range(n):
            left_parts[c, k] = parts[c * rows : (c + 1) * rows]
        right_hi[k * width : (k + 1) * width, :], right_lo[k * width : (k + 1) * width, :] = split(right_ref[k].T)


def stacked(block):
    hi, lo = split(block)
    return jnp.concatenate([hi, lo, hi], axis=0)


def place_rows(n, target, blocks):
    for j, block in enumerate(blocks):
        rows = block.shape[-2]
        target[..., pl.ds(pl.multiple_of(ring_place(n, j) * rows, rows), rows), :] = block


def assemble(n, *refs):
    parts, psi = refs[n:]
    place_rows(n, psi, [ref[...] for ref in refs[:n]])
    for i in range(parts.shape[0]):
        parts[i] = stacked(psi[i])


def first_product(left, parts, allowed_ref, source, high, low):
    kops, sectors = allowed_ref.shape
    block = jnp.dot(left, parts, preferred_element_type=F32)
    rows = block.shape[0] // kops
    source = jnp.clip(source, 0, sectors - 1)
    for k in range(kops):
        at = slice(k * rows, (k + 1) * rows)
        high[at], low[at] = split(block[at] * allowed_ref[k, source].astype(F32))


def chunk_left(n, step, left_parts):
    return left_parts[ring_place(n, step + 1)].reshape(-1, left_parts.shape[-1])


def own_sectors(n, allowed_ref, *refs):
    (outer, left_parts), (inner, high, low, psi) = refs[n : n + 2], refs[n + 2 :]
    assemble(n, *refs[:n], inner, psi)
    left = chunk_left(n, 0, left_parts)
    nloc = high.shape[0]
    first = lax.axis_index(("sec", "sub")) * nloc
    sources = [outer.at[0], *[inner.at[i] for i in range(nloc - 2)], outer.at[1]]
    for i, ref in enumerate(sources):
        first_product(left, ref[...], allowed_ref, first + i, high.at[i], low.at[i])


def outside_sectors(n, nloc, allowed_ref, above, below, left_parts, outside, high, low, psi):
    place_rows(n, psi.at[0], [above[j] for j in range(n)])
    place_rows(n, psi.at[1], [below[j] for j in range(n)])
    left = chunk_left(n, 0, left_parts)
    first = lax.axis_index(("sec", "sub")) * nloc
    for i in range(2):
        outside[i] = stacked(psi[i])
        first_product(left, outside[i], allowed_ref, first - 1 + i * (nloc + 1), high.at[i], low.at[i])


def second_product(blocks_of, shifts_ref, high, low, right_hi, right_lo, out):
    rows, width = out.shape[1:]

    def left(parts):
        columns = []
        for k in range(shifts_ref.shape[0]):
            at = slice(k * rows, (k + 1) * rows)
            columns.append(jnp.concatenate(blocks_of(parts, shifts_ref[k], at)))
        return jnp.concatenate(columns, axis=1)

    out[...] = dot3((left(high), left(low)), (right_hi[...], right_lo[...])).reshape(out.shape)


def first_inner(nloc, shifts_ref, high, low, right_hi, right_lo, out):
    def blocks_of(own, shift, at):
        return [own[t - shift, at] for t in range(1, nloc - 1)]

    second_product(blocks_of, shifts_ref, high, low, right_hi, right_lo, out)


def first_outer(nloc, shifts_ref, high, low, end_high, end_low, right_hi, right_lo, out):
    def blocks_of(parts, shift, at):
        own, ends = parts
        start = jnp.where(shift == 1, ends[0, at], own[jnp.maximum(-shift, 0), at])
        end = jnp.where(shift == -1, ends[1, at], own[jnp.minimum(nloc - 1 - shift, nloc - 1), at])
        return [start, end]

    second_product(blocks_of, shifts_ref, (high, end_high), (low, end_low), right_hi, right_lo, out)


def later_chunk(n, nloc, step, shifts_ref, allowed_ref, outer, inner, outside, left_parts, right_hi, right_lo, outer_out, inner_out, high, low):
    left = chunk_left(n, step, left_parts)
    first = lax.axis_index(("sec", "sub")) * nloc
    sources = [outside.at[0], outer.at[0], *[inner.at[i] for i in range(nloc - 2)], outer.at[1], outside.at[1]]
    for i, ref in enumerate(sources):
        first_product(left, ref[...], allowed_ref, first - 1 + i, high.at[i], low.at[i])

    def inner_blocks(parts, shift, at):
        return [parts[t + 1 - shift, at] for t in range(1, nloc - 1)]

    def outer_blocks(parts, shift, at):
        return [parts[t + 1 - shift, at] for t in (0, nloc - 1)]

    second_product(inner_blocks, shifts_ref, high, low, right_hi, right_lo, inner_out)
    second_product(outer_blocks, shifts_ref, high, low, right_hi, right_lo, outer_out)


def call(body, name, flops, out_shape, in_specs, operands, scratch=()):
    return pl.pallas_call(
        body,
        name=name,
        out_shape=out_shape,
        in_specs=in_specs,
        out_specs=jax.tree.map(lambda _: VMEM, out_shape),
        scratch_shapes=list(scratch),
        compiler_params=pltpu.CompilerParams(vmem_limit_bytes=24 * 2**20),
        cost_estimate=pl.CostEstimate(flops=flops, bytes_accessed=2**20, transcendentals=0),
    )(*operands)


def shards(psi, left_ops, right_ops, shifts, allowed):
    nloc, rows, width = psi.shape
    kops = left_ops.shape[0]
    n = lax.axis_size("op")
    route = ring_route(n)
    one = 6 * width**3

    tall = jax.ShapeDtypeStruct((kops * width, width), BF16)
    parts = jax.ShapeDtypeStruct((n, kops, rows, 3 * width), BF16)
    zero = jax.ShapeDtypeStruct((1, 128), F32)
    left_parts, right_hi, right_lo, zero = call(
        prepare, "prepare", 4 * kops * one, [parts, tall, tall, zero], [VMEM] * 2, [left_ops, right_ops]
    )

    blocks = [psi, lax.ppermute(psi, "op", route)]
    outer, inner = [[b[:: nloc - 1] for b in blocks], [b[1 : nloc - 1] for b in blocks]]
    for step in range(1, n - 1):
        outer.append(lax.ppermute(outer[-1] + zero[0, 0] if step == 1 else outer[-1], "op", route))
        inner.append(lax.ppermute(inner[-1] + zero[0, 0] if step == 1 else inner[-1], "op", route))

    above = shifted(jnp.concatenate([b[1:] for b in outer]), ("sec", "sub"), 1)
    below = shifted(jnp.concatenate([b[:1] for b in outer]), ("sec", "sub"), -1)

    def split_parts(sectors):
        return jax.ShapeDtypeStruct((sectors, 3 * width, width), BF16)

    def whole(sectors):
        return [pltpu.VMEM((sectors, width, width), F32)]

    parts_outer = call(functools.partial(assemble, n), "assemble", 4 * kops * one, split_parts(2), [VMEM] * n, outer, whole(2))
    def products(sectors):
        return [jax.ShapeDtypeStruct((sectors, kops * rows, width), BF16)] * 2

    chunk = jax.ShapeDtypeStruct((2, rows, width), F32)
    chunk_inner = jax.ShapeDtypeStruct((nloc - 2, rows, width), F32)
    parts_inner, *own = call(
        functools.partial(own_sectors, n), "own", 4 * kops * one, [split_parts(nloc - 2), *products(nloc)],
        [SMEM] + [VMEM] * (n + 2), [allowed, *inner, parts_outer, left_parts], whole(nloc - 2),
    )
    result_inner = call(
        functools.partial(first_inner, nloc), "first_inner", nloc * kops * one // n, chunk_inner,
        [SMEM] + [VMEM] * 4, [shifts, *own, right_hi, right_lo],
    )
    parts_outside, *ends = call(
        functools.partial(outside_sectors, n, nloc), "outside", 2 * kops * one, [split_parts(2), *products(2)],
        [SMEM] + [VMEM] * 3, [allowed, above, below, left_parts], whole(2),
    )
    result_outer = call(
        functools.partial(first_outer, nloc), "first_outer", nloc * kops * one // n, chunk,
        [SMEM] + [VMEM] * 6, [shifts, *own, *ends, right_hi, right_lo],
    )

    def mine(step):
        return call(
            functools.partial(later_chunk, n, nloc, step), "chunk", 4 * nloc * kops * one // n, [chunk, chunk_inner],
            [SMEM] * 2 + [VMEM] * 6,
            [shifts, allowed, parts_outer, parts_inner, parts_outside, left_parts, right_hi, right_lo],
            [pltpu.VMEM((nloc + 2, kops * rows, width), BF16)] * 2,
        )

    for step in range(1, n):
        next_outer, next_inner = mine(step)
        result_inner = lax.ppermute(result_inner, "op", route) + next_inner
        result_outer = lax.ppermute(result_outer, "op", route) + next_outer
    return jnp.concatenate([result_outer[:1], result_inner, result_outer[1:]])


def solution(mesh):
    return jax.shard_map(
        shards,
        mesh=mesh,
        in_specs=(
            P(("parts", "sec", "sub"), "op", None),
            P("op", None, None),
            P("op", None, None),
            P("op"),
            P("op", None),
        ),
        out_specs=P(("parts", "sec", "sub"), "op", None),
        check_vma=False,
    )
```

```python
import functools

import jax
import jax.numpy as jnp
from jax import lax
from jax.experimental import pallas as pl
from jax.experimental.pallas import tpu as pltpu
from jax.sharding import PartitionSpec as P

F32, BF16 = jnp.float32, jnp.bfloat16
SMEM = pl.BlockSpec(memory_space=pltpu.SMEM)
VMEM = pl.BlockSpec(memory_space=pltpu.VMEM)


def shifted(block, axis, distance):
    devices = range(lax.axis_size(axis))
    route = [(i - distance, i) for i in devices if i - distance in devices]
    return lax.ppermute(block, axis, route)


def ring_route(n):
    order = [0] + [i for i in range(n) if i % 2] + [i for i in reversed(range(1, n)) if i % 2 == 0]
    return [(order[i], order[(i + 1) % n]) for i in range(n)]


def ring_place(n, steps_back):
    me = lax.axis_index("op")
    place = jnp.where(me == 0, 0, jnp.where(lax.rem(me, 2) == 1, (me + 1) // 2, n - me // 2))
    at = lax.rem(place - steps_back + 2 * n, n)
    return jnp.where(at == 0, 0, jnp.where(at <= n // 2, 2 * at - 1, 2 * (n - at)))


def on_line(n):
    return n == 4


def block_owner(n, j):
    return jnp.bitwise_xor(lax.axis_index("op"), j) if on_line(n) else ring_place(n, j)


def chunk_target(n, step):
    return jnp.bitwise_xor(lax.axis_index("op"), n - 1 - step) if on_line(n) else ring_place(n, step + 1)


def split(x):
    hi = x.astype(BF16)
    return hi, (x - hi.astype(F32)).astype(BF16)


def dot3(a, b):
    one = functools.partial(jnp.dot, preferred_element_type=F32)
    return one(a[0], b[0]) + (one(a[0], b[1]) + one(a[1], b[0]))


def prepare(left_ref, right_ref, left_parts, right_hi, right_lo, zero):
    n, kops, rows, _ = left_parts.shape
    width = left_ref.shape[1]
    zero[...] = jnp.zeros_like(zero)
    for k in range(kops):
        hi, lo = split(left_ref[k])
        parts = jnp.concatenate([hi, hi, lo], axis=1)
        for c in range(n):
            left_parts[c, k] = parts[c * rows : (c + 1) * rows]
        right_hi[k * width : (k + 1) * width, :], right_lo[k * width : (k + 1) * width, :] = split(right_ref[k].T)


def stacked(block):
    hi, lo = split(block)
    return jnp.concatenate([hi, lo, hi], axis=0)


def place_rows(n, target, blocks):
    for j, block in enumerate(blocks):
        rows = block.shape[-2]
        target[..., pl.ds(pl.multiple_of(block_owner(n, j) * rows, rows), rows), :] = block


def assemble(n, *refs):
    parts, psi = refs[n:]
    place_rows(n, psi, [ref[...] for ref in refs[:n]])
    for i in range(parts.shape[0]):
        parts[i] = stacked(psi[i])


def first_product(left, parts, allowed_ref, source, high, low):
    kops, sectors = allowed_ref.shape
    block = jnp.dot(left, parts, preferred_element_type=F32)
    rows = block.shape[0] // kops
    source = jnp.clip(source, 0, sectors - 1)
    for k in range(kops):
        at = slice(k * rows, (k + 1) * rows)
        high[at], low[at] = split(block[at] * allowed_ref[k, source].astype(F32))


def chunk_left(n, step, left_parts):
    return left_parts[chunk_target(n, step)].reshape(-1, left_parts.shape[-1])


def own_sectors(n, allowed_ref, *refs):
    (outer, left_parts), (inner, high, low, psi) = refs[n : n + 2], refs[n + 2 :]
    assemble(n, *refs[:n], inner, psi)
    left = chunk_left(n, 0, left_parts)
    nloc = high.shape[0]
    first = lax.axis_index(("sec", "sub")) * nloc
    sources = [outer.at[0], *[inner.at[i] for i in range(nloc - 2)], outer.at[1]]
    for i, ref in enumerate(sources):
        first_product(left, ref[...], allowed_ref, first + i, high.at[i], low.at[i])


def outside_sectors(n, nloc, allowed_ref, above, below, left_parts, outside, high, low, psi):
    place_rows(n, psi.at[0], [above[j] for j in range(n)])
    place_rows(n, psi.at[1], [below[j] for j in range(n)])
    left = chunk_left(n, 0, left_parts)
    first = lax.axis_index(("sec", "sub")) * nloc
    for i in range(2):
        outside[i] = stacked(psi[i])
        first_product(left, outside[i], allowed_ref, first - 1 + i * (nloc + 1), high.at[i], low.at[i])


def second_product(blocks_of, shifts_ref, high, low, right_hi, right_lo, rows):

    def left(parts):
        columns = []
        for k in range(shifts_ref.shape[0]):
            at = slice(k * rows, (k + 1) * rows)
            columns.append(jnp.concatenate(blocks_of(parts, shifts_ref[k], at)))
        return jnp.concatenate(columns, axis=1)

    total = dot3((left(high), left(low)), (right_hi[...], right_lo[...]))
    return total.reshape(-1, rows, total.shape[1])


def first_inner(nloc, shifts_ref, high, low, right_hi, right_lo, out):
    def blocks_of(own, shift, at):
        return [own[t - shift, at] for t in range(1, nloc - 1)]

    out[...] = second_product(blocks_of, shifts_ref, high, low, right_hi, right_lo, out.shape[1])


def first_outer(nloc, shifts_ref, high, low, end_high, end_low, right_hi, right_lo, out):
    def blocks_of(parts, shift, at):
        own, ends = parts
        start = jnp.where(shift == 1, ends[0, at], own[jnp.maximum(-shift, 0), at])
        end = jnp.where(shift == -1, ends[1, at], own[jnp.minimum(nloc - 1 - shift, nloc - 1), at])
        return [start, end]

    out[...] = second_product(blocks_of, shifts_ref, (high, end_high), (low, end_low), right_hi, right_lo, out.shape[1])


def later_chunk(n, nloc, step, shifts_ref, allowed_ref, outer, inner, outside, left_parts, right_hi, right_lo, *refs):
    out, high, low = refs[-3:]
    left = chunk_left(n, step, left_parts)
    first = lax.axis_index(("sec", "sub")) * nloc
    sources = [outside.at[0], outer.at[0], *[inner.at[i] for i in range(nloc - 2)], outer.at[1], outside.at[1]]
    for i, ref in enumerate(sources):
        first_product(left, ref[...], allowed_ref, first - 1 + i, high.at[i], low.at[i])

    def inner_blocks(parts, shift, at):
        return [parts[t + 1 - shift, at] for t in range(1, nloc - 1)]

    def outer_blocks(parts, shift, at):
        return [parts[t + 1 - shift, at] for t in (0, nloc - 1)]

    out[1 : nloc - 1] = second_product(inner_blocks, shifts_ref, high, low, right_hi, right_lo, out.shape[1])
    ends = second_product(outer_blocks, shifts_ref, high, low, right_hi, right_lo, out.shape[1])
    out[0], out[nloc - 1] = ends[0], ends[1]


def call(body, name, flops, out_shape, in_specs, operands, scratch=()):
    return pl.pallas_call(
        body,
        name=name,
        out_shape=out_shape,
        in_specs=in_specs,
        out_specs=jax.tree.map(lambda _: VMEM, out_shape),
        scratch_shapes=list(scratch),
        compiler_params=pltpu.CompilerParams(vmem_limit_bytes=24 * 2**20),
        cost_estimate=pl.CostEstimate(flops=flops, bytes_accessed=2**20, transcendentals=0),
    )(*operands)


INWARDS, ACROSS, OUTWARDS, PAIRS = [(0, 1), (3, 2)], [(1, 2), (2, 1)], [(1, 0), (2, 3)], [(0, 1), (1, 0), (2, 3), (3, 2)]


def gather(n, psi, zero):
    nloc = psi.shape[0]
    halves = [lambda b: b[:: nloc - 1], lambda b: b[1 : nloc - 1]]
    if not on_line(n):
        blocks = [psi]
        for _ in range(n - 1):
            blocks.append(lax.ppermute(blocks[-1], "op", ring_route(n)))
        return [[part(b) for b in blocks] for part in halves]
    one = lax.ppermute(psi, "op", PAIRS)
    three = lax.ppermute(psi, "op", ACROSS)
    far = lax.ppermute(one + zero, "op", ACROSS)
    two = far + lax.ppermute(three + zero, "op", OUTWARDS)
    three, far = [lax.optimization_barrier([part(b) for part in halves]) for b in (three, far)]
    last = [t + lax.ppermute(f, "op", OUTWARDS) for t, f in zip(three, far)]
    return [[part(psi), part(one), part(two), end] for part, end in zip(halves, last)]


def joined(outer, inner):
    return jnp.concatenate([outer[:1], inner, outer[1:]])


def scatter(n, outer, inner, mine):
    first = joined(outer, inner)
    if not on_line(n):
        result = first
        for step in range(1, n):
            result = lax.ppermute(result, "op", ring_route(n)) + mine(step)
        return result
    from_end = joined(lax.ppermute(outer, "op", INWARDS), lax.ppermute(inner, "op", INWARDS))
    second = mine(1)
    near = lax.ppermute(second, "op", INWARDS)
    through = second + from_end
    far = lax.ppermute(through, "op", ACROSS)
    across = lax.ppermute(first + near, "op", ACROSS)
    pair = lax.ppermute(mine(2, through) + far, "op", PAIRS)
    return mine(3) + across + pair


def shards(psi, left_ops, right_ops, shifts, allowed):
    nloc, rows, width = psi.shape
    kops = left_ops.shape[0]
    n = lax.axis_size("op")
    one = 6 * width**3

    tall = jax.ShapeDtypeStruct((kops * width, width), BF16)
    parts = jax.ShapeDtypeStruct((n, kops, rows, 3 * width), BF16)
    zero = jax.ShapeDtypeStruct((1, 128), F32)
    left_parts, right_hi, right_lo, zero = call(
        prepare, "prepare", 4 * kops * one, [parts, tall, tall, zero], [VMEM] * 2, [left_ops, right_ops]
    )

    outer, inner = gather(n, psi, zero[0, 0])
    above = shifted(jnp.concatenate([b[1:] for b in outer]), ("sec", "sub"), 1)
    below = shifted(jnp.concatenate([b[:1] for b in outer]), ("sec", "sub"), -1)

    def split_parts(sectors):
        return jax.ShapeDtypeStruct((sectors, 3 * width, width), BF16)

    def whole(sectors):
        return [pltpu.VMEM((sectors, width, width), F32)]

    parts_outer = call(functools.partial(assemble, n), "assemble", 4 * kops * one, split_parts(2), [VMEM] * n, outer, whole(2))
    def products(sectors):
        return [jax.ShapeDtypeStruct((sectors, kops * rows, width), BF16)] * 2

    chunk = jax.ShapeDtypeStruct((2, rows, width), F32)
    chunk_inner = jax.ShapeDtypeStruct((nloc - 2, rows, width), F32)
    parts_inner, *own = call(
        functools.partial(own_sectors, n), "own", 4 * kops * one, [split_parts(nloc - 2), *products(nloc)],
        [SMEM] + [VMEM] * (n + 2), [allowed, *inner, parts_outer, left_parts], whole(nloc - 2),
    )
    result_inner = call(
        functools.partial(first_inner, nloc), "first_inner", nloc * kops * one // n, chunk_inner,
        [SMEM] + [VMEM] * 4, [shifts, *own, right_hi, right_lo],
    )
    parts_outside, *ends = call(
        functools.partial(outside_sectors, n, nloc), "outside", 2 * kops * one, [split_parts(2), *products(2)],
        [SMEM] + [VMEM] * 3, [allowed, above, below, left_parts], whole(2),
    )
    result_outer = call(
        functools.partial(first_outer, nloc), "first_outer", nloc * kops * one // n, chunk,
        [SMEM] + [VMEM] * 6, [shifts, *own, *ends, right_hi, right_lo],
    )

    def mine(step, *before):
        return call(
            functools.partial(later_chunk, n, nloc, step), "chunk", 4 * nloc * kops * one // n,
            jax.ShapeDtypeStruct((nloc, rows, width), F32), [SMEM] * 2 + [VMEM] * 6 + [pl.BlockSpec(memory_space=pl.ANY)] * len(before),
            [shifts, allowed, parts_outer, parts_inner, parts_outside, left_parts, right_hi, right_lo, *before],
            [pltpu.VMEM((nloc + 2, kops * rows, width), BF16)] * 2,
        )

    return scatter(n, result_outer, result_inner, mine)


def solution(mesh):
    return jax.shard_map(
        shards,
        mesh=mesh,
        in_specs=(
            P(("parts", "sec", "sub"), "op", None),
            P("op", None, None),
            P("op", None, None),
            P("op"),
            P("op", None),
        ),
        out_specs=P(("parts", "sec", "sub"), "op", None),
        check_vma=False,
    )
```

```python
import functools

import jax
import jax.numpy as jnp
from jax import lax
from jax.experimental import pallas as pl
from jax.experimental.pallas import tpu as pltpu
from jax.sharding import PartitionSpec as P

F32, BF16 = jnp.float32, jnp.bfloat16
SMEM = pl.BlockSpec(memory_space=pltpu.SMEM)
VMEM = pl.BlockSpec(memory_space=pltpu.VMEM)


def sector_group():
    return lax.axis_index(("sec", "sub"))


def swapped(block, odd):
    groups = lax.axis_size(("sec", "sub"))
    pairs = [(i, i + 1) for i in range(odd, groups - 1, 2)]
    return lax.ppermute(block, ("sec", "sub"), pairs + [(j, i) for i, j in pairs])


def ring_route(n):
    order = [0] + [i for i in range(n) if i % 2] + [i for i in reversed(range(1, n)) if i % 2 == 0]
    return [(order[i], order[(i + 1) % n]) for i in range(n)]


def ring_place(n, steps_back):
    me = lax.axis_index("op")
    place = jnp.where(me == 0, 0, jnp.where(lax.rem(me, 2) == 1, (me + 1) // 2, n - me // 2))
    at = lax.rem(place - steps_back + 2 * n, n)
    return jnp.where(at == 0, 0, jnp.where(at <= n // 2, 2 * at - 1, 2 * (n - at)))


def split(x):
    hi = x.astype(BF16)
    return hi, (x - hi.astype(F32)).astype(BF16)


def dot3(a, b):
    one = functools.partial(jnp.dot, preferred_element_type=F32)
    return one(a[0], b[0]) + (one(a[0], b[1]) + one(a[1], b[0]))


def prepare(left_ref, right_ref, left_parts, right_hi, right_lo, zero):
    n, kops, rows, _ = left_parts.shape
    width = left_ref.shape[1]
    zero[...] = jnp.zeros_like(zero)
    for k in range(kops):
        hi, lo = split(left_ref[k])
        parts = jnp.concatenate([hi, hi, lo], axis=1)
        for c in range(n):
            left_parts[c, k] = parts[c * rows : (c + 1) * rows]
        right_hi[k * width : (k + 1) * width, :], right_lo[k * width : (k + 1) * width, :] = split(right_ref[k].T)


def stacked(block):
    hi, lo = split(block)
    return jnp.concatenate([hi, lo, hi], axis=0)


def place_rows(n, target, blocks):
    for j, block in enumerate(blocks):
        rows = block.shape[-2]
        target[..., pl.ds(pl.multiple_of(ring_place(n, j) * rows, rows), rows), :] = block


def assemble(n, *refs):
    parts, psi = refs[n:]
    place_rows(n, psi, [ref[...] for ref in refs[:n]])
    for i in range(parts.shape[0]):
        parts[i] = stacked(psi[i])


def first_product(left, parts, allowed_ref, source, high, low):
    kops, sectors = allowed_ref.shape
    block = jnp.dot(left, parts, preferred_element_type=F32)
    rows = block.shape[0] // kops
    source = jnp.clip(source, 0, sectors - 1)
    for k in range(kops):
        at = slice(k * rows, (k + 1) * rows)
        high[at], low[at] = split(block[at] * allowed_ref[k, source].astype(F32))


def chunk_left(n, step, left_parts):
    return left_parts[ring_place(n, step + 1)].reshape(-1, left_parts.shape[-1])


def own_sectors(n, allowed_ref, *refs):
    (outer, left_parts), (inner, high, low, psi) = refs[n : n + 2], refs[n + 2 :]
    assemble(n, *refs[:n], inner, psi)
    left = chunk_left(n, 0, left_parts)
    nloc = high.shape[0]
    first = sector_group() * nloc
    sources = [outer.at[0], *[inner.at[i] for i in range(nloc - 2)], outer.at[1]]
    for i, ref in enumerate(sources):
        first_product(left, ref[...], allowed_ref, first + i, high.at[i], low.at[i])


def outside_sectors(n, nloc, allowed_ref, paired, apart, left_parts, outside, high, low, psi):
    odd = lax.rem(sector_group(), 2)
    place_rows(n, psi.at[odd], [apart[j] for j in range(n)])
    place_rows(n, psi.at[1 - odd], [paired[j] for j in range(n)])
    left = chunk_left(n, 0, left_parts)
    first = sector_group() * nloc
    for i in range(2):
        outside[i] = stacked(psi[i])
        first_product(left, outside[i], allowed_ref, first - 1 + i * (nloc + 1), high.at[i], low.at[i])


def second_product(blocks_of, shifts_ref, high, low, right_hi, right_lo, out):
    rows, width = out.shape[1:]

    def left(parts):
        columns = []
        for k in range(shifts_ref.shape[0]):
            at = slice(k * rows, (k + 1) * rows)
            columns.append(jnp.concatenate(blocks_of(parts, shifts_ref[k], at)))
        return jnp.concatenate(columns, axis=1)

    out[...] = dot3((left(high), left(low)), (right_hi[...], right_lo[...])).reshape(out.shape)


def first_inner(nloc, shifts_ref, high, low, right_hi, right_lo, out):
    def blocks_of(own, shift, at):
        return [own[t - shift, at] for t in range(1, nloc - 1)]

    second_product(blocks_of, shifts_ref, high, low, right_hi, right_lo, out)


def first_outer(nloc, shifts_ref, high, low, end_high, end_low, right_hi, right_lo, out):
    def blocks_of(parts, shift, at):
        own, ends = parts
        start = jnp.where(shift == 1, ends[0, at], own[jnp.maximum(-shift, 0), at])
        end = jnp.where(shift == -1, ends[1, at], own[jnp.minimum(nloc - 1 - shift, nloc - 1), at])
        return [start, end]

    second_product(blocks_of, shifts_ref, (high, end_high), (low, end_low), right_hi, right_lo, out)


def later_chunk(n, nloc, step, shifts_ref, allowed_ref, outer, inner, outside, left_parts, right_hi, right_lo, outer_out, inner_out, high, low):
    left = chunk_left(n, step, left_parts)
    first = sector_group() * nloc
    sources = [outside.at[0], outer.at[0], *[inner.at[i] for i in range(nloc - 2)], outer.at[1], outside.at[1]]
    for i, ref in enumerate(sources):
        first_product(left, ref[...], allowed_ref, first - 1 + i, high.at[i], low.at[i])

    def inner_blocks(parts, shift, at):
        return [parts[t + 1 - shift, at] for t in range(1, nloc - 1)]

    def outer_blocks(parts, shift, at):
        return [parts[t + 1 - shift, at] for t in (0, nloc - 1)]

    second_product(inner_blocks, shifts_ref, high, low, right_hi, right_lo, inner_out)
    second_product(outer_blocks, shifts_ref, high, low, right_hi, right_lo, outer_out)


def call(body, name, flops, out_shape, in_specs, operands, scratch=()):
    return pl.pallas_call(
        body,
        name=name,
        out_shape=out_shape,
        in_specs=in_specs,
        out_specs=jax.tree.map(lambda _: VMEM, out_shape),
        scratch_shapes=list(scratch),
        compiler_params=pltpu.CompilerParams(vmem_limit_bytes=24 * 2**20),
        cost_estimate=pl.CostEstimate(flops=flops, bytes_accessed=2**20, transcendentals=0),
    )(*operands)


def shards(psi, left_ops, right_ops, shifts, allowed):
    nloc, rows, width = psi.shape
    kops = left_ops.shape[0]
    n = lax.axis_size("op")
    route = ring_route(n)
    one = 6 * width**3

    tall = jax.ShapeDtypeStruct((kops * width, width), BF16)
    parts = jax.ShapeDtypeStruct((n, kops, rows, 3 * width), BF16)
    zero = jax.ShapeDtypeStruct((1, 128), F32)
    left_parts, right_hi, right_lo, zero = call(
        prepare, "prepare", 4 * kops * one, [parts, tall, tall, zero], [VMEM] * 2, [left_ops, right_ops]
    )

    blocks = [psi, lax.ppermute(psi, "op", route)]
    outer, inner = [[b[:: nloc - 1] for b in blocks], [b[1 : nloc - 1] for b in blocks]]
    for step in range(1, n - 1):
        outer.append(lax.ppermute(outer[-1] + zero[0, 0] if step == 1 else outer[-1], "op", route))
        inner.append(lax.ppermute(inner[-1] + zero[0, 0] if step == 1 else inner[-1], "op", route))

    even = lax.rem(sector_group(), 2) == 0
    first_sector, last_sector = jnp.concatenate([b[:1] for b in outer]), jnp.concatenate([b[1:] for b in outer])
    apart = swapped(jnp.where(even, first_sector, last_sector), 1)
    paired = swapped(jnp.where(even, last_sector, first_sector), 0)

    def split_parts(sectors):
        return jax.ShapeDtypeStruct((sectors, 3 * width, width), BF16)

    def whole(sectors):
        return [pltpu.VMEM((sectors, width, width), F32)]

    parts_outer = call(functools.partial(assemble, n), "assemble", 4 * kops * one, split_parts(2), [VMEM] * n, outer, whole(2))
    def products(sectors):
        return [jax.ShapeDtypeStruct((sectors, kops * rows, width), BF16)] * 2

    chunk = jax.ShapeDtypeStruct((2, rows, width), F32)
    chunk_inner = jax.ShapeDtypeStruct((nloc - 2, rows, width), F32)
    parts_inner, *own = call(
        functools.partial(own_sectors, n), "own", 4 * kops * one, [split_parts(nloc - 2), *products(nloc)],
        [SMEM] + [VMEM] * (n + 2), [allowed, *inner, parts_outer, left_parts], whole(nloc - 2),
    )
    result_inner = call(
        functools.partial(first_inner, nloc), "first_inner", nloc * kops * one // n, chunk_inner,
        [SMEM] + [VMEM] * 4, [shifts, *own, right_hi, right_lo],
    )
    parts_outside, *ends = call(
        functools.partial(outside_sectors, n, nloc), "outside", 2 * kops * one, [split_parts(2), *products(2)],
        [SMEM] + [VMEM] * 3, [allowed, paired, apart, left_parts], whole(2),
    )
    result_outer = call(
        functools.partial(first_outer, nloc), "first_outer", nloc * kops * one // n, chunk,
        [SMEM] + [VMEM] * 6, [shifts, *own, *ends, right_hi, right_lo],
    )

    def mine(step):
        return call(
            functools.partial(later_chunk, n, nloc, step), "chunk", 4 * nloc * kops * one // n, [chunk, chunk_inner],
            [SMEM] * 2 + [VMEM] * 6,
            [shifts, allowed, parts_outer, parts_inner, parts_outside, left_parts, right_hi, right_lo],
            [pltpu.VMEM((nloc + 2, kops * rows, width), BF16)] * 2,
        )

    for step in range(1, n):
        next_outer, next_inner = mine(step)
        result_inner = lax.ppermute(result_inner, "op", route) + next_inner
        result_outer = lax.ppermute(result_outer, "op", route) + next_outer
    return jnp.concatenate([result_outer[:1], result_inner, result_outer[1:]])


def solution(mesh):
    return jax.shard_map(
        shards,
        mesh=mesh,
        in_specs=(
            P(("parts", "sec", "sub"), "op", None),
            P("op", None, None),
            P("op", None, None),
            P("op"),
            P("op", None),
        ),
        out_specs=P(("parts", "sec", "sub"), "op", None),
        check_vma=False,
    )
```

```python
import functools

import jax
import jax.numpy as jnp
from jax import lax
from jax.experimental import pallas as pl
from jax.experimental.pallas import tpu as pltpu
from jax.sharding import PartitionSpec as P

F32, BF16 = jnp.float32, jnp.bfloat16
SMEM = pl.BlockSpec(memory_space=pltpu.SMEM)
VMEM = pl.BlockSpec(memory_space=pltpu.VMEM)
ANY = pl.BlockSpec(memory_space=pl.ANY)


def shifted(block, axis, distance):
    devices = range(lax.axis_size(axis))
    route = [(i - distance, i) for i in devices if i - distance in devices]
    return lax.ppermute(block, axis, route)


def ring_route(n):
    order = [0] + [i for i in range(n) if i % 2] + [i for i in reversed(range(1, n)) if i % 2 == 0]
    return [(order[i], order[(i + 1) % n]) for i in range(n)]


def ring_place(n, steps_back):
    me = lax.axis_index("op")
    place = jnp.where(me == 0, 0, jnp.where(lax.rem(me, 2) == 1, (me + 1) // 2, n - me // 2))
    at = lax.rem(place - steps_back + 2 * n, n)
    return jnp.where(at == 0, 0, jnp.where(at <= n // 2, 2 * at - 1, 2 * (n - at)))


def split(x):
    hi = x.astype(BF16)
    return hi, (x - hi.astype(F32)).astype(BF16)


def dot3(a, b):
    one = functools.partial(jnp.dot, preferred_element_type=F32)
    return one(a[0], b[0]) + (one(a[0], b[1]) + one(a[1], b[0]))


def prepare(left_ref, right_ref, left_parts, right_hi, right_lo, zero):
    n, kops, rows, _ = left_parts.shape
    width = left_ref.shape[1]
    zero[...] = jnp.zeros_like(zero)
    for k in range(kops):
        hi, lo = split(left_ref[k])
        parts = jnp.concatenate([hi, hi, lo], axis=1)
        for c in range(n):
            left_parts[c, k] = parts[c * rows : (c + 1) * rows]
        right_hi[k * width : (k + 1) * width, :], right_lo[k * width : (k + 1) * width, :] = split(right_ref[k].T)


def stacked(block):
    hi, lo = split(block)
    return jnp.concatenate([hi, lo, hi], axis=0)


def place_rows(n, target, blocks):
    for j, block in enumerate(blocks):
        rows = block.shape[-2]
        target[..., pl.ds(pl.multiple_of(ring_place(n, j) * rows, rows), rows), :] = block


def assemble(n, *refs):
    parts, psi = refs[n:]
    place_rows(n, psi, [ref[...] for ref in refs[:n]])
    for i in range(parts.shape[0]):
        parts[i] = stacked(psi[i])


def first_product(left, parts, allowed_ref, source, high, low):
    kops, sectors = allowed_ref.shape
    block = jnp.dot(left, parts, preferred_element_type=F32)
    rows = block.shape[0] // kops
    source = jnp.clip(source, 0, sectors - 1)
    for k in range(kops):
        at = slice(k * rows, (k + 1) * rows)
        high[at], low[at] = split(block[at] * allowed_ref[k, source].astype(F32))


def chunk_left(n, step, left_parts):
    return left_parts[ring_place(n, step + 1)].reshape(-1, left_parts.shape[-1])


def own_sectors(n, allowed_ref, *refs):
    (outer, left_parts), (inner, high, low, psi) = refs[n : n + 2], refs[n + 2 :]
    assemble(n, *refs[:n], inner, psi)
    left = chunk_left(n, 0, left_parts)
    nloc = high.shape[0]
    first = lax.axis_index(("sec", "sub")) * nloc
    sources = [outer.at[0], *[inner.at[i] for i in range(nloc - 2)], outer.at[1]]
    for i, ref in enumerate(sources):
        first_product(left, ref[...], allowed_ref, first + i, high.at[i], low.at[i])


def outside_sectors(n, nloc, allowed_ref, above, below, left_parts, before, outside, high, low, psi):
    place_rows(n, psi.at[0], [above[j] for j in range(n)])
    place_rows(n, psi.at[1], [below[j] for j in range(n)])
    left = chunk_left(n, 0, left_parts)
    first = lax.axis_index(("sec", "sub")) * nloc
    for i in range(2):
        outside[i] = stacked(psi[i])
        first_product(left, outside[i], allowed_ref, first - 1 + i * (nloc + 1), high.at[i], low.at[i])


def second_product(blocks_of, shifts_ref, high, low, right_hi, right_lo, out):
    rows, width = out.shape[1:]

    def left(parts):
        columns = []
        for k in range(shifts_ref.shape[0]):
            at = slice(k * rows, (k + 1) * rows)
            columns.append(jnp.concatenate(blocks_of(parts, shifts_ref[k], at)))
        return jnp.concatenate(columns, axis=1)

    out[...] = dot3((left(high), left(low)), (right_hi[...], right_lo[...])).reshape(out.shape)


def inner_targets(nloc, shifts_ref, high, low, right_hi, right_lo, out):
    def blocks_of(own, shift, at):
        return [own[t - shift, at] for t in range(1, nloc - 1)]

    second_product(blocks_of, shifts_ref, high, low, right_hi, right_lo, out)


def first_inner(nloc, shifts_ref, high, low, right_hi, right_lo, out):
    inner_targets(nloc, shifts_ref, high, low, right_hi, right_lo, out)


def next_inner(n, nloc, shifts_ref, allowed_ref, outer, inner, left_parts, right_hi, right_lo, before, out, high, low):
    left = chunk_left(n, 1, left_parts)
    first = lax.axis_index(("sec", "sub")) * nloc
    for i, ref in enumerate([outer.at[0], *[inner.at[i] for i in range(nloc - 2)], outer.at[1]]):
        first_product(left, ref[...], allowed_ref, first + i, high.at[i], low.at[i])
    inner_targets(nloc, shifts_ref, high, low, right_hi, right_lo, out)


def outer_targets(nloc, shifts_ref, high, low, end_high, end_low, right_hi, right_lo, out):
    def blocks_of(parts, shift, at):
        own, ends = parts
        start = jnp.where(shift == 1, ends[0, at], own[jnp.maximum(-shift, 0), at])
        end = jnp.where(shift == -1, ends[1, at], own[jnp.minimum(nloc - 1 - shift, nloc - 1), at])
        return [start, end]

    second_product(blocks_of, shifts_ref, (high, end_high), (low, end_low), right_hi, right_lo, out)


def first_outer(nloc, shifts_ref, high, low, end_high, end_low, right_hi, right_lo, out):
    outer_targets(nloc, shifts_ref, high, low, end_high, end_low, right_hi, right_lo, out)


def next_outer(n, nloc, shifts_ref, allowed_ref, high, low, outside, left_parts, right_hi, right_lo, before, out, end_high, end_low):
    left = chunk_left(n, 1, left_parts)
    first = lax.axis_index(("sec", "sub")) * nloc
    for i in range(2):
        first_product(left, outside[i], allowed_ref, first - 1 + i * (nloc + 1), end_high.at[i], end_low.at[i])
    outer_targets(nloc, shifts_ref, high, low, end_high, end_low, right_hi, right_lo, out)


def later_chunk(n, nloc, step, shifts_ref, allowed_ref, outer, inner, outside, left_parts, right_hi, right_lo, outer_out, inner_out, high, low):
    left = chunk_left(n, step, left_parts)
    first = lax.axis_index(("sec", "sub")) * nloc
    sources = [outside.at[0], outer.at[0], *[inner.at[i] for i in range(nloc - 2)], outer.at[1], outside.at[1]]
    for i, ref in enumerate(sources):
        first_product(left, ref[...], allowed_ref, first - 1 + i, high.at[i], low.at[i])

    def inner_blocks(parts, shift, at):
        return [parts[t + 1 - shift, at] for t in range(1, nloc - 1)]

    def outer_blocks(parts, shift, at):
        return [parts[t + 1 - shift, at] for t in (0, nloc - 1)]

    second_product(inner_blocks, shifts_ref, high, low, right_hi, right_lo, inner_out)
    second_product(outer_blocks, shifts_ref, high, low, right_hi, right_lo, outer_out)


def call(body, name, flops, out_shape, in_specs, operands, scratch=()):
    return pl.pallas_call(
        body,
        name=name,
        out_shape=out_shape,
        in_specs=in_specs,
        out_specs=jax.tree.map(lambda _: VMEM, out_shape),
        scratch_shapes=list(scratch),
        compiler_params=pltpu.CompilerParams(vmem_limit_bytes=24 * 2**20),
        cost_estimate=pl.CostEstimate(flops=flops, bytes_accessed=2**20, transcendentals=0),
    )(*operands)


def shards(psi, left_ops, right_ops, shifts, allowed):
    nloc, rows, width = psi.shape
    kops = left_ops.shape[0]
    n = lax.axis_size("op")
    route = ring_route(n)
    one = 6 * width**3

    tall = jax.ShapeDtypeStruct((kops * width, width), BF16)
    parts = jax.ShapeDtypeStruct((n, kops, rows, 3 * width), BF16)
    zero = jax.ShapeDtypeStruct((1, 128), F32)
    left_parts, right_hi, right_lo, zero = call(
        prepare, "prepare", 4 * kops * one, [parts, tall, tall, zero], [VMEM] * 2, [left_ops, right_ops]
    )

    blocks = [psi, lax.ppermute(psi, "op", route)]
    outer, inner = [[b[:: nloc - 1] for b in blocks], [b[1 : nloc - 1] for b in blocks]]
    for step in range(1, n - 1):
        outer.append(lax.ppermute(outer[-1] + zero[0, 0] if step == 1 else outer[-1], "op", route))
        inner.append(lax.ppermute(inner[-1] + zero[0, 0] if step == 1 else inner[-1], "op", route))

    above = shifted(jnp.concatenate([b[1:] for b in outer]), ("sec", "sub"), 1)
    below = shifted(jnp.concatenate([b[:1] for b in outer]), ("sec", "sub"), -1)

    def split_parts(sectors):
        return jax.ShapeDtypeStruct((sectors, 3 * width, width), BF16)

    def whole(sectors):
        return [pltpu.VMEM((sectors, width, width), F32)]

    parts_outer = call(functools.partial(assemble, n), "assemble", 4 * kops * one, split_parts(2), [VMEM] * n, outer, whole(2))
    def products(sectors):
        return [jax.ShapeDtypeStruct((sectors, kops * rows, width), BF16)] * 2

    chunk = jax.ShapeDtypeStruct((2, rows, width), F32)
    chunk_inner = jax.ShapeDtypeStruct((nloc - 2, rows, width), F32)
    parts_inner, *own = call(
        functools.partial(own_sectors, n), "own", 4 * kops * one, [split_parts(nloc - 2), *products(nloc)],
        [SMEM] + [VMEM] * (n + 2), [allowed, *inner, parts_outer, left_parts], whole(nloc - 2),
    )
    result_inner = call(
        functools.partial(first_inner, nloc), "first_inner", nloc * kops * one // n, chunk_inner,
        [SMEM] + [VMEM] * 4, [shifts, *own, right_hi, right_lo],
    )
    next_inner_rows, *own_next = call(
        functools.partial(next_inner, n, nloc), "next_inner", 2 * kops * one, [chunk_inner, *products(nloc)],
        [SMEM] * 2 + [VMEM] * 5 + [ANY],
        [shifts, allowed, parts_outer, parts_inner, left_parts, right_hi, right_lo, result_inner],
    )
    parts_outside, *ends = call(
        functools.partial(outside_sectors, n, nloc), "outside", 2 * kops * one, [split_parts(2), *products(2)],
        [SMEM] + [VMEM] * 3 + [ANY], [allowed, above, below, left_parts, next_inner_rows], whole(2),
    )
    result_outer = call(
        functools.partial(first_outer, nloc), "first_outer", nloc * kops * one // n, chunk,
        [SMEM] + [VMEM] * 6, [shifts, *own, *ends, right_hi, right_lo],
    )

    next_outer_rows = call(
        functools.partial(next_outer, n, nloc), "next_outer", kops * one, chunk,
        [SMEM] * 2 + [VMEM] * 6 + [ANY],
        [shifts, allowed, *own_next, parts_outside, left_parts, right_hi, right_lo, result_outer],
        [pltpu.VMEM((2, kops * rows, width), BF16)] * 2,
    )

    def mine(step):
        if step == 1:
            return next_outer_rows, next_inner_rows
        return call(
            functools.partial(later_chunk, n, nloc, step), "chunk", 4 * nloc * kops * one // n, [chunk, chunk_inner],
            [SMEM] * 2 + [VMEM] * 6,
            [shifts, allowed, parts_outer, parts_inner, parts_outside, left_parts, right_hi, right_lo],
            [pltpu.VMEM((nloc + 2, kops * rows, width), BF16)] * 2,
        )

    for step in range(1, n):
        next_outer_chunk, next_inner_chunk = mine(step)
        result_inner = lax.ppermute(result_inner, "op", route) + next_inner_chunk
        result_outer = lax.ppermute(result_outer, "op", route) + next_outer_chunk
    return jnp.concatenate([result_outer[:1], result_inner, result_outer[1:]])


def solution(mesh):
    return jax.shard_map(
        shards,
        mesh=mesh,
        in_specs=(
            P(("parts", "sec", "sub"), "op", None),
            P("op", None, None),
            P("op", None, None),
            P("op"),
            P("op", None),
        ),
        out_specs=P(("parts", "sec", "sub"), "op", None),
        check_vma=False,
    )
```

```python
import functools

import jax
import jax.numpy as jnp
from jax import lax
from jax.experimental import pallas as pl
from jax.experimental.pallas import tpu as pltpu
from jax.sharding import PartitionSpec as P

F32, BF16 = jnp.float32, jnp.bfloat16
SMEM = pl.BlockSpec(memory_space=pltpu.SMEM)
VMEM = pl.BlockSpec(memory_space=pltpu.VMEM)


def shifted(block, axis, distance):
    devices = range(lax.axis_size(axis))
    route = [(i - distance, i) for i in devices if i - distance in devices]
    return lax.ppermute(block, axis, route)


def ring_route(n):
    order = [0] + [i for i in range(n) if i % 2] + [i for i in reversed(range(1, n)) if i % 2 == 0]
    return [(order[i], order[(i + 1) % n]) for i in range(n)]


def ring_place(n, steps_back):
    me = lax.axis_index("op")
    place = jnp.where(me == 0, 0, jnp.where(lax.rem(me, 2) == 1, (me + 1) // 2, n - me // 2))
    at = lax.rem(place - steps_back + 2 * n, n)
    return jnp.where(at == 0, 0, jnp.where(at <= n // 2, 2 * at - 1, 2 * (n - at)))


def split(x):
    hi = x.astype(BF16)
    return hi, (x - hi.astype(F32)).astype(BF16)


def dot3(a, b):
    one = functools.partial(jnp.dot, preferred_element_type=F32)
    return one(a[0], b[0]) + (one(a[0], b[1]) + one(a[1], b[0]))


def prepare(left_ref, right_ref, left_parts, right_hi, right_lo, zero):
    n, kops, rows, _ = left_parts.shape
    width = left_ref.shape[1]
    zero[...] = jnp.zeros_like(zero)
    for k in range(kops):
        hi, lo = split(left_ref[k])
        parts = jnp.concatenate([hi, hi, lo], axis=1)
        for c in range(n):
            left_parts[c, k] = parts[c * rows : (c + 1) * rows]
        right_hi[k * width : (k + 1) * width, :], right_lo[k * width : (k + 1) * width, :] = split(right_ref[k].T)


def stacked(block):
    hi, lo = split(block)
    return jnp.concatenate([hi, lo, hi], axis=0)


def place_rows(n, target, blocks):
    for j, block in enumerate(blocks):
        rows = block.shape[-2]
        target[..., pl.ds(pl.multiple_of(ring_place(n, j) * rows, rows), rows), :] = block


def assemble(n, *refs):
    parts, psi = refs[n:]
    place_rows(n, psi, [ref[...] for ref in refs[:n]])
    for i in range(parts.shape[0]):
        parts[i] = stacked(psi[i])


def first_product(left, parts, allowed_ref, source, high, low):
    kops, sectors = allowed_ref.shape
    block = jnp.dot(left, parts, preferred_element_type=F32)
    rows = block.shape[0] // kops
    source = jnp.clip(source, 0, sectors - 1)
    for k in range(kops):
        at = slice(k * rows, (k + 1) * rows)
        high[at], low[at] = split(block[at] * allowed_ref[k, source].astype(F32))


def chunk_left(n, step, left_parts):
    return left_parts[ring_place(n, step + 1)].reshape(-1, left_parts.shape[-1])


def own_sectors(n, allowed_ref, *refs):
    (outer, left_parts), (inner, high, low, psi) = refs[n : n + 2], refs[n + 2 :]
    assemble(n, *refs[:n], inner, psi)
    left = chunk_left(n, 0, left_parts)
    nloc = high.shape[0]
    first = lax.axis_index(("sec", "sub")) * nloc
    sources = [outer.at[0], *[inner.at[i] for i in range(nloc - 2)], outer.at[1]]
    for i, ref in enumerate(sources):
        first_product(left, ref[...], allowed_ref, first + i, high.at[i], low.at[i])


def second_product(blocks_of, shifts_ref, high, low, right_hi, right_lo, out):
    rows, width = out.shape[1:]

    def left(parts):
        columns = []
        for k in range(shifts_ref.shape[0]):
            at = slice(k * rows, (k + 1) * rows)
            columns.append(jnp.concatenate(blocks_of(parts, shifts_ref[k], at)))
        return jnp.concatenate(columns, axis=1)

    out[...] = dot3((left(high), left(low)), (right_hi[...], right_lo[...])).reshape(out.shape)


def first_chunk(n, nloc, shifts_ref, allowed_ref, own_high, own_low, above, below, left_parts, right_hi, right_lo, *refs):
    outer_out, inner_out, outside, end_high, end_low, psi = refs
    place_rows(n, psi.at[0], [above[j] for j in range(n)])
    place_rows(n, psi.at[1], [below[j] for j in range(n)])
    left = chunk_left(n, 0, left_parts)
    first = lax.axis_index(("sec", "sub")) * nloc
    for i in range(2):
        outside[i] = stacked(psi[i])
        first_product(left, outside[i], allowed_ref, first - 1 + i * (nloc + 1), end_high.at[i], end_low.at[i])

    def inner_blocks(parts, shift, at):
        return [parts[0][t - shift, at] for t in range(1, nloc - 1)]

    def outer_blocks(parts, shift, at):
        own, ends = parts
        start = jnp.where(shift == 1, ends[0, at], own[jnp.maximum(-shift, 0), at])
        end = jnp.where(shift == -1, ends[1, at], own[jnp.minimum(nloc - 1 - shift, nloc - 1), at])
        return [start, end]

    high, low = (own_high, end_high), (own_low, end_low)
    second_product(inner_blocks, shifts_ref, high, low, right_hi, right_lo, inner_out)
    second_product(outer_blocks, shifts_ref, high, low, right_hi, right_lo, outer_out)


def later_chunk(n, nloc, step, shifts_ref, allowed_ref, outer, inner, outside, left_parts, right_hi, right_lo, outer_out, inner_out, high, low):
    left = chunk_left(n, step, left_parts)
    first = lax.axis_index(("sec", "sub")) * nloc
    sources = [outside.at[0], outer.at[0], *[inner.at[i] for i in range(nloc - 2)], outer.at[1], outside.at[1]]
    for i, ref in enumerate(sources):
        first_product(left, ref[...], allowed_ref, first - 1 + i, high.at[i], low.at[i])

    def inner_blocks(parts, shift, at):
        return [parts[t + 1 - shift, at] for t in range(1, nloc - 1)]

    def outer_blocks(parts, shift, at):
        return [parts[t + 1 - shift, at] for t in (0, nloc - 1)]

    second_product(inner_blocks, shifts_ref, high, low, right_hi, right_lo, inner_out)
    second_product(outer_blocks, shifts_ref, high, low, right_hi, right_lo, outer_out)


def call(body, name, flops, out_shape, in_specs, operands, scratch=()):
    return pl.pallas_call(
        body,
        name=name,
        out_shape=out_shape,
        in_specs=in_specs,
        out_specs=jax.tree.map(lambda _: VMEM, out_shape),
        scratch_shapes=list(scratch),
        compiler_params=pltpu.CompilerParams(vmem_limit_bytes=24 * 2**20),
        cost_estimate=pl.CostEstimate(flops=flops, bytes_accessed=2**20, transcendentals=0),
    )(*operands)


def shards(psi, left_ops, right_ops, shifts, allowed):
    nloc, rows, width = psi.shape
    kops = left_ops.shape[0]
    n = lax.axis_size("op")
    route = ring_route(n)
    one = 6 * width**3

    tall = jax.ShapeDtypeStruct((kops * width, width), BF16)
    parts = jax.ShapeDtypeStruct((n, kops, rows, 3 * width), BF16)
    zero = jax.ShapeDtypeStruct((1, 128), F32)
    left_parts, right_hi, right_lo, zero = call(
        prepare, "prepare", 4 * kops * one, [parts, tall, tall, zero], [VMEM] * 2, [left_ops, right_ops]
    )

    blocks = [psi, lax.ppermute(psi, "op", route)]
    outer, inner = [[b[:: nloc - 1] for b in blocks], [b[1 : nloc - 1] for b in blocks]]
    for step in range(1, n - 1):
        outer.append(lax.ppermute(outer[-1] + zero[0, 0] if step == 1 else outer[-1], "op", route))
        inner.append(lax.ppermute(inner[-1] + zero[0, 0] if step == 1 else inner[-1], "op", route))

    above = shifted(jnp.concatenate([b[1:] for b in outer]), ("sec", "sub"), 1)
    below = shifted(jnp.concatenate([b[:1] for b in outer]), ("sec", "sub"), -1)

    def split_parts(sectors):
        return jax.ShapeDtypeStruct((sectors, 3 * width, width), BF16)

    def whole(sectors):
        return [pltpu.VMEM((sectors, width, width), F32)]

    parts_outer = call(functools.partial(assemble, n), "assemble", 4 * kops * one, split_parts(2), [VMEM] * n, outer, whole(2))
    def products(sectors):
        return [jax.ShapeDtypeStruct((sectors, kops * rows, width), BF16)] * 2

    chunk = jax.ShapeDtypeStruct((2, rows, width), F32)
    chunk_inner = jax.ShapeDtypeStruct((nloc - 2, rows, width), F32)
    parts_inner, *own = call(
        functools.partial(own_sectors, n), "own", 4 * kops * one, [split_parts(nloc - 2), *products(nloc)],
        [SMEM] + [VMEM] * (n + 2), [allowed, *inner, parts_outer, left_parts], whole(nloc - 2),
    )
    result_outer, result_inner, parts_outside = call(
        functools.partial(first_chunk, n, nloc), "first_chunk", 2 * kops * one, [chunk, chunk_inner, split_parts(2)],
        [SMEM] * 2 + [VMEM] * 7, [shifts, allowed, *own, above, below, left_parts, right_hi, right_lo],
        [pltpu.VMEM((2, kops * rows, width), BF16)] * 2 + whole(2),
    )

    def mine(step):
        return call(
            functools.partial(later_chunk, n, nloc, step), "chunk", 4 * nloc * kops * one // n, [chunk, chunk_inner],
            [SMEM] * 2 + [VMEM] * 6,
            [shifts, allowed, parts_outer, parts_inner, parts_outside, left_parts, right_hi, right_lo],
            [pltpu.VMEM((nloc + 2, kops * rows, width), BF16)] * 2,
        )

    for step in range(1, n):
        next_outer, next_inner = mine(step)
        result_inner = lax.ppermute(result_inner, "op", route) + next_inner
        result_outer = lax.ppermute(result_outer, "op", route) + next_outer
    return jnp.concatenate([result_outer[:1], result_inner, result_outer[1:]])


def solution(mesh):
    return jax.shard_map(
        shards,
        mesh=mesh,
        in_specs=(
            P(("parts", "sec", "sub"), "op", None),
            P("op", None, None),
            P("op", None, None),
            P("op"),
            P("op", None),
        ),
        out_specs=P(("parts", "sec", "sub"), "op", None),
        check_vma=False,
    )
```

```python
import functools

import jax
import jax.numpy as jnp
from jax import lax
from jax.experimental import pallas as pl
from jax.experimental.pallas import tpu as pltpu
from jax.sharding import PartitionSpec as P

F32, BF16 = jnp.float32, jnp.bfloat16
SMEM = pl.BlockSpec(memory_space=pltpu.SMEM)
VMEM = pl.BlockSpec(memory_space=pltpu.VMEM)


def shifted(block, axis, distance):
    devices = range(lax.axis_size(axis))
    route = [(i - distance, i) for i in devices if i - distance in devices]
    return lax.ppermute(block, axis, route)


def ring_route(n):
    order = [0] + [i for i in range(n) if i % 2] + [i for i in reversed(range(1, n)) if i % 2 == 0]
    return [(order[i], order[(i + 1) % n]) for i in range(n)]


def ring_place(n, steps_back):
    me = lax.axis_index("op")
    place = jnp.where(me == 0, 0, jnp.where(lax.rem(me, 2) == 1, (me + 1) // 2, n - me // 2))
    at = lax.rem(place - steps_back + 2 * n, n)
    return jnp.where(at == 0, 0, jnp.where(at <= n // 2, 2 * at - 1, 2 * (n - at)))


def split(x):
    hi = x.astype(BF16)
    return hi, (x - hi.astype(F32)).astype(BF16)


def dot3(a, b):
    one = functools.partial(jnp.dot, preferred_element_type=F32)
    return one(a[0], b[0]) + (one(a[0], b[1]) + one(a[1], b[0]))


def prepare(left_ref, right_ref, left_parts, right_hi, right_lo, zero):
    n, kops, rows, _ = left_parts.shape
    width = left_ref.shape[1]
    zero[...] = jnp.zeros_like(zero)
    for k in range(kops):
        hi, lo = split(left_ref[k])
        parts = jnp.concatenate([hi, hi, lo], axis=1)
        for c in range(n):
            left_parts[c, k] = parts[c * rows : (c + 1) * rows]
        right_hi[k * width : (k + 1) * width, :], right_lo[k * width : (k + 1) * width, :] = split(right_ref[k].T)


def stacked(block):
    hi, lo = split(block)
    return jnp.concatenate([hi, lo, hi], axis=0)


def place_rows(n, target, blocks):
    for j, block in enumerate(blocks):
        rows = block.shape[-2]
        target[..., pl.ds(pl.multiple_of(ring_place(n, j) * rows, rows), rows), :] = block


def assemble(n, *refs):
    parts, psi = refs[n:]
    place_rows(n, psi, [ref[...] for ref in refs[:n]])
    for i in range(parts.shape[0]):
        parts[i] = stacked(psi[i])


def first_product(left, parts, allowed_ref, source, high, low):
    kops, sectors = allowed_ref.shape
    block = jnp.dot(left, parts, preferred_element_type=F32)
    rows = block.shape[0] // kops
    source = jnp.clip(source, 0, sectors - 1)
    for k in range(kops):
        at = slice(k * rows, (k + 1) * rows)
        high[at], low[at] = split(block[at] * allowed_ref[k, source].astype(F32))


def chunk_left(n, step, left_parts):
    return left_parts[ring_place(n, step + 1)].reshape(-1, left_parts.shape[-1])


def own_sectors(n, allowed_ref, *refs):
    (outer, left_parts), (inner, high, low, psi) = refs[n : n + 2], refs[n + 2 :]
    assemble(n, *refs[:n], inner, psi)
    left = chunk_left(n, 0, left_parts)
    nloc = high.shape[0]
    first = lax.axis_index(("sec", "sub")) * nloc
    sources = [outer.at[0], *[inner.at[i] for i in range(nloc - 2)], outer.at[1]]
    for i, ref in enumerate(sources):
        first_product(left, ref[...], allowed_ref, first + i, high.at[i], low.at[i])


def second_product(blocks_of, shifts_ref, high, low, right_hi, right_lo, out):
    rows, width = out.shape[1:]

    def left(parts):
        columns = []
        for k in range(shifts_ref.shape[0]):
            at = slice(k * rows, (k + 1) * rows)
            columns.append(jnp.concatenate(blocks_of(parts, shifts_ref[k], at)))
        return jnp.concatenate(columns, axis=1)

    out[...] = dot3((left(high), left(low)), (right_hi[...], right_lo[...])).reshape(out.shape)


def first_chunk(n, nloc, shifts_ref, allowed_ref, own_high, own_low, above, below, left_parts, right_hi, right_lo, *refs):
    outer_out, inner_out, outside, end_high, end_low, psi = refs
    place_rows(n, psi.at[0], [above[j] for j in range(n)])
    place_rows(n, psi.at[1], [below[j] for j in range(n)])
    left = chunk_left(n, 0, left_parts)
    first = lax.axis_index(("sec", "sub")) * nloc
    for i in range(2):
        outside[i] = stacked(psi[i])
        first_product(left, outside[i], allowed_ref, first - 1 + i * (nloc + 1), end_high.at[i], end_low.at[i])

    def inner_blocks(parts, shift, at):
        return [parts[0][t - shift, at] for t in range(1, nloc - 1)]

    def outer_blocks(parts, shift, at):
        own, ends = parts
        start = jnp.where(shift == 1, ends[0, at], own[jnp.maximum(-shift, 0), at])
        end = jnp.where(shift == -1, ends[1, at], own[jnp.minimum(nloc - 1 - shift, nloc - 1), at])
        return [start, end]

    high, low = (own_high, end_high), (own_low, end_low)
    second_product(inner_blocks, shifts_ref, high, low, right_hi, right_lo, inner_out)
    second_product(outer_blocks, shifts_ref, high, low, right_hi, right_lo, outer_out)


def later_chunk(n, nloc, step, shifts_ref, allowed_ref, outer, inner, outside, left_parts, right_hi, right_lo, *refs):
    outer_out, inner_out, high, low = refs[-4:]
    left = chunk_left(n, step, left_parts)
    first = lax.axis_index(("sec", "sub")) * nloc
    sources = [outside.at[0], outer.at[0], *[inner.at[i] for i in range(nloc - 2)], outer.at[1], outside.at[1]]
    for i, ref in enumerate(sources):
        first_product(left, ref[...], allowed_ref, first - 1 + i, high.at[i], low.at[i])

    def inner_blocks(parts, shift, at):
        return [parts[t + 1 - shift, at] for t in range(1, nloc - 1)]

    def outer_blocks(parts, shift, at):
        return [parts[t + 1 - shift, at] for t in (0, nloc - 1)]

    second_product(inner_blocks, shifts_ref, high, low, right_hi, right_lo, inner_out)
    second_product(outer_blocks, shifts_ref, high, low, right_hi, right_lo, outer_out)


def call(body, name, flops, out_shape, in_specs, operands, scratch=()):
    return pl.pallas_call(
        body,
        name=name,
        out_shape=out_shape,
        in_specs=in_specs,
        out_specs=jax.tree.map(lambda _: VMEM, out_shape),
        scratch_shapes=list(scratch),
        compiler_params=pltpu.CompilerParams(vmem_limit_bytes=24 * 2**20),
        cost_estimate=pl.CostEstimate(flops=flops, bytes_accessed=2**20, transcendentals=0),
    )(*operands)


def shards(psi, left_ops, right_ops, shifts, allowed):
    nloc, rows, width = psi.shape
    kops = left_ops.shape[0]
    n = lax.axis_size("op")
    route = ring_route(n)
    one = 6 * width**3

    tall = jax.ShapeDtypeStruct((kops * width, width), BF16)
    parts = jax.ShapeDtypeStruct((n, kops, rows, 3 * width), BF16)
    zero = jax.ShapeDtypeStruct((1, 128), F32)
    left_parts, right_hi, right_lo, zero = call(
        prepare, "prepare", 4 * kops * one, [parts, tall, tall, zero], [VMEM] * 2, [left_ops, right_ops]
    )

    blocks = [psi, lax.ppermute(psi, "op", route)]
    outer, inner = [[b[:: nloc - 1] for b in blocks], [b[1 : nloc - 1] for b in blocks]]
    for step in range(1, n - 1):
        outer.append(lax.ppermute(outer[-1] + zero[0, 0] if step == 1 else outer[-1], "op", route))
        inner.append(lax.ppermute(inner[-1] + zero[0, 0] if step == 1 else inner[-1], "op", route))

    above = shifted(jnp.concatenate([b[1:] for b in outer]), ("sec", "sub"), 1)
    below = shifted(jnp.concatenate([b[:1] for b in outer]), ("sec", "sub"), -1)

    def split_parts(sectors):
        return jax.ShapeDtypeStruct((sectors, 3 * width, width), BF16)

    def whole(sectors):
        return [pltpu.VMEM((sectors, width, width), F32)]

    parts_outer = call(functools.partial(assemble, n), "assemble", 4 * kops * one, split_parts(2), [VMEM] * n, outer, whole(2))
    def products(sectors):
        return [jax.ShapeDtypeStruct((sectors, kops * rows, width), BF16)] * 2

    chunk = jax.ShapeDtypeStruct((2, rows, width), F32)
    chunk_inner = jax.ShapeDtypeStruct((nloc - 2, rows, width), F32)
    parts_inner, *own = call(
        functools.partial(own_sectors, n), "own", 4 * kops * one, [split_parts(nloc - 2), *products(nloc)],
        [SMEM] + [VMEM] * (n + 2), [allowed, *inner, parts_outer, left_parts], whole(nloc - 2),
    )
    result_outer, result_inner, parts_outside = call(
        functools.partial(first_chunk, n, nloc), "first_chunk", 2 * kops * one, [chunk, chunk_inner, split_parts(2)],
        [SMEM] * 2 + [VMEM] * 7, [shifts, allowed, *own, above, below, left_parts, right_hi, right_lo],
        [pltpu.VMEM((2, kops * rows, width), BF16)] * 2 + whole(2),
    )

    def mine(step, *before):
        return call(
            functools.partial(later_chunk, n, nloc, step), "chunk", 4 * nloc * kops * one // n, [chunk, chunk_inner],
            [SMEM] * 2 + [VMEM] * 6 + [pl.BlockSpec(memory_space=pl.ANY)] * len(before),
            [shifts, allowed, parts_outer, parts_inner, parts_outside, left_parts, right_hi, right_lo, *before],
            [pltpu.VMEM((nloc + 2, kops * rows, width), BF16)] * 2,
        )

    for step in range(1, n):
        moved_outer, moved_inner = lax.ppermute(result_outer, "op", route), lax.ppermute(result_inner, "op", route)
        before = [result_outer, result_inner] if step < n - 1 else [moved_inner]
        next_outer, next_inner = mine(step, *before)
        result_outer, result_inner = moved_outer + next_outer, moved_inner + next_inner
    return jnp.concatenate([result_outer[:1], result_inner, result_outer[1:]])


def solution(mesh):
    return jax.shard_map(
        shards,
        mesh=mesh,
        in_specs=(
            P(("parts", "sec", "sub"), "op", None),
            P("op", None, None),
            P("op", None, None),
            P("op"),
            P("op", None),
        ),
        out_specs=P(("parts", "sec", "sub"), "op", None),
        check_vma=False,
    )
```

```python
import functools

import jax
import jax.numpy as jnp
from jax import lax
from jax.experimental import pallas as pl
from jax.experimental.pallas import tpu as pltpu
from jax.sharding import PartitionSpec as P

F32, BF16 = jnp.float32, jnp.bfloat16
SMEM = pl.BlockSpec(memory_space=pltpu.SMEM)
VMEM = pl.BlockSpec(memory_space=pltpu.VMEM)


def shifted(block, axis, distance):
    devices = range(lax.axis_size(axis))
    route = [(i - distance, i) for i in devices if i - distance in devices]
    return lax.ppermute(block, axis, route)


def ring_route(n):
    order = [0] + [i for i in range(n) if i % 2] + [i for i in reversed(range(1, n)) if i % 2 == 0]
    return [(order[i], order[(i + 1) % n]) for i in range(n)]


def ring_place(n, steps_back):
    me = lax.axis_index("op")
    place = jnp.where(me == 0, 0, jnp.where(lax.rem(me, 2) == 1, (me + 1) // 2, n - me // 2))
    at = lax.rem(place - steps_back + 2 * n, n)
    return jnp.where(at == 0, 0, jnp.where(at <= n // 2, 2 * at - 1, 2 * (n - at)))


def split(x):
    hi = x.astype(BF16)
    return hi, (x - hi.astype(F32)).astype(BF16)


def dot3(a, b):
    one = functools.partial(jnp.dot, preferred_element_type=F32)
    return one(a[0], b[0]) + (one(a[0], b[1]) + one(a[1], b[0]))


def prepare(left_ref, right_ref, left_parts, right_hi, right_lo, zero):
    n, kops, rows, _ = left_parts.shape
    width = left_ref.shape[1]
    zero[...] = jnp.zeros_like(zero)
    for k in range(kops):
        hi, lo = split(left_ref[k])
        parts = jnp.concatenate([hi, hi, lo], axis=1)
        for c in range(n):
            left_parts[c, k] = parts[c * rows : (c + 1) * rows]
        right_hi[k * width : (k + 1) * width, :], right_lo[k * width : (k + 1) * width, :] = split(right_ref[k].T)


def stacked(block):
    hi, lo = split(block)
    return jnp.concatenate([hi, lo, hi], axis=0)


def place_rows(n, target, blocks):
    for j, block in enumerate(blocks):
        rows = block.shape[-2]
        target[..., pl.ds(pl.multiple_of(ring_place(n, j) * rows, rows), rows), :] = block


def assemble(n, *refs):
    parts, psi = refs[n:]
    place_rows(n, psi, [ref[...] for ref in refs[:n]])
    for i in range(parts.shape[0]):
        parts[i] = stacked(psi[i])


def first_product(left, parts, allowed_ref, source, high, low):
    kops, sectors = allowed_ref.shape
    block = jnp.dot(left, parts, preferred_element_type=F32)
    rows = block.shape[0] // kops
    source = jnp.clip(source, 0, sectors - 1)
    for k in range(kops):
        at = slice(k * rows, (k + 1) * rows)
        high[at], low[at] = split(block[at] * allowed_ref[k, source].astype(F32))


def chunk_left(n, step, left_parts):
    return left_parts[ring_place(n, step + 1)].reshape(-1, left_parts.shape[-1])


def own_sectors(n, allowed_ref, *refs):
    (outer, left_parts), (inner, high, low, psi) = refs[n : n + 2], refs[n + 2 :]
    assemble(n, *refs[:n], inner, psi)
    left = chunk_left(n, 0, left_parts)
    nloc = high.shape[0]
    first = lax.axis_index(("sec", "sub")) * nloc
    sources = [outer.at[0], *[inner.at[i] for i in range(nloc - 2)], outer.at[1]]
    for i, ref in enumerate(sources):
        first_product(left, ref[...], allowed_ref, first + i, high.at[i], low.at[i])


def second_product(blocks_of, shifts_ref, high, low, right_hi, right_lo, out):
    rows, width = out.shape[1:]

    def left(parts):
        columns = []
        for k in range(shifts_ref.shape[0]):
            at = slice(k * rows, (k + 1) * rows)
            columns.append(jnp.concatenate(blocks_of(parts, shifts_ref[k], at)))
        return jnp.concatenate(columns, axis=1)

    out[...] = dot3((left(high), left(low)), (right_hi[...], right_lo[...])).reshape(out.shape)


def first_chunk(n, nloc, shifts_ref, allowed_ref, own_high, own_low, above, below, left_parts, right_hi, right_lo, *refs):
    outer_out, inner_out, outside, end_high, end_low, psi = refs
    place_rows(n, psi.at[0], [above[j] for j in range(n)])
    place_rows(n, psi.at[1], [below[j] for j in range(n)])
    left = chunk_left(n, 0, left_parts)
    first = lax.axis_index(("sec", "sub")) * nloc
    for i in range(2):
        outside[i] = stacked(psi[i])
        first_product(left, outside[i], allowed_ref, first - 1 + i * (nloc + 1), end_high.at[i], end_low.at[i])

    def inner_blocks(parts, shift, at):
        return [parts[0][t - shift, at] for t in range(1, nloc - 1)]

    def outer_blocks(parts, shift, at):
        own, ends = parts
        start = jnp.where(shift == 1, ends[0, at], own[jnp.maximum(-shift, 0), at])
        end = jnp.where(shift == -1, ends[1, at], own[jnp.minimum(nloc - 1 - shift, nloc - 1), at])
        return [start, end]

    high, low = (own_high, end_high), (own_low, end_low)
    second_product(inner_blocks, shifts_ref, high, low, right_hi, right_lo, inner_out)
    second_product(outer_blocks, shifts_ref, high, low, right_hi, right_lo, outer_out)


def later_chunk(n, nloc, step, shifts_ref, allowed_ref, outer, inner, outside, left_parts, right_hi, right_lo, *refs):
    outer_out, inner_out, high, low = refs[-4:]
    left = chunk_left(n, step, left_parts)
    first = lax.axis_index(("sec", "sub")) * nloc
    sources = [outside.at[0], outer.at[0], *[inner.at[i] for i in range(nloc - 2)], outer.at[1], outside.at[1]]
    for i, ref in enumerate(sources):
        first_product(left, ref[...], allowed_ref, first - 1 + i, high.at[i], low.at[i])

    def inner_blocks(parts, shift, at):
        return [parts[t + 1 - shift, at] for t in range(1, nloc - 1)]

    def outer_blocks(parts, shift, at):
        return [parts[t + 1 - shift, at] for t in (0, nloc - 1)]

    second_product(inner_blocks, shifts_ref, high, low, right_hi, right_lo, inner_out)
    second_product(outer_blocks, shifts_ref, high, low, right_hi, right_lo, outer_out)


def call(body, name, flops, out_shape, in_specs, operands, scratch=()):
    return pl.pallas_call(
        body,
        name=name,
        out_shape=out_shape,
        in_specs=in_specs,
        out_specs=jax.tree.map(lambda _: VMEM, out_shape),
        scratch_shapes=list(scratch),
        compiler_params=pltpu.CompilerParams(vmem_limit_bytes=24 * 2**20),
        cost_estimate=pl.CostEstimate(flops=flops, bytes_accessed=2**20, transcendentals=0),
    )(*operands)


def shards(psi, left_ops, right_ops, shifts, allowed):
    nloc, rows, width = psi.shape
    kops = left_ops.shape[0]
    n = lax.axis_size("op")
    route = ring_route(n)
    one = 6 * width**3

    tall = jax.ShapeDtypeStruct((kops * width, width), BF16)
    parts = jax.ShapeDtypeStruct((n, kops, rows, 3 * width), BF16)
    zero = jax.ShapeDtypeStruct((1, 128), F32)
    left_parts, right_hi, right_lo, zero = call(
        prepare, "prepare", 4 * kops * one, [parts, tall, tall, zero], [VMEM] * 2, [left_ops, right_ops]
    )

    blocks = [psi, lax.ppermute(psi, "op", route)]
    outer, inner = [[b[:: nloc - 1] for b in blocks], [b[1 : nloc - 1] for b in blocks]]
    for step in range(1, n - 1):
        outer.append(lax.ppermute(outer[-1] + zero[0, 0] if step == 1 else outer[-1], "op", route))
        inner.append(lax.ppermute(inner[-1] + zero[0, 0] if step == 1 else inner[-1], "op", route))

    above = shifted(jnp.concatenate([b[1:] for b in outer]), ("sec", "sub"), 1)
    below = shifted(jnp.concatenate([b[:1] for b in outer]), ("sec", "sub"), -1)

    def split_parts(sectors):
        return jax.ShapeDtypeStruct((sectors, 3 * width, width), BF16)

    def whole(sectors):
        return [pltpu.VMEM((sectors, width, width), F32)]

    parts_outer = call(functools.partial(assemble, n), "assemble", 4 * kops * one, split_parts(2), [VMEM] * n, outer, whole(2))
    def products(sectors):
        return [jax.ShapeDtypeStruct((sectors, kops * rows, width), BF16)] * 2

    chunk = jax.ShapeDtypeStruct((2, rows, width), F32)
    chunk_inner = jax.ShapeDtypeStruct((nloc - 2, rows, width), F32)
    parts_inner, *own = call(
        functools.partial(own_sectors, n), "own", 4 * kops * one, [split_parts(nloc - 2), *products(nloc)],
        [SMEM] + [VMEM] * (n + 2), [allowed, *inner, parts_outer, left_parts], whole(nloc - 2),
    )
    result_outer, result_inner, parts_outside = call(
        functools.partial(first_chunk, n, nloc), "first_chunk", 2 * kops * one, [chunk, chunk_inner, split_parts(2)],
        [SMEM] * 2 + [VMEM] * 7, [shifts, allowed, *own, above, below, left_parts, right_hi, right_lo],
        [pltpu.VMEM((2, kops * rows, width), BF16)] * 2 + whole(2),
    )

    def mine(step, *before):
        return call(
            functools.partial(later_chunk, n, nloc, step), "chunk", 4 * nloc * kops * one // n, [chunk, chunk_inner],
            [SMEM] * 2 + [VMEM] * 6 + [pl.BlockSpec(memory_space=pl.ANY)] * len(before),
            [shifts, allowed, parts_outer, parts_inner, parts_outside, left_parts, right_hi, right_lo, *before],
            [pltpu.VMEM((nloc + 2, kops * rows, width), BF16)] * 2,
        )

    result_outer = result_outer + 0 * result_inner[:1]
    for step in range(1, n):
        moved_outer, moved_inner = lax.ppermute(result_outer, "op", route), lax.ppermute(result_inner, "op", route)
        before = [result_outer, result_inner] if step < n - 1 else [moved_inner]
        next_outer, next_inner = mine(step, *before)
        result_outer, result_inner = moved_outer + next_outer, moved_inner + next_inner
    return jnp.concatenate([result_outer[:1], result_inner, result_outer[1:]])


def solution(mesh):
    return jax.shard_map(
        shards,
        mesh=mesh,
        in_specs=(
            P(("parts", "sec", "sub"), "op", None),
            P("op", None, None),
            P("op", None, None),
            P("op"),
            P("op", None),
        ),
        out_specs=P(("parts", "sec", "sub"), "op", None),
        check_vma=False,
    )
```

```python
import functools

import jax
import jax.numpy as jnp
from jax import lax
from jax.experimental import pallas as pl
from jax.experimental.pallas import tpu as pltpu
from jax.sharding import PartitionSpec as P

F32, BF16 = jnp.float32, jnp.bfloat16
SMEM = pl.BlockSpec(memory_space=pltpu.SMEM)
VMEM = pl.BlockSpec(memory_space=pltpu.VMEM)


def shifted(block, axis, distance):
    devices = range(lax.axis_size(axis))
    route = [(i - distance, i) for i in devices if i - distance in devices]
    return lax.ppermute(block, axis, route)


def ring_route(n):
    order = [0] + [i for i in range(n) if i % 2] + [i for i in reversed(range(1, n)) if i % 2 == 0]
    return [(order[i], order[(i + 1) % n]) for i in range(n)]


def ring_place(n, steps_back):
    me = lax.axis_index("op")
    place = jnp.where(me == 0, 0, jnp.where(lax.rem(me, 2) == 1, (me + 1) // 2, n - me // 2))
    at = lax.rem(place - steps_back + 2 * n, n)
    return jnp.where(at == 0, 0, jnp.where(at <= n // 2, 2 * at - 1, 2 * (n - at)))


def split(x):
    hi = x.astype(BF16)
    return hi, (x - hi.astype(F32)).astype(BF16)


def dot3(a, b):
    one = functools.partial(jnp.dot, preferred_element_type=F32)
    return one(a[0], b[0]) + (one(a[0], b[1]) + one(a[1], b[0]))


def prepare(left_ref, right_ref, left_parts, right_hi, right_lo, zero):
    n, kops, rows, _ = left_parts.shape
    width = left_ref.shape[1]
    zero[...] = jnp.zeros_like(zero)
    for k in range(kops):
        hi, lo = split(left_ref[k])
        parts = jnp.concatenate([hi, hi, lo], axis=1)
        for c in range(n):
            left_parts[c, k] = parts[c * rows : (c + 1) * rows]
        right_hi[k * width : (k + 1) * width, :], right_lo[k * width : (k + 1) * width, :] = split(right_ref[k].T)


def stacked(block):
    hi, lo = split(block)
    return jnp.concatenate([hi, lo, hi], axis=0)


def place_rows(n, target, blocks):
    for j, block in enumerate(blocks):
        rows = block.shape[-2]
        target[..., pl.ds(pl.multiple_of(ring_place(n, j) * rows, rows), rows), :] = block


def assemble(n, *refs):
    parts, psi = refs[n:]
    place_rows(n, psi, [ref[...] for ref in refs[:n]])
    for i in range(parts.shape[0]):
        parts[i] = stacked(psi[i])


def first_product(left, parts, allowed_ref, source, high, low):
    kops, sectors = allowed_ref.shape
    block = jnp.dot(left, parts, preferred_element_type=F32)
    rows = block.shape[0] // kops
    source = jnp.clip(source, 0, sectors - 1)
    for k in range(kops):
        at = slice(k * rows, (k + 1) * rows)
        high[at], low[at] = split(block[at] * allowed_ref[k, source].astype(F32))


def chunk_left(n, step, left_parts):
    return left_parts[ring_place(n, step + 1)].reshape(-1, left_parts.shape[-1])


def own_sectors(n, allowed_ref, *refs):
    (outer, left_parts), (inner, high, low, psi) = refs[n : n + 2], refs[n + 2 :]
    assemble(n, *refs[:n], inner, psi)
    left = chunk_left(n, 0, left_parts)
    nloc = high.shape[0]
    first = lax.axis_index(("sec", "sub")) * nloc
    sources = [outer.at[0], *[inner.at[i] for i in range(nloc - 2)], outer.at[1]]
    for i, ref in enumerate(sources):
        first_product(left, ref[...], allowed_ref, first + i, high.at[i], low.at[i])


def second_product(blocks_of, shifts_ref, high, low, right_hi, right_lo, out):
    rows, width = out.shape[1:]

    def left(parts):
        columns = []
        for k in range(shifts_ref.shape[0]):
            at = slice(k * rows, (k + 1) * rows)
            columns.append(jnp.concatenate(blocks_of(parts, shifts_ref[k], at)))
        return jnp.concatenate(columns, axis=1)

    out[...] = dot3((left(high), left(low)), (right_hi[...], right_lo[...])).reshape(out.shape)


def first_chunk(n, nloc, shifts_ref, allowed_ref, own_high, own_low, above, below, left_parts, right_hi, right_lo, *refs):
    outer_out, inner_out, outside, end_high, end_low, psi = refs
    place_rows(n, psi.at[0], [above[j] for j in range(n)])
    place_rows(n, psi.at[1], [below[j] for j in range(n)])
    left = chunk_left(n, 0, left_parts)
    first = lax.axis_index(("sec", "sub")) * nloc
    for i in range(2):
        outside[i] = stacked(psi[i])
        first_product(left, outside[i], allowed_ref, first - 1 + i * (nloc + 1), end_high.at[i], end_low.at[i])

    def inner_blocks(parts, shift, at):
        return [parts[0][t - shift, at] for t in range(1, nloc - 1)]

    def outer_blocks(parts, shift, at):
        own, ends = parts
        start = jnp.where(shift == 1, ends[0, at], own[jnp.maximum(-shift, 0), at])
        end = jnp.where(shift == -1, ends[1, at], own[jnp.minimum(nloc - 1 - shift, nloc - 1), at])
        return [start, end]

    high, low = (own_high, end_high), (own_low, end_low)
    second_product(inner_blocks, shifts_ref, high, low, right_hi, right_lo, inner_out)
    second_product(outer_blocks, shifts_ref, high, low, right_hi, right_lo, outer_out)


def later_chunk(n, nloc, step, shifts_ref, allowed_ref, outer, inner, outside, left_parts, right_hi, right_lo, *refs):
    outer_out, inner_out, high, low = refs[-4:]
    left = chunk_left(n, step, left_parts)
    first = lax.axis_index(("sec", "sub")) * nloc
    sources = [outside.at[0], outer.at[0], *[inner.at[i] for i in range(nloc - 2)], outer.at[1], outside.at[1]]
    for i, ref in enumerate(sources):
        first_product(left, ref[...], allowed_ref, first - 1 + i, high.at[i], low.at[i])

    def inner_blocks(parts, shift, at):
        return [parts[t + 1 - shift, at] for t in range(1, nloc - 1)]

    def outer_blocks(parts, shift, at):
        return [parts[t + 1 - shift, at] for t in (0, nloc - 1)]

    second_product(inner_blocks, shifts_ref, high, low, right_hi, right_lo, inner_out)
    second_product(outer_blocks, shifts_ref, high, low, right_hi, right_lo, outer_out)


def call(body, name, flops, out_shape, in_specs, operands, scratch=()):
    return pl.pallas_call(
        body,
        name=name,
        out_shape=out_shape,
        in_specs=in_specs,
        out_specs=jax.tree.map(lambda _: VMEM, out_shape),
        scratch_shapes=list(scratch),
        compiler_params=pltpu.CompilerParams(vmem_limit_bytes=24 * 2**20),
        cost_estimate=pl.CostEstimate(flops=flops, bytes_accessed=2**20, transcendentals=0),
    )(*operands)


def shards(psi, left_ops, right_ops, shifts, allowed):
    nloc, rows, width = psi.shape
    kops = left_ops.shape[0]
    n = lax.axis_size("op")
    route = ring_route(n)
    one = 6 * width**3

    tall = jax.ShapeDtypeStruct((kops * width, width), BF16)
    parts = jax.ShapeDtypeStruct((n, kops, rows, 3 * width), BF16)
    zero = jax.ShapeDtypeStruct((1, 128), F32)
    left_parts, right_hi, right_lo, zero = call(
        prepare, "prepare", 4 * kops * one, [parts, tall, tall, zero], [VMEM] * 2, [left_ops, right_ops]
    )

    blocks = [psi, lax.ppermute(psi, "op", route)]
    outer, inner = [[b[:: nloc - 1] for b in blocks], [b[1 : nloc - 1] for b in blocks]]
    for step in range(1, n - 1):
        outer.append(lax.ppermute(outer[-1] + zero[0, 0] if step == 1 else outer[-1], "op", route))
        inner.append(lax.ppermute(inner[-1] + zero[0, 0] if step == 1 else inner[-1], "op", route))

    above = shifted(jnp.concatenate([b[1:] for b in outer]), ("sec", "sub"), 1)
    below = shifted(jnp.concatenate([b[:1] for b in outer]), ("sec", "sub"), -1)

    def split_parts(sectors):
        return jax.ShapeDtypeStruct((sectors, 3 * width, width), BF16)

    def whole(sectors):
        return [pltpu.VMEM((sectors, width, width), F32)]

    parts_outer = call(functools.partial(assemble, n), "assemble", 4 * kops * one, split_parts(2), [VMEM] * n, outer, whole(2))
    def products(sectors):
        return [jax.ShapeDtypeStruct((sectors, kops * rows, width), BF16)] * 2

    chunk = jax.ShapeDtypeStruct((2, rows, width), F32)
    chunk_inner = jax.ShapeDtypeStruct((nloc - 2, rows, width), F32)
    parts_inner, *own = call(
        functools.partial(own_sectors, n), "own", 4 * kops * one, [split_parts(nloc - 2), *products(nloc)],
        [SMEM] + [VMEM] * (n + 2), [allowed, *inner, parts_outer, left_parts], whole(nloc - 2),
    )
    result_outer, result_inner, parts_outside = call(
        functools.partial(first_chunk, n, nloc), "first_chunk", 2 * kops * one, [chunk, chunk_inner, split_parts(2)],
        [SMEM] * 2 + [VMEM] * 7, [shifts, allowed, *own, above, below, left_parts, right_hi, right_lo],
        [pltpu.VMEM((2, kops * rows, width), BF16)] * 2 + whole(2),
    )

    def mine(step, *before):
        return call(
            functools.partial(later_chunk, n, nloc, step), "chunk", 4 * nloc * kops * one // n, [chunk, chunk_inner],
            [SMEM] * 2 + [VMEM] * 6 + [pl.BlockSpec(memory_space=pl.ANY)] * len(before),
            [shifts, allowed, parts_outer, parts_inner, parts_outside, left_parts, right_hi, right_lo, *before],
            [pltpu.VMEM((nloc + 2, kops * rows, width), BF16)] * 2,
        )

    result_outer = result_outer + 0 * result_inner[:1]
    for step in range(1, n):
        moved_outer, moved_inner = lax.ppermute(result_outer, "op", route), lax.ppermute(result_inner, "op", route)
        before = [] if step < n - 1 else [result_outer, result_inner]
        next_outer, next_inner = mine(step, *before)
        result_outer, result_inner = moved_outer + next_outer, moved_inner + next_inner
    return jnp.concatenate([result_outer[:1], result_inner, result_outer[1:]])


def solution(mesh):
    return jax.shard_map(
        shards,
        mesh=mesh,
        in_specs=(
            P(("parts", "sec", "sub"), "op", None),
            P("op", None, None),
            P("op", None, None),
            P("op"),
            P("op", None),
        ),
        out_specs=P(("parts", "sec", "sub"), "op", None),
        check_vma=False,
    )
```

```python
import functools

import jax
import jax.numpy as jnp
from jax import lax
from jax.experimental import pallas as pl
from jax.experimental.pallas import tpu as pltpu
from jax.sharding import PartitionSpec as P

F32, BF16 = jnp.float32, jnp.bfloat16
SMEM = pl.BlockSpec(memory_space=pltpu.SMEM)
VMEM = pl.BlockSpec(memory_space=pltpu.VMEM)


def shifted(block, axis, distance):
    devices = range(lax.axis_size(axis))
    route = [(i - distance, i) for i in devices if i - distance in devices]
    return lax.ppermute(block, axis, route)


def ring_route(n):
    order = [0] + [i for i in range(n) if i % 2] + [i for i in reversed(range(1, n)) if i % 2 == 0]
    cores = lax.axis_size("sub")
    hops = [(order[i], order[(i + 1) % n]) for i in range(n)]
    return [(hop[core % 2] * cores + core, hop[1 - core % 2] * cores + core) for hop in hops for core in range(cores)]


def ring_place(n, steps_back):
    me = lax.axis_index("op")
    place = jnp.where(me == 0, 0, jnp.where(lax.rem(me, 2) == 1, (me + 1) // 2, n - me // 2))
    steps = jnp.where(lax.rem(lax.axis_index("sub"), 2) == 0, steps_back, -steps_back)
    at = lax.rem(place - steps + 2 * n, n)
    return jnp.where(at == 0, 0, jnp.where(at <= n // 2, 2 * at - 1, 2 * (n - at)))


def split(x):
    hi = x.astype(BF16)
    return hi, (x - hi.astype(F32)).astype(BF16)


def dot3(a, b):
    one = functools.partial(jnp.dot, preferred_element_type=F32)
    return one(a[0], b[0]) + (one(a[0], b[1]) + one(a[1], b[0]))


def prepare(left_ref, right_ref, left_parts, right_hi, right_lo, zero):
    n, kops, rows, _ = left_parts.shape
    width = left_ref.shape[1]
    zero[...] = jnp.zeros_like(zero)
    for k in range(kops):
        hi, lo = split(left_ref[k])
        parts = jnp.concatenate([hi, hi, lo], axis=1)
        for c in range(n):
            left_parts[c, k] = parts[c * rows : (c + 1) * rows]
        right_hi[k * width : (k + 1) * width, :], right_lo[k * width : (k + 1) * width, :] = split(right_ref[k].T)


def stacked(block):
    hi, lo = split(block)
    return jnp.concatenate([hi, lo, hi], axis=0)


def place_rows(n, target, blocks, way=1):
    for j, block in enumerate(blocks):
        rows = block.shape[-2]
        target[..., pl.ds(pl.multiple_of(ring_place(n, way * j) * rows, rows), rows), :] = block


def assemble(n, *refs):
    parts, psi = refs[n:]
    place_rows(n, psi, [ref[...] for ref in refs[:n]])
    for i in range(parts.shape[0]):
        parts[i] = stacked(psi[i])


def first_product(left, parts, allowed_ref, source, high, low):
    kops, sectors = allowed_ref.shape
    block = jnp.dot(left, parts, preferred_element_type=F32)
    rows = block.shape[0] // kops
    source = jnp.clip(source, 0, sectors - 1)
    for k in range(kops):
        at = slice(k * rows, (k + 1) * rows)
        high[at], low[at] = split(block[at] * allowed_ref[k, source].astype(F32))


def chunk_left(n, step, left_parts):
    return left_parts[ring_place(n, step + 1)].reshape(-1, left_parts.shape[-1])


def own_sectors(n, allowed_ref, *refs):
    (outer, left_parts), (inner, high, low, psi) = refs[n : n + 2], refs[n + 2 :]
    assemble(n, *refs[:n], inner, psi)
    left = chunk_left(n, 0, left_parts)
    nloc = high.shape[0]
    first = lax.axis_index(("sec", "sub")) * nloc
    sources = [outer.at[0], *[inner.at[i] for i in range(nloc - 2)], outer.at[1]]
    for i, ref in enumerate(sources):
        first_product(left, ref[...], allowed_ref, first + i, high.at[i], low.at[i])


def outside_sectors(n, nloc, allowed_ref, above, below, left_parts, outside, high, low, psi):
    place_rows(n, psi.at[0], [above[j] for j in range(n)], -1)
    place_rows(n, psi.at[1], [below[j] for j in range(n)], -1)
    left = chunk_left(n, 0, left_parts)
    first = lax.axis_index(("sec", "sub")) * nloc
    for i in range(2):
        outside[i] = stacked(psi[i])
        first_product(left, outside[i], allowed_ref, first - 1 + i * (nloc + 1), high.at[i], low.at[i])


def second_product(blocks_of, shifts_ref, high, low, right_hi, right_lo, out):
    rows, width = out.shape[1:]

    def left(parts):
        columns = []
        for k in range(shifts_ref.shape[0]):
            at = slice(k * rows, (k + 1) * rows)
            columns.append(jnp.concatenate(blocks_of(parts, shifts_ref[k], at)))
        return jnp.concatenate(columns, axis=1)

    out[...] = dot3((left(high), left(low)), (right_hi[...], right_lo[...])).reshape(out.shape)


def first_inner(nloc, shifts_ref, high, low, right_hi, right_lo, out):
    def blocks_of(own, shift, at):
        return [own[t - shift, at] for t in range(1, nloc - 1)]

    second_product(blocks_of, shifts_ref, high, low, right_hi, right_lo, out)


def first_outer(nloc, shifts_ref, high, low, end_high, end_low, right_hi, right_lo, out):
    def blocks_of(parts, shift, at):
        own, ends = parts
        start = jnp.where(shift == 1, ends[0, at], own[jnp.maximum(-shift, 0), at])
        end = jnp.where(shift == -1, ends[1, at], own[jnp.minimum(nloc - 1 - shift, nloc - 1), at])
        return [start, end]

    second_product(blocks_of, shifts_ref, (high, end_high), (low, end_low), right_hi, right_lo, out)


def later_chunk(n, nloc, step, shifts_ref, allowed_ref, outer, inner, outside, left_parts, right_hi, right_lo, outer_out, inner_out, high, low):
    left = chunk_left(n, step, left_parts)
    first = lax.axis_index(("sec", "sub")) * nloc
    sources = [outside.at[0], outer.at[0], *[inner.at[i] for i in range(nloc - 2)], outer.at[1], outside.at[1]]
    for i, ref in enumerate(sources):
        first_product(left, ref[...], allowed_ref, first - 1 + i, high.at[i], low.at[i])

    def inner_blocks(parts, shift, at):
        return [parts[t + 1 - shift, at] for t in range(1, nloc - 1)]

    def outer_blocks(parts, shift, at):
        return [parts[t + 1 - shift, at] for t in (0, nloc - 1)]

    second_product(inner_blocks, shifts_ref, high, low, right_hi, right_lo, inner_out)
    second_product(outer_blocks, shifts_ref, high, low, right_hi, right_lo, outer_out)


def call(body, name, flops, out_shape, in_specs, operands, scratch=()):
    return pl.pallas_call(
        body,
        name=name,
        out_shape=out_shape,
        in_specs=in_specs,
        out_specs=jax.tree.map(lambda _: VMEM, out_shape),
        scratch_shapes=list(scratch),
        compiler_params=pltpu.CompilerParams(vmem_limit_bytes=24 * 2**20),
        cost_estimate=pl.CostEstimate(flops=flops, bytes_accessed=2**20, transcendentals=0),
    )(*operands)


def shards(psi, left_ops, right_ops, shifts, allowed):
    nloc, rows, width = psi.shape
    kops = left_ops.shape[0]
    n = lax.axis_size("op")
    route = ring_route(n)
    one = 6 * width**3

    tall = jax.ShapeDtypeStruct((kops * width, width), BF16)
    parts = jax.ShapeDtypeStruct((n, kops, rows, 3 * width), BF16)
    zero = jax.ShapeDtypeStruct((1, 128), F32)
    left_parts, right_hi, right_lo, zero = call(
        prepare, "prepare", 4 * kops * one, [parts, tall, tall, zero], [VMEM] * 2, [left_ops, right_ops]
    )

    blocks = [psi, lax.ppermute(psi, ("op", "sub"), route)]
    outer, inner = [[b[:: nloc - 1] for b in blocks], [b[1 : nloc - 1] for b in blocks]]
    for step in range(1, n - 1):
        outer.append(lax.ppermute(outer[-1] + zero[0, 0] if step == 1 else outer[-1], ("op", "sub"), route))
        inner.append(lax.ppermute(inner[-1] + zero[0, 0] if step == 1 else inner[-1], ("op", "sub"), route))

    above = shifted(jnp.concatenate([b[1:] for b in outer]), ("sec", "sub"), 1)
    below = shifted(jnp.concatenate([b[:1] for b in outer]), ("sec", "sub"), -1)

    def split_parts(sectors):
        return jax.ShapeDtypeStruct((sectors, 3 * width, width), BF16)

    def whole(sectors):
        return [pltpu.VMEM((sectors, width, width), F32)]

    parts_outer = call(functools.partial(assemble, n), "assemble", 4 * kops * one, split_parts(2), [VMEM] * n, outer, whole(2))
    def products(sectors):
        return [jax.ShapeDtypeStruct((sectors, kops * rows, width), BF16)] * 2

    chunk = jax.ShapeDtypeStruct((2, rows, width), F32)
    chunk_inner = jax.ShapeDtypeStruct((nloc - 2, rows, width), F32)
    parts_inner, *own = call(
        functools.partial(own_sectors, n), "own", 4 * kops * one, [split_parts(nloc - 2), *products(nloc)],
        [SMEM] + [VMEM] * (n + 2), [allowed, *inner, parts_outer, left_parts], whole(nloc - 2),
    )
    result_inner = call(
        functools.partial(first_inner, nloc), "first_inner", nloc * kops * one // n, chunk_inner,
        [SMEM] + [VMEM] * 4, [shifts, *own, right_hi, right_lo],
    )
    parts_outside, *ends = call(
        functools.partial(outside_sectors, n, nloc), "outside", 2 * kops * one, [split_parts(2), *products(2)],
        [SMEM] + [VMEM] * 3, [allowed, above, below, left_parts], whole(2),
    )
    result_outer = call(
        functools.partial(first_outer, nloc), "first_outer", nloc * kops * one // n, chunk,
        [SMEM] + [VMEM] * 6, [shifts, *own, *ends, right_hi, right_lo],
    )

    def mine(step):
        return call(
            functools.partial(later_chunk, n, nloc, step), "chunk", 4 * nloc * kops * one // n, [chunk, chunk_inner],
            [SMEM] * 2 + [VMEM] * 6,
            [shifts, allowed, parts_outer, parts_inner, parts_outside, left_parts, right_hi, right_lo],
            [pltpu.VMEM((nloc + 2, kops * rows, width), BF16)] * 2,
        )

    for step in range(1, n):
        next_outer, next_inner = mine(step)
        result_inner = lax.ppermute(result_inner, ("op", "sub"), route) + next_inner
        result_outer = lax.ppermute(result_outer, ("op", "sub"), route) + next_outer
    return jnp.concatenate([result_outer[:1], result_inner, result_outer[1:]])


def solution(mesh):
    return jax.shard_map(
        shards,
        mesh=mesh,
        in_specs=(
            P(("parts", "sec", "sub"), "op", None),
            P("op", None, None),
            P("op", None, None),
            P("op"),
            P("op", None),
        ),
        out_specs=P(("parts", "sec", "sub"), "op", None),
        check_vma=False,
    )
```

```python
import functools

import jax
import jax.numpy as jnp
from jax import lax
from jax.experimental import pallas as pl
from jax.experimental.pallas import tpu as pltpu
from jax.sharding import PartitionSpec as P

F32, BF16 = jnp.float32, jnp.bfloat16
SMEM = pl.BlockSpec(memory_space=pltpu.SMEM)
VMEM = pl.BlockSpec(memory_space=pltpu.VMEM)


def shifted(block, axis, distance):
    devices = range(lax.axis_size(axis))
    route = [(i - distance, i) for i in devices if i - distance in devices]
    return lax.ppermute(block, axis, route)


def ring_route(n):
    order = [0] + [i for i in range(n) if i % 2] + [i for i in reversed(range(1, n)) if i % 2 == 0]
    return [(order[i], order[(i + 1) % n]) for i in range(n)]


def ring_place(n, steps_back):
    me = lax.axis_index("op")
    place = jnp.where(me == 0, 0, jnp.where(lax.rem(me, 2) == 1, (me + 1) // 2, n - me // 2))
    at = lax.rem(place - steps_back + 2 * n, n)
    return jnp.where(at == 0, 0, jnp.where(at <= n // 2, 2 * at - 1, 2 * (n - at)))


def split(x):
    hi = x.astype(BF16)
    return hi, (x - hi.astype(F32)).astype(BF16)


def dot3(a, b):
    one = functools.partial(jnp.dot, preferred_element_type=F32)
    return one(a[0], b[0]) + (one(a[0], b[1]) + one(a[1], b[0]))


def prepare(left_ref, right_ref, left_parts, right_hi, right_lo, zero):
    n, kops, rows, _ = left_parts.shape
    width = left_ref.shape[1]
    zero[...] = jnp.zeros_like(zero)
    for k in range(kops):
        hi, lo = split(left_ref[k])
        parts = jnp.concatenate([hi, hi, lo], axis=1)
        for c in range(n):
            left_parts[c, k] = parts[c * rows : (c + 1) * rows]
        right_hi[k * width : (k + 1) * width, :], right_lo[k * width : (k + 1) * width, :] = split(right_ref[k].T)


def stacked(block):
    hi, lo = split(block)
    return jnp.concatenate([hi, lo, hi], axis=0)


def place_rows(n, target, blocks):
    for j, block in enumerate(blocks):
        rows = block.shape[-2]
        target[..., pl.ds(pl.multiple_of(ring_place(n, j) * rows, rows), rows), :] = block


def assemble(n, *refs):
    parts, psi = refs[n:]
    place_rows(n, psi, [ref[...] for ref in refs[:n]])
    for i in range(parts.shape[0]):
        parts[i] = stacked(psi[i])


def first_product(left, parts, allowed_ref, source, high, low):
    kops, sectors = allowed_ref.shape
    block = jnp.dot(left, parts, preferred_element_type=F32)
    rows = block.shape[0] // kops
    source = jnp.clip(source, 0, sectors - 1)
    for k in range(kops):
        at = slice(k * rows, (k + 1) * rows)
        high[at], low[at] = split(block[at] * allowed_ref[k, source].astype(F32))


def chunk_left(n, step, left_parts):
    return left_parts[ring_place(n, step + 1)].reshape(-1, left_parts.shape[-1])


def own_sectors(n, allowed_ref, outer, *refs):
    left_parts, inner, high, low, psi = refs[n:]
    assemble(n, *refs[:n], inner, psi)
    left = chunk_left(n, 0, left_parts)
    nloc = high.shape[0]
    first = lax.axis_index(("sec", "sub")) * nloc
    sources = [outer.at[0], *[inner.at[i] for i in range(nloc - 2)], outer.at[1]]
    for i, ref in enumerate(sources):
        first_product(left, ref[...], allowed_ref, first + i, high.at[i], low.at[i])


def second_product(blocks_of, shifts_ref, high, low, right_hi, right_lo, out):
    rows, width = out.shape[1:]

    def left(parts):
        columns = []
        for k in range(shifts_ref.shape[0]):
            at = slice(k * rows, (k + 1) * rows)
            columns.append(jnp.concatenate(blocks_of(parts, shifts_ref[k], at)))
        return jnp.concatenate(columns, axis=1)

    out[...] = dot3((left(high), left(low)), (right_hi[...], right_lo[...])).reshape(out.shape)


def first_inner(nloc, shifts_ref, high, low, right_hi, right_lo, out):
    def blocks_of(own, shift, at):
        return [own[t - shift, at] for t in range(1, nloc - 1)]

    second_product(blocks_of, shifts_ref, high, low, right_hi, right_lo, out)


def first_outer(n, nloc, shifts_ref, allowed_ref, own_high, own_low, above, below, left_parts, right_hi, right_lo, *refs):
    out, outside, end_high, end_low, psi = refs
    place_rows(n, psi.at[0], [above[j] for j in range(n)])
    place_rows(n, psi.at[1], [below[j] for j in range(n)])
    left = chunk_left(n, 0, left_parts)
    first = lax.axis_index(("sec", "sub")) * nloc
    for i in range(2):
        outside[i] = stacked(psi[i])
        first_product(left, outside[i], allowed_ref, first - 1 + i * (nloc + 1), end_high.at[i], end_low.at[i])

    def blocks_of(parts, shift, at):
        own, ends = parts
        start = jnp.where(shift == 1, ends[0, at], own[jnp.maximum(-shift, 0), at])
        end = jnp.where(shift == -1, ends[1, at], own[jnp.minimum(nloc - 1 - shift, nloc - 1), at])
        return [start, end]

    second_product(blocks_of, shifts_ref, (own_high, end_high), (own_low, end_low), right_hi, right_lo, out)


def later_chunk(n, nloc, step, shifts_ref, allowed_ref, outer, inner, outside, left_parts, right_hi, right_lo, outer_out, inner_out, high, low):
    left = chunk_left(n, step, left_parts)
    first = lax.axis_index(("sec", "sub")) * nloc
    sources = [outside.at[0], outer.at[0], *[inner.at[i] for i in range(nloc - 2)], outer.at[1], outside.at[1]]
    for i, ref in enumerate(sources):
        first_product(left, ref[...], allowed_ref, first - 1 + i, high.at[i], low.at[i])

    def inner_blocks(parts, shift, at):
        return [parts[t + 1 - shift, at] for t in range(1, nloc - 1)]

    def outer_blocks(parts, shift, at):
        return [parts[t + 1 - shift, at] for t in (0, nloc - 1)]

    second_product(inner_blocks, shifts_ref, high, low, right_hi, right_lo, inner_out)
    second_product(outer_blocks, shifts_ref, high, low, right_hi, right_lo, outer_out)


def call(body, name, flops, out_shape, in_specs, operands, scratch=()):
    return pl.pallas_call(
        body,
        name=name,
        out_shape=out_shape,
        in_specs=in_specs,
        out_specs=jax.tree.map(lambda _: VMEM, out_shape),
        scratch_shapes=list(scratch),
        compiler_params=pltpu.CompilerParams(vmem_limit_bytes=24 * 2**20),
        cost_estimate=pl.CostEstimate(flops=flops, bytes_accessed=2**20, transcendentals=0),
    )(*operands)


def shards(psi, left_ops, right_ops, shifts, allowed):
    nloc, rows, width = psi.shape
    kops = left_ops.shape[0]
    n = lax.axis_size("op")
    route = ring_route(n)
    one = 6 * width**3

    tall = jax.ShapeDtypeStruct((kops * width, width), BF16)
    parts = jax.ShapeDtypeStruct((n, kops, rows, 3 * width), BF16)
    zero = jax.ShapeDtypeStruct((1, 128), F32)
    left_parts, right_hi, right_lo, zero = call(
        prepare, "prepare", 4 * kops * one, [parts, tall, tall, zero], [VMEM] * 2, [left_ops, right_ops]
    )

    blocks = [psi, lax.ppermute(psi, "op", route)]
    outer, inner = [[b[:: nloc - 1] for b in blocks], [b[1 : nloc - 1] for b in blocks]]
    for step in range(1, n - 1):
        outer.append(lax.ppermute(outer[-1] + zero[0, 0] if step == 1 else outer[-1], "op", route))
        inner.append(lax.ppermute(inner[-1] + zero[0, 0] if step == 1 else inner[-1], "op", route))

    above = shifted(jnp.concatenate([b[1:] for b in outer]), ("sec", "sub"), 1)
    below = shifted(jnp.concatenate([b[:1] for b in outer]), ("sec", "sub"), -1)

    def split_parts(sectors):
        return jax.ShapeDtypeStruct((sectors, 3 * width, width), BF16)

    def whole(sectors):
        return [pltpu.VMEM((sectors, width, width), F32)]

    parts_outer = call(functools.partial(assemble, n), "assemble", 4 * kops * one, split_parts(2), [VMEM] * n, outer, whole(2))
    def products(sectors):
        return [jax.ShapeDtypeStruct((sectors, kops * rows, width), BF16)] * 2

    chunk = jax.ShapeDtypeStruct((2, rows, width), F32)
    chunk_inner = jax.ShapeDtypeStruct((nloc - 2, rows, width), F32)
    parts_inner, *own = call(
        functools.partial(own_sectors, n), "own", 4 * kops * one, [split_parts(nloc - 2), *products(nloc)],
        [SMEM] + [VMEM] * (n + 2), [allowed, parts_outer, *inner, left_parts], whole(nloc - 2),
    )
    result_inner = call(
        functools.partial(first_inner, nloc), "first_inner", nloc * kops * one // n, chunk_inner,
        [SMEM] + [VMEM] * 4, [shifts, *own, right_hi, right_lo],
    )
    result_outer, parts_outside = call(
        functools.partial(first_outer, n, nloc), "first_outer", 2 * kops * one, [chunk, split_parts(2)],
        [SMEM] * 2 + [VMEM] * 7, [shifts, allowed, *own, above, below, left_parts, right_hi, right_lo],
        [pltpu.VMEM((2, kops * rows, width), BF16)] * 2 + whole(2),
    )

    def mine(step):
        return call(
            functools.partial(later_chunk, n, nloc, step), "chunk", 4 * nloc * kops * one // n, [chunk, chunk_inner],
            [SMEM] * 2 + [VMEM] * 6,
            [shifts, allowed, parts_outer, parts_inner, parts_outside, left_parts, right_hi, right_lo],
            [pltpu.VMEM((nloc + 2, kops * rows, width), BF16)] * 2,
        )

    for step in range(1, n):
        next_outer, next_inner = mine(step)
        result_inner = lax.ppermute(result_inner, "op", route) + next_inner
        result_outer = lax.ppermute(result_outer, "op", route) + next_outer
    return jnp.concatenate([result_outer[:1], result_inner, result_outer[1:]])


def solution(mesh):
    return jax.shard_map(
        shards,
        mesh=mesh,
        in_specs=(
            P(("parts", "sec", "sub"), "op", None),
            P("op", None, None),
            P("op", None, None),
            P("op"),
            P("op", None),
        ),
        out_specs=P(("parts", "sec", "sub"), "op", None),
        check_vma=False,
    )
```

```python
import functools

import jax
import jax.numpy as jnp
from jax import lax
from jax.experimental import pallas as pl
from jax.experimental.pallas import tpu as pltpu
from jax.sharding import PartitionSpec as P

F32, BF16 = jnp.float32, jnp.bfloat16
SMEM = pl.BlockSpec(memory_space=pltpu.SMEM)
VMEM = pl.BlockSpec(memory_space=pltpu.VMEM)


def shifted(block, axis, distance):
    devices = range(lax.axis_size(axis))
    route = [(i - distance, i) for i in devices if i - distance in devices]
    return lax.ppermute(block, axis, route)


def ring_route(n):
    order = [0] + [i for i in range(n) if i % 2] + [i for i in reversed(range(1, n)) if i % 2 == 0]
    return [(order[i], order[(i + 1) % n]) for i in range(n)]


def ring_place(n, steps_back):
    me = lax.axis_index("op")
    place = jnp.where(me == 0, 0, jnp.where(lax.rem(me, 2) == 1, (me + 1) // 2, n - me // 2))
    at = lax.rem(place - steps_back + 2 * n, n)
    return jnp.where(at == 0, 0, jnp.where(at <= n // 2, 2 * at - 1, 2 * (n - at)))


def split(x):
    hi = x.astype(BF16)
    return hi, (x - hi.astype(F32)).astype(BF16)


def dot3(a, b):
    one = functools.partial(jnp.dot, preferred_element_type=F32)
    return one(a[0], b[0]) + (one(a[0], b[1]) + one(a[1], b[0]))


def prepare(left_ref, right_ref, left_parts, right_hi, right_lo, zero):
    n, kops, rows, _ = left_parts.shape
    width = left_ref.shape[1]
    zero[...] = jnp.zeros_like(zero)
    for k in range(kops):
        hi, lo = split(left_ref[k])
        parts = jnp.concatenate([hi, hi, lo], axis=1)
        for c in range(n):
            left_parts[c, k] = parts[c * rows : (c + 1) * rows]
        right_hi[k * width : (k + 1) * width, :], right_lo[k * width : (k + 1) * width, :] = split(right_ref[k].T)


def stacked(block):
    hi, lo = split(block)
    return jnp.concatenate([hi, lo, hi], axis=0)


def place_rows(n, target, blocks):
    for j, block in enumerate(blocks):
        rows = block.shape[-2]
        target[..., pl.ds(pl.multiple_of(ring_place(n, j) * rows, rows), rows), :] = block


def assemble(n, *refs):
    parts, psi = refs[n:]
    place_rows(n, psi, [ref[...] for ref in refs[:n]])
    for i in range(parts.shape[0]):
        parts[i] = stacked(psi[i])


def first_product(left, parts, allowed_ref, source, high, low):
    kops, sectors = allowed_ref.shape
    rows = left.shape[0] // kops
    source = jnp.clip(source, 0, sectors - 1)
    some = max(kops // 2, 1)
    for start in range(0, kops, some):
        block = jnp.dot(left[start * rows : (start + some) * rows], parts, preferred_element_type=F32)
        for k in range(start, min(start + some, kops)):
            piece = block[(k - start) * rows : (k - start + 1) * rows]
            at = slice(k * rows, (k + 1) * rows)
            high[at], low[at] = split(piece * allowed_ref[k, source].astype(F32))


def chunk_left(n, step, left_parts):
    return left_parts[ring_place(n, step + 1)].reshape(-1, left_parts.shape[-1])


def own_sectors(n, allowed_ref, outer, *refs):
    left_parts, inner, high, low, psi = refs[n:]
    assemble(n, *refs[:n], inner, psi)
    left = chunk_left(n, 0, left_parts)
    nloc = high.shape[0]
    first = lax.axis_index(("sec", "sub")) * nloc
    sources = [outer.at[0], *[inner.at[i] for i in range(nloc - 2)], outer.at[1]]
    for i, ref in enumerate(sources):
        first_product(left, ref[...], allowed_ref, first + i, high.at[i], low.at[i])


def second_product(blocks_of, shifts_ref, high, low, right_hi, right_lo, out):
    rows, width = out.shape[1:]

    def left(parts):
        columns = []
        for k in range(shifts_ref.shape[0]):
            at = slice(k * rows, (k + 1) * rows)
            columns.append(jnp.concatenate(blocks_of(parts, shifts_ref[k], at)))
        return jnp.concatenate(columns, axis=1)

    out[...] = dot3((left(high), left(low)), (right_hi[...], right_lo[...])).reshape(out.shape)


def first_inner(nloc, shifts_ref, high, low, right_hi, right_lo, out):
    def blocks_of(own, shift, at):
        return [own[t - shift, at] for t in range(1, nloc - 1)]

    second_product(blocks_of, shifts_ref, high, low, right_hi, right_lo, out)


def first_outer(n, nloc, shifts_ref, allowed_ref, own_high, own_low, above, below, left_parts, right_hi, right_lo, *refs):
    out, outside, end_high, end_low, psi = refs
    place_rows(n, psi.at[0], [above[j] for j in range(n)])
    place_rows(n, psi.at[1], [below[j] for j in range(n)])
    left = chunk_left(n, 0, left_parts)
    first = lax.axis_index(("sec", "sub")) * nloc
    for i in range(2):
        outside[i] = stacked(psi[i])
        first_product(left, outside[i], allowed_ref, first - 1 + i * (nloc + 1), end_high.at[i], end_low.at[i])

    def blocks_of(parts, shift, at):
        own, ends = parts
        start = jnp.where(shift == 1, ends[0, at], own[jnp.maximum(-shift, 0), at])
        end = jnp.where(shift == -1, ends[1, at], own[jnp.minimum(nloc - 1 - shift, nloc - 1), at])
        return [start, end]

    second_product(blocks_of, shifts_ref, (own_high, end_high), (own_low, end_low), right_hi, right_lo, out)


def later_chunk(n, nloc, step, shifts_ref, allowed_ref, outer, inner, outside, left_parts, right_hi, right_lo, outer_out, inner_out, high, low):
    left = chunk_left(n, step, left_parts)
    first = lax.axis_index(("sec", "sub")) * nloc
    sources = [outside.at[0], outer.at[0], *[inner.at[i] for i in range(nloc - 2)], outer.at[1], outside.at[1]]
    for i, ref in enumerate(sources):
        first_product(left, ref[...], allowed_ref, first - 1 + i, high.at[i], low.at[i])

    def inner_blocks(parts, shift, at):
        return [parts[t + 1 - shift, at] for t in range(1, nloc - 1)]

    def outer_blocks(parts, shift, at):
        return [parts[t + 1 - shift, at] for t in (0, nloc - 1)]

    second_product(inner_blocks, shifts_ref, high, low, right_hi, right_lo, inner_out)
    second_product(outer_blocks, shifts_ref, high, low, right_hi, right_lo, outer_out)


def call(body, name, flops, out_shape, in_specs, operands, scratch=()):
    return pl.pallas_call(
        body,
        name=name,
        out_shape=out_shape,
        in_specs=in_specs,
        out_specs=jax.tree.map(lambda _: VMEM, out_shape),
        scratch_shapes=list(scratch),
        compiler_params=pltpu.CompilerParams(vmem_limit_bytes=24 * 2**20),
        cost_estimate=pl.CostEstimate(flops=flops, bytes_accessed=2**20, transcendentals=0),
    )(*operands)


def shards(psi, left_ops, right_ops, shifts, allowed):
    nloc, rows, width = psi.shape
    kops = left_ops.shape[0]
    n = lax.axis_size("op")
    route = ring_route(n)
    one = 6 * width**3

    tall = jax.ShapeDtypeStruct((kops * width, width), BF16)
    parts = jax.ShapeDtypeStruct((n, kops, rows, 3 * width), BF16)
    zero = jax.ShapeDtypeStruct((1, 128), F32)
    left_parts, right_hi, right_lo, zero = call(
        prepare, "prepare", 4 * kops * one, [parts, tall, tall, zero], [VMEM] * 2, [left_ops, right_ops]
    )

    blocks = [psi, lax.ppermute(psi, "op", route)]
    outer, inner = [[b[:: nloc - 1] for b in blocks], [b[1 : nloc - 1] for b in blocks]]
    for step in range(1, n - 1):
        outer.append(lax.ppermute(outer[-1] + zero[0, 0] if step == 1 else outer[-1], "op", route))
        inner.append(lax.ppermute(inner[-1] + zero[0, 0] if step == 1 else inner[-1], "op", route))

    above = shifted(jnp.concatenate([b[1:] for b in outer]), ("sec", "sub"), 1)
    below = shifted(jnp.concatenate([b[:1] for b in outer]), ("sec", "sub"), -1)

    def split_parts(sectors):
        return jax.ShapeDtypeStruct((sectors, 3 * width, width), BF16)

    def whole(sectors):
        return [pltpu.VMEM((sectors, width, width), F32)]

    parts_outer = call(functools.partial(assemble, n), "assemble", 4 * kops * one, split_parts(2), [VMEM] * n, outer, whole(2))
    def products(sectors):
        return [jax.ShapeDtypeStruct((sectors, kops * rows, width), BF16)] * 2

    chunk = jax.ShapeDtypeStruct((2, rows, width), F32)
    chunk_inner = jax.ShapeDtypeStruct((nloc - 2, rows, width), F32)
    parts_inner, *own = call(
        functools.partial(own_sectors, n), "own", 4 * kops * one, [split_parts(nloc - 2), *products(nloc)],
        [SMEM] + [VMEM] * (n + 2), [allowed, parts_outer, *inner, left_parts], whole(nloc - 2),
    )
    result_inner = call(
        functools.partial(first_inner, nloc), "first_inner", nloc * kops * one // n, chunk_inner,
        [SMEM] + [VMEM] * 4, [shifts, *own, right_hi, right_lo],
    )
    result_outer, parts_outside = call(
        functools.partial(first_outer, n, nloc), "first_outer", 2 * kops * one, [chunk, split_parts(2)],
        [SMEM] * 2 + [VMEM] * 7, [shifts, allowed, *own, above, below, left_parts, right_hi, right_lo],
        [pltpu.VMEM((2, kops * rows, width), BF16)] * 2 + whole(2),
    )

    def mine(step):
        return call(
            functools.partial(later_chunk, n, nloc, step), "chunk", 4 * nloc * kops * one // n, [chunk, chunk_inner],
            [SMEM] * 2 + [VMEM] * 6,
            [shifts, allowed, parts_outer, parts_inner, parts_outside, left_parts, right_hi, right_lo],
            [pltpu.VMEM((nloc + 2, kops * rows, width), BF16)] * 2,
        )

    for step in range(1, n):
        next_outer, next_inner = mine(step)
        result_inner = lax.ppermute(result_inner, "op", route) + next_inner
        result_outer = lax.ppermute(result_outer, "op", route) + next_outer
    return jnp.concatenate([result_outer[:1], result_inner, result_outer[1:]])


def solution(mesh):
    return jax.shard_map(
        shards,
        mesh=mesh,
        in_specs=(
            P(("parts", "sec", "sub"), "op", None),
            P("op", None, None),
            P("op", None, None),
            P("op"),
            P("op", None),
        ),
        out_specs=P(("parts", "sec", "sub"), "op", None),
        check_vma=False,
    )
```

```python
import functools

import jax
import jax.numpy as jnp
from jax import lax
from jax.experimental import pallas as pl
from jax.experimental.pallas import tpu as pltpu
from jax.sharding import PartitionSpec as P

F32, BF16 = jnp.float32, jnp.bfloat16
SMEM = pl.BlockSpec(memory_space=pltpu.SMEM)
VMEM = pl.BlockSpec(memory_space=pltpu.VMEM)


def sector_group():
    return lax.axis_index(("sec", "sub"))


def swapped(block, odd):
    groups = lax.axis_size(("sec", "sub"))
    pairs = [(i, i + 1) for i in range(odd, groups - 1, 2)]
    return lax.ppermute(block, ("sec", "sub"), pairs + [(j, i) for i, j in pairs])


def ring_route(n):
    order = [0] + [i for i in range(n) if i % 2] + [i for i in reversed(range(1, n)) if i % 2 == 0]
    return [(order[i], order[(i + 1) % n]) for i in range(n)]


def ring_place(n, steps_back):
    me = lax.axis_index("op")
    place = jnp.where(me == 0, 0, jnp.where(lax.rem(me, 2) == 1, (me + 1) // 2, n - me // 2))
    at = lax.rem(place - steps_back + 2 * n, n)
    return jnp.where(at == 0, 0, jnp.where(at <= n // 2, 2 * at - 1, 2 * (n - at)))


def split(x):
    hi = x.astype(BF16)
    return hi, (x - hi.astype(F32)).astype(BF16)


def dot3(a, b):
    one = functools.partial(jnp.dot, preferred_element_type=F32)
    return one(a[0], b[0]) + (one(a[0], b[1]) + one(a[1], b[0]))


def prepare(left_ref, right_ref, left_parts, right_hi, right_lo, zero):
    n, kops, rows, _ = left_parts.shape
    width = left_ref.shape[1]
    zero[...] = jnp.zeros_like(zero)
    for k in range(kops):
        hi, lo = split(left_ref[k])
        parts = jnp.concatenate([hi, hi, lo], axis=1)
        for c in range(n):
            left_parts[c, k] = parts[c * rows : (c + 1) * rows]
        right_hi[k * width : (k + 1) * width, :], right_lo[k * width : (k + 1) * width, :] = split(right_ref[k].T)


def stacked(block):
    hi, lo = split(block)
    return jnp.concatenate([hi, lo, hi], axis=0)


def place_rows(n, target, blocks):
    for j, block in enumerate(blocks):
        rows = block.shape[-2]
        target[..., pl.ds(pl.multiple_of(ring_place(n, j) * rows, rows), rows), :] = block


def assemble(n, *refs):
    parts, psi = refs[n:]
    place_rows(n, psi, [ref[...] for ref in refs[:n]])
    for i in range(parts.shape[0]):
        parts[i] = stacked(psi[i])


def first_product(left, parts, allowed_ref, source, high, low):
    kops, sectors = allowed_ref.shape
    block = jnp.dot(left, parts, preferred_element_type=F32)
    rows = block.shape[0] // kops
    source = jnp.clip(source, 0, sectors - 1)
    for k in range(kops):
        at = slice(k * rows, (k + 1) * rows)
        high[at], low[at] = split(block[at] * allowed_ref[k, source].astype(F32))


def chunk_left(n, step, left_parts):
    return left_parts[ring_place(n, step + 1)].reshape(-1, left_parts.shape[-1])


def own_sectors(n, allowed_ref, *refs):
    (outer, left_parts), (inner, high, low, psi) = refs[n : n + 2], refs[n + 2 :]
    assemble(n, *refs[:n], inner, psi)
    left = chunk_left(n, 0, left_parts)
    nloc = high.shape[0]
    first = sector_group() * nloc
    sources = [outer.at[0], *[inner.at[i] for i in range(nloc - 2)], outer.at[1]]
    for i, ref in enumerate(sources):
        first_product(left, ref[...], allowed_ref, first + i, high.at[i], low.at[i])


def second_product(blocks_of, shifts_ref, high, low, right_hi, right_lo, out):
    rows, width = out.shape[1:]

    def left(parts):
        columns = []
        for k in range(shifts_ref.shape[0]):
            at = slice(k * rows, (k + 1) * rows)
            columns.append(jnp.concatenate(blocks_of(parts, shifts_ref[k], at)))
        return jnp.concatenate(columns, axis=1)

    out[...] = dot3((left(high), left(low)), (right_hi[...], right_lo[...])).reshape(out.shape)


def first_chunk(n, nloc, shifts_ref, allowed_ref, own_high, own_low, paired, apart, left_parts, right_hi, right_lo, *refs):
    outer_out, inner_out, outside, end_high, end_low, psi = refs
    odd = lax.rem(sector_group(), 2)
    place_rows(n, psi.at[odd], [apart[j] for j in range(n)])
    place_rows(n, psi.at[1 - odd], [paired[j] for j in range(n)])
    left = chunk_left(n, 0, left_parts)
    first = sector_group() * nloc
    for i in range(2):
        outside[i] = stacked(psi[i])
        first_product(left, outside[i], allowed_ref, first - 1 + i * (nloc + 1), end_high.at[i], end_low.at[i])

    def inner_blocks(parts, shift, at):
        return [parts[0][t - shift, at] for t in range(1, nloc - 1)]

    def outer_blocks(parts, shift, at):
        own, ends = parts
        start = jnp.where(shift == 1, ends[0, at], own[jnp.maximum(-shift, 0), at])
        end = jnp.where(shift == -1, ends[1, at], own[jnp.minimum(nloc - 1 - shift, nloc - 1), at])
        return [start, end]

    high, low = (own_high, end_high), (own_low, end_low)
    second_product(inner_blocks, shifts_ref, high, low, right_hi, right_lo, inner_out)
    second_product(outer_blocks, shifts_ref, high, low, right_hi, right_lo, outer_out)


def later_chunk(n, nloc, step, shifts_ref, allowed_ref, outer, inner, outside, left_parts, right_hi, right_lo, *refs):
    outer_out, inner_out, high, low = refs[-4:]
    left = chunk_left(n, step, left_parts)
    first = sector_group() * nloc
    sources = [outside.at[0], outer.at[0], *[inner.at[i] for i in range(nloc - 2)], outer.at[1], outside.at[1]]
    for i, ref in enumerate(sources):
        first_product(left, ref[...], allowed_ref, first - 1 + i, high.at[i], low.at[i])

    def inner_blocks(parts, shift, at):
        return [parts[t + 1 - shift, at] for t in range(1, nloc - 1)]

    def outer_blocks(parts, shift, at):
        return [parts[t + 1 - shift, at] for t in (0, nloc - 1)]

    second_product(inner_blocks, shifts_ref, high, low, right_hi, right_lo, inner_out)
    second_product(outer_blocks, shifts_ref, high, low, right_hi, right_lo, outer_out)


def call(body, name, flops, out_shape, in_specs, operands, scratch=()):
    return pl.pallas_call(
        body,
        name=name,
        out_shape=out_shape,
        in_specs=in_specs,
        out_specs=jax.tree.map(lambda _: VMEM, out_shape),
        scratch_shapes=list(scratch),
        compiler_params=pltpu.CompilerParams(vmem_limit_bytes=24 * 2**20),
        cost_estimate=pl.CostEstimate(flops=flops, bytes_accessed=2**20, transcendentals=0),
    )(*operands)


def shards(psi, left_ops, right_ops, shifts, allowed):
    nloc, rows, width = psi.shape
    kops = left_ops.shape[0]
    n = lax.axis_size("op")
    route = ring_route(n)
    one = 6 * width**3

    tall = jax.ShapeDtypeStruct((kops * width, width), BF16)
    parts = jax.ShapeDtypeStruct((n, kops, rows, 3 * width), BF16)
    zero = jax.ShapeDtypeStruct((1, 128), F32)
    left_parts, right_hi, right_lo, zero = call(
        prepare, "prepare", 4 * kops * one, [parts, tall, tall, zero], [VMEM] * 2, [left_ops, right_ops]
    )

    blocks = [psi, lax.ppermute(psi, "op", route)]
    outer, inner = [[b[:: nloc - 1] for b in blocks], [b[1 : nloc - 1] for b in blocks]]
    for step in range(1, n - 1):
        outer.append(lax.ppermute(outer[-1] + zero[0, 0] if step == 1 else outer[-1], "op", route))
        inner.append(lax.ppermute(inner[-1] + zero[0, 0] if step == 1 else inner[-1], "op", route))

    even = lax.rem(sector_group(), 2) == 0
    first_sector, last_sector = jnp.concatenate([b[:1] for b in outer]), jnp.concatenate([b[1:] for b in outer])
    apart = swapped(jnp.where(even, first_sector, last_sector), 1)
    paired = swapped(jnp.where(even, last_sector, first_sector), 0)

    def split_parts(sectors):
        return jax.ShapeDtypeStruct((sectors, 3 * width, width), BF16)

    def whole(sectors):
        return [pltpu.VMEM((sectors, width, width), F32)]

    parts_outer = call(functools.partial(assemble, n), "assemble", 4 * kops * one, split_parts(2), [VMEM] * n, outer, whole(2))
    def products(sectors):
        return [jax.ShapeDtypeStruct((sectors, kops * rows, width), BF16)] * 2

    chunk = jax.ShapeDtypeStruct((2, rows, width), F32)
    chunk_inner = jax.ShapeDtypeStruct((nloc - 2, rows, width), F32)
    parts_inner, *own = call(
        functools.partial(own_sectors, n), "own", 4 * kops * one, [split_parts(nloc - 2), *products(nloc)],
        [SMEM] + [VMEM] * (n + 2), [allowed, *inner, parts_outer, left_parts], whole(nloc - 2),
    )
    result_outer, result_inner, parts_outside = call(
        functools.partial(first_chunk, n, nloc), "first_chunk", 2 * kops * one, [chunk, chunk_inner, split_parts(2)],
        [SMEM] * 2 + [VMEM] * 7, [shifts, allowed, *own, paired, apart, left_parts, right_hi, right_lo],
        [pltpu.VMEM((2, kops * rows, width), BF16)] * 2 + whole(2),
    )

    def mine(step, *before):
        return call(
            functools.partial(later_chunk, n, nloc, step), "chunk", 4 * nloc * kops * one // n, [chunk, chunk_inner],
            [SMEM] * 2 + [VMEM] * 6 + [pl.BlockSpec(memory_space=pl.ANY)] * len(before),
            [shifts, allowed, parts_outer, parts_inner, parts_outside, left_parts, right_hi, right_lo, *before],
            [pltpu.VMEM((nloc + 2, kops * rows, width), BF16)] * 2,
        )

    result_outer = result_outer + 0 * result_inner[:1]
    for step in range(1, n):
        moved_outer, moved_inner = lax.ppermute(result_outer, "op", route), lax.ppermute(result_inner, "op", route)
        before = [] if step < n - 1 else [result_outer, result_inner]
        next_outer, next_inner = mine(step, *before)
        result_outer, result_inner = moved_outer + next_outer, moved_inner + next_inner
    return jnp.concatenate([result_outer[:1], result_inner, result_outer[1:]])


def solution(mesh):
    return jax.shard_map(
        shards,
        mesh=mesh,
        in_specs=(
            P(("parts", "sec", "sub"), "op", None),
            P("op", None, None),
            P("op", None, None),
            P("op"),
            P("op", None),
        ),
        out_specs=P(("parts", "sec", "sub"), "op", None),
        check_vma=False,
    )
```

```python
import functools

import jax
import jax.numpy as jnp
from jax import lax
from jax.experimental import pallas as pl
from jax.experimental.pallas import tpu as pltpu
from jax.sharding import PartitionSpec as P

F32, BF16 = jnp.float32, jnp.bfloat16
SMEM = pl.BlockSpec(memory_space=pltpu.SMEM)
VMEM = pl.BlockSpec(memory_space=pltpu.VMEM)


def shifted(block, axis, distance):
    devices = range(lax.axis_size(axis))
    route = [(i - distance, i) for i in devices if i - distance in devices]
    return lax.ppermute(block, axis, route)


def ring_route(n):
    order = [0] + [i for i in range(n) if i % 2] + [i for i in reversed(range(1, n)) if i % 2 == 0]
    return [(order[i], order[(i + 1) % n]) for i in range(n)]


def ring_place(n, steps_back):
    me = lax.axis_index("op")
    place = jnp.where(me == 0, 0, jnp.where(lax.rem(me, 2) == 1, (me + 1) // 2, n - me // 2))
    at = lax.rem(place - steps_back + 2 * n, n)
    return jnp.where(at == 0, 0, jnp.where(at <= n // 2, 2 * at - 1, 2 * (n - at)))


def split(x):
    hi = x.astype(BF16)
    return hi, (x - hi.astype(F32)).astype(BF16)


def dot3(a, b):
    one = functools.partial(jnp.dot, preferred_element_type=F32)
    return one(a[0], b[0]) + (one(a[0], b[1]) + one(a[1], b[0]))


def prepare(left_ref, right_ref, left_parts, right_hi, right_lo, zero):
    n, kops, rows, _ = left_parts.shape
    width = left_ref.shape[1]
    zero[...] = jnp.zeros_like(zero)
    for k in range(kops):
        hi, lo = split(left_ref[k])
        parts = jnp.concatenate([hi, hi, lo], axis=1)
        for c in range(n):
            left_parts[c, k] = parts[c * rows : (c + 1) * rows]
        right_hi[k * width : (k + 1) * width, :], right_lo[k * width : (k + 1) * width, :] = split(right_ref[k].T)


def stacked(block):
    hi, lo = split(block)
    return jnp.concatenate([hi, lo, hi], axis=0)


def place_rows(n, target, blocks):
    for j, block in enumerate(blocks):
        rows = block.shape[-2]
        target[..., pl.ds(pl.multiple_of(ring_place(n, j) * rows, rows), rows), :] = block


def assemble(n, *refs):
    parts, psi = refs[n:]
    place_rows(n, psi, [ref[...] for ref in refs[:n]])
    for i in range(parts.shape[0]):
        parts[i] = stacked(psi[i])


def first_product(left, parts, allowed_ref, source, high, low):
    kops, sectors = allowed_ref.shape
    block = jnp.dot(left, parts, preferred_element_type=F32)
    rows = block.shape[0] // kops
    source = jnp.clip(source, 0, sectors - 1)
    for k in range(kops):
        at = slice(k * rows, (k + 1) * rows)
        high[at], low[at] = split(block[at] * allowed_ref[k, source].astype(F32))


def chunk_left(n, step, left_parts):
    return left_parts[ring_place(n, step + 1)].reshape(-1, left_parts.shape[-1])


def own_sectors(n, shifts_ref, allowed_ref, *refs):
    (outer, left_parts, right_hi, right_lo), (inner, high, low, out, psi) = refs[n : n + 4], refs[n + 4 :]
    assemble(n, *refs[:n], inner, psi)
    left = chunk_left(n, 0, left_parts)
    nloc = high.shape[0]
    first = lax.axis_index(("sec", "sub")) * nloc
    sources = [outer.at[0], *[inner.at[i] for i in range(nloc - 2)], outer.at[1]]
    for i, ref in enumerate(sources):
        first_product(left, ref[...], allowed_ref, first + i, high.at[i], low.at[i])

    def blocks_of(own, shift, at):
        return [own[t - shift, at] for t in range(1, nloc - 1)]

    second_product(blocks_of, shifts_ref, high, low, right_hi, right_lo, out)


def second_product(blocks_of, shifts_ref, high, low, right_hi, right_lo, out):
    rows, width = out.shape[1:]

    def left(parts):
        columns = []
        for k in range(shifts_ref.shape[0]):
            at = slice(k * rows, (k + 1) * rows)
            columns.append(jnp.concatenate(blocks_of(parts, shifts_ref[k], at)))
        return jnp.concatenate(columns, axis=1)

    out[...] = dot3((left(high), left(low)), (right_hi[...], right_lo[...])).reshape(out.shape)


def first_outer(n, nloc, shifts_ref, allowed_ref, own_high, own_low, above, below, left_parts, right_hi, right_lo, *refs):
    out, outside, end_high, end_low, psi = refs
    place_rows(n, psi.at[0], [above[j] for j in range(n)])
    place_rows(n, psi.at[1], [below[j] for j in range(n)])
    left = chunk_left(n, 0, left_parts)
    first = lax.axis_index(("sec", "sub")) * nloc
    for i in range(2):
        outside[i] = stacked(psi[i])
        first_product(left, outside[i], allowed_ref, first - 1 + i * (nloc + 1), end_high.at[i], end_low.at[i])

    def blocks_of(parts, shift, at):
        own, ends = parts
        start = jnp.where(shift == 1, ends[0, at], own[jnp.maximum(-shift, 0), at])
        end = jnp.where(shift == -1, ends[1, at], own[jnp.minimum(nloc - 1 - shift, nloc - 1), at])
        return [start, end]

    second_product(blocks_of, shifts_ref, (own_high, end_high), (own_low, end_low), right_hi, right_lo, out)


def later_chunk(n, nloc, step, shifts_ref, allowed_ref, outer, inner, outside, left_parts, right_hi, right_lo, outer_out, inner_out, high, low):
    left = chunk_left(n, step, left_parts)
    first = lax.axis_index(("sec", "sub")) * nloc
    sources = [outside.at[0], outer.at[0], *[inner.at[i] for i in range(nloc - 2)], outer.at[1], outside.at[1]]
    for i, ref in enumerate(sources):
        first_product(left, ref[...], allowed_ref, first - 1 + i, high.at[i], low.at[i])

    def inner_blocks(parts, shift, at):
        return [parts[t + 1 - shift, at] for t in range(1, nloc - 1)]

    def outer_blocks(parts, shift, at):
        return [parts[t + 1 - shift, at] for t in (0, nloc - 1)]

    second_product(inner_blocks, shifts_ref, high, low, right_hi, right_lo, inner_out)
    second_product(outer_blocks, shifts_ref, high, low, right_hi, right_lo, outer_out)


def call(body, name, flops, out_shape, in_specs, operands, scratch=()):
    return pl.pallas_call(
        body,
        name=name,
        out_shape=out_shape,
        in_specs=in_specs,
        out_specs=jax.tree.map(lambda _: VMEM, out_shape),
        scratch_shapes=list(scratch),
        compiler_params=pltpu.CompilerParams(vmem_limit_bytes=24 * 2**20),
        cost_estimate=pl.CostEstimate(flops=flops, bytes_accessed=2**20, transcendentals=0),
    )(*operands)


def shards(psi, left_ops, right_ops, shifts, allowed):
    nloc, rows, width = psi.shape
    kops = left_ops.shape[0]
    n = lax.axis_size("op")
    route = ring_route(n)
    one = 6 * width**3

    tall = jax.ShapeDtypeStruct((kops * width, width), BF16)
    parts = jax.ShapeDtypeStruct((n, kops, rows, 3 * width), BF16)
    zero = jax.ShapeDtypeStruct((1, 128), F32)
    left_parts, right_hi, right_lo, zero = call(
        prepare, "prepare", 4 * kops * one, [parts, tall, tall, zero], [VMEM] * 2, [left_ops, right_ops]
    )

    blocks = [psi, lax.ppermute(psi, "op", route)]
    outer, inner = [[b[:: nloc - 1] for b in blocks], [b[1 : nloc - 1] for b in blocks]]
    for step in range(1, n - 1):
        outer.append(lax.ppermute(outer[-1] + zero[0, 0] if step == 1 else outer[-1], "op", route))
        inner.append(lax.ppermute(inner[-1] + zero[0, 0] if step == 1 else inner[-1], "op", route))

    above = shifted(jnp.concatenate([b[1:] for b in outer]), ("sec", "sub"), 1)
    below = shifted(jnp.concatenate([b[:1] for b in outer]), ("sec", "sub"), -1)

    def split_parts(sectors):
        return jax.ShapeDtypeStruct((sectors, 3 * width, width), BF16)

    def whole(sectors):
        return [pltpu.VMEM((sectors, width, width), F32)]

    parts_outer = call(functools.partial(assemble, n), "assemble", 4 * kops * one, split_parts(2), [VMEM] * n, outer, whole(2))
    def products(sectors):
        return [jax.ShapeDtypeStruct((sectors, kops * rows, width), BF16)] * 2

    chunk = jax.ShapeDtypeStruct((2, rows, width), F32)
    chunk_inner = jax.ShapeDtypeStruct((nloc - 2, rows, width), F32)
    parts_inner, *own, result_inner = call(
        functools.partial(own_sectors, n), "own", 4 * kops * one, [split_parts(nloc - 2), *products(nloc), chunk_inner],
        [SMEM] * 2 + [VMEM] * (n + 4), [shifts, allowed, *inner, parts_outer, left_parts, right_hi, right_lo], whole(nloc - 2),
    )
    result_outer, parts_outside = call(
        functools.partial(first_outer, n, nloc), "first_outer", 2 * kops * one, [chunk, split_parts(2)],
        [SMEM] * 2 + [VMEM] * 7, [shifts, allowed, *own, above, below, left_parts, right_hi, right_lo],
        [pltpu.VMEM((2, kops * rows, width), BF16)] * 2 + whole(2),
    )

    def mine(step):
        return call(
            functools.partial(later_chunk, n, nloc, step), "chunk", 4 * nloc * kops * one // n, [chunk, chunk_inner],
            [SMEM] * 2 + [VMEM] * 6,
            [shifts, allowed, parts_outer, parts_inner, parts_outside, left_parts, right_hi, right_lo],
            [pltpu.VMEM((nloc + 2, kops * rows, width), BF16)] * 2,
        )

    for step in range(1, n):
        next_outer, next_inner = mine(step)
        result_inner = lax.ppermute(result_inner, "op", route) + next_inner
        result_outer = lax.ppermute(result_outer, "op", route) + next_outer
    return jnp.concatenate([result_outer[:1], result_inner, result_outer[1:]])


def solution(mesh):
    return jax.shard_map(
        shards,
        mesh=mesh,
        in_specs=(
            P(("parts", "sec", "sub"), "op", None),
            P("op", None, None),
            P("op", None, None),
            P("op"),
            P("op", None),
        ),
        out_specs=P(("parts", "sec", "sub"), "op", None),
        check_vma=False,
    )
```

```python
import functools

import jax
import jax.numpy as jnp
from jax import lax
from jax.experimental import pallas as pl
from jax.experimental.pallas import tpu as pltpu
from jax.sharding import PartitionSpec as P

F32, BF16 = jnp.float32, jnp.bfloat16
SMEM = pl.BlockSpec(memory_space=pltpu.SMEM)
VMEM = pl.BlockSpec(memory_space=pltpu.VMEM)


def shifted(block, axis, distance):
    devices = range(lax.axis_size(axis))
    route = [(i - distance, i) for i in devices if i - distance in devices]
    return lax.ppermute(block, axis, route)


def ring_route(n):
    order = [0] + [i for i in range(n) if i % 2] + [i for i in reversed(range(1, n)) if i % 2 == 0]
    return [(order[i], order[(i + 1) % n]) for i in range(n)]


def ring_place(n, steps_back):
    me = lax.axis_index("op")
    place = jnp.where(me == 0, 0, jnp.where(lax.rem(me, 2) == 1, (me + 1) // 2, n - me // 2))
    at = lax.rem(place - steps_back + 2 * n, n)
    return jnp.where(at == 0, 0, jnp.where(at <= n // 2, 2 * at - 1, 2 * (n - at)))


def split(x):
    hi = x.astype(BF16)
    return hi, (x - hi.astype(F32)).astype(BF16)


def dot3(a, b):
    one = functools.partial(jnp.dot, preferred_element_type=F32)
    return one(a[0], b[0]) + (one(a[0], b[1]) + one(a[1], b[0]))


def prepare(left_ref, right_ref, left_parts, right_hi, right_lo, zero):
    n, kops, rows, _ = left_parts.shape
    width = left_ref.shape[1]
    zero[...] = jnp.zeros_like(zero)
    for k in range(kops):
        hi, lo = split(left_ref[k])
        parts = jnp.concatenate([hi, hi, lo], axis=1)
        for c in range(n):
            left_parts[c, k] = parts[c * rows : (c + 1) * rows]
        right_hi[k * width : (k + 1) * width, :], right_lo[k * width : (k + 1) * width, :] = split(right_ref[k].T)


def stacked(block):
    hi, lo = split(block)
    return jnp.concatenate([hi, lo, hi], axis=0)


def place_rows(n, target, blocks):
    for j, block in enumerate(blocks):
        rows = block.shape[-2]
        target[..., pl.ds(pl.multiple_of(ring_place(n, j) * rows, rows), rows), :] = block


def assemble(n, *refs):
    parts, psi = refs[n:]
    place_rows(n, psi, [ref[...] for ref in refs[:n]])
    for i in range(parts.shape[0]):
        parts[i] = stacked(psi[i])


def first_product(left, parts, allowed_ref, source, high, low):
    kops, sectors = allowed_ref.shape
    cut = 2 * parts.shape[0] // 3
    block = jnp.dot(left[:, :cut], parts[:cut], preferred_element_type=F32)
    block = block + jnp.dot(left[:, cut:], parts[cut:], preferred_element_type=F32)
    rows = block.shape[0] // kops
    source = jnp.clip(source, 0, sectors - 1)
    for k in range(kops):
        at = slice(k * rows, (k + 1) * rows)
        high[at], low[at] = split(block[at] * allowed_ref[k, source].astype(F32))


def chunk_left(n, step, left_parts):
    return left_parts[ring_place(n, step + 1)].reshape(-1, left_parts.shape[-1])


def own_sectors(n, allowed_ref, outer, *refs):
    left_parts, inner, high, low, psi = refs[n:]
    assemble(n, *refs[:n], inner, psi)
    left = chunk_left(n, 0, left_parts)
    nloc = high.shape[0]
    first = lax.axis_index(("sec", "sub")) * nloc
    sources = [outer.at[0], *[inner.at[i] for i in range(nloc - 2)], outer.at[1]]
    for i, ref in enumerate(sources):
        first_product(left, ref[...], allowed_ref, first + i, high.at[i], low.at[i])


def second_product(blocks_of, shifts_ref, high, low, right_hi, right_lo, out):
    rows, width = out.shape[1:]

    def left(parts):
        columns = []
        for k in range(shifts_ref.shape[0]):
            at = slice(k * rows, (k + 1) * rows)
            columns.append(jnp.concatenate(blocks_of(parts, shifts_ref[k], at)))
        return jnp.concatenate(columns, axis=1)

    out[...] = dot3((left(high), left(low)), (right_hi[...], right_lo[...])).reshape(out.shape)


def first_inner(nloc, shifts_ref, high, low, right_hi, right_lo, out):
    def blocks_of(own, shift, at):
        return [own[t - shift, at] for t in range(1, nloc - 1)]

    second_product(blocks_of, shifts_ref, high, low, right_hi, right_lo, out)


def first_outer(n, nloc, shifts_ref, allowed_ref, own_high, own_low, above, below, left_parts, right_hi, right_lo, *refs):
    out, outside, end_high, end_low, psi = refs
    place_rows(n, psi.at[0], [above[j] for j in range(n)])
    place_rows(n, psi.at[1], [below[j] for j in range(n)])
    left = chunk_left(n, 0, left_parts)
    first = lax.axis_index(("sec", "sub")) * nloc
    for i in range(2):
        outside[i] = stacked(psi[i])
        first_product(left, outside[i], allowed_ref, first - 1 + i * (nloc + 1), end_high.at[i], end_low.at[i])

    def blocks_of(parts, shift, at):
        own, ends = parts
        start = jnp.where(shift == 1, ends[0, at], own[jnp.maximum(-shift, 0), at])
        end = jnp.where(shift == -1, ends[1, at], own[jnp.minimum(nloc - 1 - shift, nloc - 1), at])
        return [start, end]

    second_product(blocks_of, shifts_ref, (own_high, end_high), (own_low, end_low), right_hi, right_lo, out)


def later_chunk(n, nloc, step, shifts_ref, allowed_ref, outer, inner, outside, left_parts, right_hi, right_lo, outer_out, inner_out, high, low):
    left = chunk_left(n, step, left_parts)
    first = lax.axis_index(("sec", "sub")) * nloc
    sources = [outside.at[0], outer.at[0], *[inner.at[i] for i in range(nloc - 2)], outer.at[1], outside.at[1]]
    for i, ref in enumerate(sources):
        first_product(left, ref[...], allowed_ref, first - 1 + i, high.at[i], low.at[i])

    def inner_blocks(parts, shift, at):
        return [parts[t + 1 - shift, at] for t in range(1, nloc - 1)]

    def outer_blocks(parts, shift, at):
        return [parts[t + 1 - shift, at] for t in (0, nloc - 1)]

    second_product(inner_blocks, shifts_ref, high, low, right_hi, right_lo, inner_out)
    second_product(outer_blocks, shifts_ref, high, low, right_hi, right_lo, outer_out)


def call(body, name, flops, out_shape, in_specs, operands, scratch=()):
    return pl.pallas_call(
        body,
        name=name,
        out_shape=out_shape,
        in_specs=in_specs,
        out_specs=jax.tree.map(lambda _: VMEM, out_shape),
        scratch_shapes=list(scratch),
        compiler_params=pltpu.CompilerParams(vmem_limit_bytes=24 * 2**20),
        cost_estimate=pl.CostEstimate(flops=flops, bytes_accessed=2**20, transcendentals=0),
    )(*operands)


def shards(psi, left_ops, right_ops, shifts, allowed):
    nloc, rows, width = psi.shape
    kops = left_ops.shape[0]
    n = lax.axis_size("op")
    route = ring_route(n)
    one = 6 * width**3

    tall = jax.ShapeDtypeStruct((kops * width, width), BF16)
    parts = jax.ShapeDtypeStruct((n, kops, rows, 3 * width), BF16)
    zero = jax.ShapeDtypeStruct((1, 128), F32)
    left_parts, right_hi, right_lo, zero = call(
        prepare, "prepare", 4 * kops * one, [parts, tall, tall, zero], [VMEM] * 2, [left_ops, right_ops]
    )

    blocks = [psi, lax.ppermute(psi, "op", route)]
    outer, inner = [[b[:: nloc - 1] for b in blocks], [b[1 : nloc - 1] for b in blocks]]
    for step in range(1, n - 1):
        outer.append(lax.ppermute(outer[-1] + zero[0, 0] if step == 1 else outer[-1], "op", route))
        inner.append(lax.ppermute(inner[-1] + zero[0, 0] if step == 1 else inner[-1], "op", route))

    above = shifted(jnp.concatenate([b[1:] for b in outer]), ("sec", "sub"), 1)
    below = shifted(jnp.concatenate([b[:1] for b in outer]), ("sec", "sub"), -1)

    def split_parts(sectors):
        return jax.ShapeDtypeStruct((sectors, 3 * width, width), BF16)

    def whole(sectors):
        return [pltpu.VMEM((sectors, width, width), F32)]

    parts_outer = call(functools.partial(assemble, n), "assemble", 4 * kops * one, split_parts(2), [VMEM] * n, outer, whole(2))
    def products(sectors):
        return [jax.ShapeDtypeStruct((sectors, kops * rows, width), BF16)] * 2

    chunk = jax.ShapeDtypeStruct((2, rows, width), F32)
    chunk_inner = jax.ShapeDtypeStruct((nloc - 2, rows, width), F32)
    parts_inner, *own = call(
        functools.partial(own_sectors, n), "own", 4 * kops * one, [split_parts(nloc - 2), *products(nloc)],
        [SMEM] + [VMEM] * (n + 2), [allowed, parts_outer, *inner, left_parts], whole(nloc - 2),
    )
    result_inner = call(
        functools.partial(first_inner, nloc), "first_inner", nloc * kops * one // n, chunk_inner,
        [SMEM] + [VMEM] * 4, [shifts, *own, right_hi, right_lo],
    )
    result_outer, parts_outside = call(
        functools.partial(first_outer, n, nloc), "first_outer", 2 * kops * one, [chunk, split_parts(2)],
        [SMEM] * 2 + [VMEM] * 7, [shifts, allowed, *own, above, below, left_parts, right_hi, right_lo],
        [pltpu.VMEM((2, kops * rows, width), BF16)] * 2 + whole(2),
    )

    def mine(step):
        return call(
            functools.partial(later_chunk, n, nloc, step), "chunk", 4 * nloc * kops * one // n, [chunk, chunk_inner],
            [SMEM] * 2 + [VMEM] * 6,
            [shifts, allowed, parts_outer, parts_inner, parts_outside, left_parts, right_hi, right_lo],
            [pltpu.VMEM((nloc + 2, kops * rows, width), BF16)] * 2,
        )

    for step in range(1, n):
        next_outer, next_inner = mine(step)
        result_inner = lax.ppermute(result_inner, "op", route) + next_inner
        result_outer = lax.ppermute(result_outer, "op", route) + next_outer
    return jnp.concatenate([result_outer[:1], result_inner, result_outer[1:]])


def solution(mesh):
    return jax.shard_map(
        shards,
        mesh=mesh,
        in_specs=(
            P(("parts", "sec", "sub"), "op", None),
            P("op", None, None),
            P("op", None, None),
            P("op"),
            P("op", None),
        ),
        out_specs=P(("parts", "sec", "sub"), "op", None),
        check_vma=False,
    )
```
